32 devices in a mesh: dp: 4 (over y, x), expert: 8 (over z, core).
Axes of the slice: x: 2, y: 2, z: 4, core: 2. Of those that a mesh axis runs over, the one named last changes fastest.
Arguments:
- tokens: bfloat16 [1024, 2048], P(('dp', 'expert')), may hold values from -6 to 6
- tangent: bfloat16 [1024, 2048], P(('dp', 'expert')), may hold values from -6 to 6
- norm_gain: float32 [2048], replicated, may hold values from 0.1 to 1.9
- router: bfloat16 [2048, 16], replicated, may hold values from -0.125 to 0.125
- w_gate: bfloat16 [16, 2048, 768], P('expert', 'dp'), may hold values from -0.125 to 0.125
- w_up: bfloat16 [16, 2048, 768], P('expert', 'dp'), may hold values from -0.125 to 0.125
- w_down: bfloat16 [16, 768, 2048], P('expert', None, 'dp'), may hold values from -0.21875 to 0.21875
- routes: int32 [1024, 8], P(('dp', 'expert')), may hold values from 0 to 15, all different within a row; in each aligned block of 32 rows (0 to 31, 32 to 63, ...) at most 32 rows name the same one
Outputs:
- tangent_image: float32 [1024, 2048], P(('dp', 'expert'))
- gram_image: float32 [1024, 2048], P(('dp', 'expert'))
The draws below stay inside these ranges and needn't reach their ends.
Inputs may be any that keep to these rules, and one draw needn't show every extreme that they name: `routes`: each row names 8 different experts. Within the rows of one device (aligned blocks of 32 rows) no expert is named more than 32 times, and in some such blocks an expert is named exactly 32 times.
All inputs are finite; a program needn't handle non-finite values.
Results may differ from the reference program's by a relative error of at most 0.013.
Values may be sent and summed in bfloat16 or wider, within the bound.
A program may use at most 128 MiB of HBM per device.

```python
import math
import jax
import jax.numpy as jnp
import numpy as np
from jax import lax

D = 2048
FF = 768
TOPK = 8
TOK_DEV = 32
EXPERTS = 16
TOKENS = 1024
CAP = 32


def levels(stream_key, shape, cuts, least, top_value):
    loudness = 1.0
    for position, parts in cuts:
        draws = jax.random.uniform(jax.random.fold_in(jax.random.fold_in(stream_key, 6), position), (parts,), jnp.float32, least / len(cuts), top_value / len(cuts))
        loudness = loudness * jnp.repeat(jnp.exp(draws), shape[position] // parts).reshape((-1,) + (1,) * (len(shape) - 1 - position))
    return loudness


def shared_out(stream_key, own, number, rows, number_of, top, bound, slope):
    order = jax.random.permutation(stream_key, number_of)
    packed, common = portions_of(number_of, rows * top, bound, slope, True), portions_of(number_of, rows * top, bound, slope, False)
    places = jnp.arange(number_of)

    def named(sizes, rotation):
        used = int((sizes > 0).sum())
        fixed = max(1, used // 4)
        moved = fixed + (places - fixed + rotation * (used - fixed)) % max(1, number_of - fixed)
        return jnp.zeros((number_of,), jnp.int32).at[order[jnp.where(places < fixed, places, moved)]].set(jnp.asarray(sizes, jnp.int32))

    sizes = jnp.where(number % 4 == 0, named(packed, number // 4), named(common, number - number // 4 - 1))
    mixed = jax.random.permutation(jax.random.fold_in(own, 3), number_of)
    donor, receiver = mixed[0:number_of // 2 * 2:2], mixed[1:number_of // 2 * 2:2]
    margin = jnp.minimum(sizes[donor] - 1, bound - sizes[receiver]) // 2
    margin = jnp.where((donor == order[0]) | (receiver == order[0]) | (sizes[receiver] == 0), 0, jnp.maximum(margin, 0))
    moved = jax.random.randint(jax.random.fold_in(own, 4), (number_of // 2,), 0, 1 << 20) % (margin + 1)
    sizes = sizes.at[donor].add(-moved).at[receiver].add(moved)
    items = jnp.searchsorted(jnp.cumsum(sizes), jnp.arange(rows * top), side="right").astype(jnp.int32)
    listing = items.reshape(top, rows).T
    listing = listing[jax.random.permutation(jax.random.fold_in(own, 1), rows)]
    rotation = jax.random.randint(jax.random.fold_in(own, 2), (rows, 1), 0, top)
    return jnp.take_along_axis(listing, (jnp.arange(top)[None, :] + rotation) % top, axis=1)


def portions_of(amount, total, reach, slope, full):
    portions = [(1 << 20) // math.isqrt(standing ** slope) + 1 for standing in range(1, amount + 1)]
    largest = reach if full else min(reach, max(-(-total // amount), total * portions[0] // sum(portions)))
    least = 1 if total - largest >= amount - 1 else 0
    given, spare = [largest] + [least] * (amount - 1), total - largest - least * (amount - 1)
    while spare > 0:
        movable = [i for i in range(1, amount) if given[i] < largest] or [i for i in range(1, amount) if given[i] < reach]
        pool, remaining = sum([portions[i] for i in movable]), spare
        for i in movable:
            more = min(reach - given[i], max(1, remaining * portions[i] // pool), spare)
            given[i] = given[i] + more
            spare = spare - more
    return np.array(given)


def scatter_about(stream_key, extent, scale, most, pieces=(), kind=jnp.bfloat16):
    loudness = levels(stream_key, extent, pieces, -0.22, 0.18) if pieces else 1.0
    result = jax.random.normal(stream_key, extent, jnp.float32) * scale * loudness
    return jnp.minimum(jnp.maximum(result, -most), most).astype(kind)


def setup_inputs(seed: int = 0) -> dict:
    key_list = jax.random.split(jax.random.key(seed), 9)
    tokens = scatter_about(key_list[0], (TOKENS, D), 1.0, 6.0, ((0, 32),))
    tangent = scatter_about(key_list[1], (TOKENS, D), 1.0, 6.0, ((0, 32),))
    norm_gain = jnp.clip(1.0 + 0.18 * jax.random.normal(key_list[2], (D,), jnp.float32), 0.1, 1.9)
    router = scatter_about(key_list[3], (D, EXPERTS), D ** -0.5, 0.125)
    w_gate = scatter_about(key_list[4], (EXPERTS, D, FF), D ** -0.5, 0.125, ((0, 8), (1, 4)))
    w_up = scatter_about(key_list[5], (EXPERTS, D, FF), D ** -0.5, 0.125, ((0, 8), (1, 4)))
    w_down = scatter_about(key_list[6], (EXPERTS, FF, D), FF ** -0.5, 0.21875, ((0, 8), (2, 4)))
    routes_keys = jax.random.split(jax.random.fold_in(key_list[7], 1), TOKENS // TOK_DEV)
    routes_turns = jax.random.permutation(jax.random.fold_in(key_list[7], 3), TOKENS // TOK_DEV)
    routes = jax.vmap(lambda own, number: shared_out(jax.random.fold_in(key_list[7], 2), own, number, TOK_DEV, EXPERTS, TOPK, CAP, 2))(routes_keys, routes_turns).reshape((TOKENS, TOPK))
    return dict(tokens=tokens, tangent=tangent, norm_gain=norm_gain, router=router, w_gate=w_gate, w_up=w_up, w_down=w_down, routes=routes)


eps_value = 1e-06

def pick_columns(table, routes):
    hits = routes[:, :, None] == jnp.arange(table.shape[1], dtype=jnp.int32)[None, None, :]
    return lax.optimization_barrier(jnp.sum(jnp.where(hits, table[:, None, :], jnp.zeros((), table.dtype)), axis=2))

def round_keep(values):
    return lax.optimization_barrier(values.astype(jnp.bfloat16)).astype(jnp.float32)

def reference(tokens, tangent, norm_gain, router, w_gate, w_up, w_down, routes):
    xfull = tokens.astype(jnp.float32)
    vfull = tangent.astype(jnp.float32)
    inv_rms = lax.rsqrt(lax.optimization_barrier(jnp.mean(xfull * xfull, axis=1, keepdims=True)) + eps_value)
    normed = (norm_gain * xfull * inv_rms).astype(jnp.bfloat16)
    cross_term = lax.optimization_barrier(jnp.mean(xfull * vfull, axis=1, keepdims=True))
    normed_tan = (norm_gain * (vfull * inv_rms - xfull * inv_rms ** 3 * cross_term)).astype(jnp.bfloat16)
    logits = jnp.dot(normed, router, preferred_element_type=jnp.float32)
    logit_tan = jnp.dot(normed_tan, router, preferred_element_type=jnp.float32)
    selected = pick_columns(logits, routes)
    sel_tan = pick_columns(logit_tan, routes)
    exp_sel = jnp.exp(selected)
    gate_prob = exp_sel / lax.optimization_barrier(jnp.sum(exp_sel, axis=1, keepdims=True))
    gate_tan = gate_prob * (sel_tan - lax.optimization_barrier(jnp.sum(gate_prob * sel_tan, axis=1, keepdims=True)))
    gate_b = gate_prob.astype(jnp.bfloat16)
    gate_tan_b = gate_tan.astype(jnp.bfloat16)
    pair_count = TOKENS * TOPK
    flat_ids = routes.reshape(-1).astype(jnp.int32)
    per_expert = TOKENS // TOK_DEV * CAP
    onehot = (flat_ids[:, None] == jnp.arange(EXPERTS, dtype=jnp.int32)[None, :]).astype(jnp.int32)
    slot_rank = lax.optimization_barrier(jnp.sum(onehot * jnp.cumsum(onehot, axis=0), axis=1)) - 1
    slot_table = jnp.full((EXPERTS * per_expert,), -1, jnp.int32)
    slot_table = slot_table.at[flat_ids * per_expert + slot_rank].set(jnp.arange(pair_count, dtype=jnp.int32))
    slot_table = slot_table.reshape(EXPERTS, per_expert)

    def expert_forward(w_g, w_u, index):
        slot_valid = index >= 0
        safe_pair = jnp.maximum(index, 0)
        tok_idx = safe_pair // TOPK
        which_k = safe_pair % TOPK
        rows_n = jnp.where(slot_valid[:, None], normed[tok_idx], jnp.zeros((), jnp.bfloat16))
        rows_t = jnp.where(slot_valid[:, None], normed_tan[tok_idx], jnp.zeros((), jnp.bfloat16))
        pre_gate = jnp.dot(rows_n, w_g, preferred_element_type=jnp.float32)
        pre_up = jnp.dot(rows_n, w_u, preferred_element_type=jnp.float32)
        gate_dot = jnp.dot(rows_t, w_g, preferred_element_type=jnp.float32)
        up_dot = jnp.dot(rows_t, w_u, preferred_element_type=jnp.float32)
        sig_gate = jax.nn.sigmoid(pre_gate)
        silu_gate = pre_gate * sig_gate
        slope_gate = sig_gate * (1.0 + pre_gate * (1.0 - sig_gate))
        hidden = silu_gate * pre_up
        hidden_tan = slope_gate * gate_dot * pre_up + silu_gate * up_dot
        return (slot_valid, tok_idx, which_k, pre_up, silu_gate, slope_gate, hidden, hidden_tan)

    def jvp_step(image, inputs):
        w_g, w_u, w_d, index = inputs
        slot_valid, tok_idx, which_k, pre_up, silu_gate, slope_gate, hidden, hidden_tan = expert_forward(w_g, w_u, index)
        gate_val = gate_b[tok_idx, which_k].astype(jnp.float32)[:, None]
        tan_val = gate_tan_b[tok_idx, which_k].astype(jnp.float32)[:, None]
        mixed_rows = (tan_val * hidden + gate_val * hidden_tan).astype(jnp.bfloat16)
        pair_image = round_keep(jnp.dot(mixed_rows, w_d, preferred_element_type=jnp.float32))
        image = image.at[tok_idx].add(jnp.where(slot_valid[:, None], pair_image, 0.0))
        return (image, None)
    image_zero = jnp.zeros((TOKENS, D), jnp.float32)
    tangent_image, unused = lax.scan(jvp_step, image_zero, (w_gate, w_up, w_down, slot_table))
    image_b = tangent_image.astype(jnp.bfloat16)

    def vjp_step(carry, inputs):
        expert_grad, gate_cot = carry
        w_g, w_u, w_d, index = inputs
        slot_valid, tok_idx, which_k, pre_up, silu_gate, slope_gate, hidden, hidden_tan = expert_forward(w_g, w_u, index)
        gate_val = gate_b[tok_idx, which_k].astype(jnp.float32)[:, None]
        rows_u = jnp.where(slot_valid[:, None], image_b[tok_idx], jnp.zeros((), jnp.bfloat16))
        back_hidden = jnp.dot(rows_u, w_d.T, preferred_element_type=jnp.float32)
        pair_cot = round_keep(lax.optimization_barrier(jnp.sum(back_hidden * hidden, axis=1)))
        scaled = gate_val * back_hidden
        grad_gate = (scaled * pre_up * slope_gate).astype(jnp.bfloat16)
        grad_up = (scaled * silu_gate).astype(jnp.bfloat16)
        pair_grad = jnp.dot(grad_gate, w_g.T, preferred_element_type=jnp.float32) + jnp.dot(grad_up, w_u.T, preferred_element_type=jnp.float32)
        pair_grad = round_keep(pair_grad)
        expert_grad = expert_grad.at[tok_idx].add(jnp.where(slot_valid[:, None], pair_grad, 0.0))
        gate_cot = gate_cot.at[tok_idx, which_k].add(jnp.where(slot_valid, pair_cot, 0.0))
        return ((expert_grad, gate_cot), None)
    carry_zero = (jnp.zeros((TOKENS, D), jnp.float32), jnp.zeros((TOKENS, TOPK), jnp.float32))
    (expert_grad, gate_cot), unused = lax.scan(vjp_step, carry_zero, (w_gate, w_up, w_down, slot_table))
    logit_grad = gate_prob * (gate_cot - lax.optimization_barrier(jnp.sum(gate_prob * gate_cot, axis=1, keepdims=True)))
    hits = routes[:, :, None] == jnp.arange(EXPERTS, dtype=jnp.int32)[None, None, :]
    column_grad = lax.optimization_barrier(jnp.sum(jnp.where(hits, logit_grad[:, :, None], 0.0), axis=1))
    router_grad = jnp.dot(column_grad, router.astype(jnp.float32).T, precision=lax.Precision.HIGHEST)
    pulled = norm_gain * (expert_grad + router_grad)
    gram_image = inv_rms * pulled - xfull * inv_rms ** 3 * lax.optimization_barrier(jnp.mean(pulled * xfull, axis=1, keepdims=True))
    return (tangent_image, gram_image)
```

```python
import jax
import jax.numpy as jnp
from jax import lax
from jax.experimental import pallas as pl
from jax.experimental.pallas import tpu as pltpu
from jax.sharding import PartitionSpec as P

eps_value = 1e-06


def pick_columns(table, routes):
    hits = routes[:, :, None] == jnp.arange(table.shape[1], dtype=jnp.int32)[None, None, :]
    return jnp.sum(jnp.where(hits, table[:, None, :], jnp.zeros((), table.dtype)), axis=2)


def on_device(tokens, tangent, norm_gain, router, w_gate, w_up, w_down, routes):
    tok_rows, topk = routes.shape
    model_width = tokens.shape[1]
    experts_all = router.shape[1]
    local_experts = w_gate.shape[0]
    groups = lax.axis_size("expert")
    capacity = 2 * tok_rows * topk // experts_all
    xfull = tokens.astype(jnp.float32)
    vfull = tangent.astype(jnp.float32)
    inv_rms = lax.rsqrt(jnp.mean(xfull * xfull, axis=1, keepdims=True) + eps_value)
    normed = (norm_gain * xfull * inv_rms).astype(jnp.bfloat16)
    cross_term = jnp.mean(xfull * vfull, axis=1, keepdims=True)
    normed_tan = (norm_gain * (vfull * inv_rms - xfull * inv_rms**3 * cross_term)).astype(
        jnp.bfloat16
    )
    logits = jnp.dot(normed, router, preferred_element_type=jnp.float32)
    logit_tan = jnp.dot(normed_tan, router, preferred_element_type=jnp.float32)
    selected = pick_columns(logits, routes)
    sel_tan = pick_columns(logit_tan, routes)
    exp_sel = jnp.exp(selected)
    gate_prob = exp_sel / jnp.sum(exp_sel, axis=1, keepdims=True)
    gate_tan = gate_prob * (sel_tan - jnp.sum(gate_prob * sel_tan, axis=1, keepdims=True))
    gate_b = gate_prob.astype(jnp.bfloat16)
    gate_tan_b = gate_tan.astype(jnp.bfloat16)
    pair_count = tok_rows * topk
    flat_ids = routes.reshape(-1)
    order = jnp.arange(pair_count, dtype=jnp.int32)
    earlier = (flat_ids[None, :] == flat_ids[:, None]) & (order[None, :] < order[:, None])
    slot_rank = jnp.sum(earlier.astype(jnp.int32), axis=1)
    slot_of_pair = flat_ids * capacity + slot_rank
    slot_hits = slot_of_pair[None, :] == jnp.arange(experts_all * capacity, dtype=jnp.int32)[:, None]
    slot_table = jnp.max(
        jnp.where(slot_hits, jnp.arange(pair_count, dtype=jnp.int32)[None, :], -1), axis=1
    )
    slot_valid = slot_table >= 0
    safe_pair = jnp.maximum(slot_table, 0)
    tok_idx = safe_pair // topk
    which_k = safe_pair % topk
    bf_zero = jnp.zeros((), jnp.bfloat16)
    send_rows = jnp.stack(
        (
            jnp.where(slot_valid[:, None], normed[tok_idx], bf_zero),
            jnp.where(slot_valid[:, None], normed_tan[tok_idx], bf_zero),
        )
    )
    send_rows = send_rows.reshape(2, groups, local_experts * capacity, model_width)
    send_gates = jnp.stack(
        (
            jnp.where(slot_valid, gate_b[tok_idx, which_k], bf_zero),
            jnp.where(slot_valid, gate_tan_b[tok_idx, which_k], bf_zero),
        )
    )
    send_gates = send_gates.reshape(2, groups, local_experts * capacity)
    recv_rows, recv_gates = (
        lax.all_to_all(send_rows, "expert", split_axis=1, concat_axis=1, tiled=True),
        lax.all_to_all(send_gates, "expert", split_axis=1, concat_axis=1, tiled=True),
    )
    slot_rows = recv_rows.reshape(2, groups, local_experts, capacity, model_width)
    recv_gates = recv_gates.reshape(2, groups, local_experts, capacity).astype(jnp.float32)
    gate_val = recv_gates[0][..., None]
    tan_val = recv_gates[1][..., None]
    gate_full, up_full, down_full = (
        lax.all_gather(w_gate, "dp", axis=1, tiled=True),
        lax.all_gather(w_up, "dp", axis=1, tiled=True),
        lax.all_gather(w_down, "dp", axis=2, tiled=True),
    )
    pre_both = jnp.einsum(
        "tslkd,ldf->tslkf", slot_rows, gate_full, preferred_element_type=jnp.float32
    )
    up_both = jnp.einsum("tslkd,ldf->tslkf", slot_rows, up_full, preferred_element_type=jnp.float32)
    pre_gate = pre_both[0]
    gate_dot = pre_both[1]
    pre_up = up_both[0]
    up_dot = up_both[1]
    sig_gate = jax.nn.sigmoid(pre_gate)
    silu_gate = pre_gate * sig_gate
    slope_gate = sig_gate * (1.0 + pre_gate * (1.0 - sig_gate))
    hidden = silu_gate * pre_up
    hidden_tan = slope_gate * gate_dot * pre_up + silu_gate * up_dot
    mixed_rows = (tan_val * hidden + gate_val * hidden_tan).astype(jnp.bfloat16)
    pair_image = jnp.einsum(
        "slkf,lfd->slkd", mixed_rows, down_full, preferred_element_type=jnp.float32
    )
    pair_send = pair_image.astype(jnp.bfloat16).reshape(
        groups, local_experts * capacity, model_width
    )
    pair_back = lax.all_to_all(pair_send, "expert", split_axis=0, concat_axis=0, tiled=True)
    pair_back = pair_back.reshape(experts_all * capacity, model_width)
    tangent_image = jnp.sum(
        pair_back[slot_of_pair].astype(jnp.float32).reshape(tok_rows, topk, model_width), axis=1
    )
    image_b = tangent_image.astype(jnp.bfloat16)
    send_cot = jnp.where(slot_valid[:, None], image_b[tok_idx], bf_zero).reshape(
        groups, local_experts * capacity, model_width
    )
    recv_cot = lax.all_to_all(send_cot, "expert", split_axis=0, concat_axis=0, tiled=True)
    recv_cot = recv_cot.reshape(groups, local_experts, capacity, model_width)
    back_hidden = jnp.einsum(
        "slkd,lfd->slkf", recv_cot, down_full, preferred_element_type=jnp.float32
    )
    gate_cot = jnp.sum(back_hidden * hidden, axis=3).astype(jnp.bfloat16)
    scaled = gate_val * back_hidden
    grad_gate = (scaled * pre_up * slope_gate).astype(jnp.bfloat16)
    grad_up = (scaled * silu_gate).astype(jnp.bfloat16)
    pair_grad = jnp.einsum(
        "slkf,ldf->slkd", grad_gate, gate_full, preferred_element_type=jnp.float32
    )
    pair_grad = pair_grad + jnp.einsum(
        "slkf,ldf->slkd", grad_up, up_full, preferred_element_type=jnp.float32
    )
    grad_send = pair_grad.astype(jnp.bfloat16).reshape(
        groups, local_experts * capacity, model_width
    )
    cot_send = gate_cot.reshape(groups, local_experts * capacity)
    grad_back, cot_back = (
        lax.all_to_all(grad_send, "expert", split_axis=0, concat_axis=0, tiled=True),
        lax.all_to_all(cot_send, "expert", split_axis=0, concat_axis=0, tiled=True),
    )
    grad_back = grad_back.reshape(experts_all * capacity, model_width)
    cot_back = cot_back.reshape(experts_all * capacity)
    expert_grad = jnp.sum(
        grad_back[slot_of_pair].astype(jnp.float32).reshape(tok_rows, topk, model_width), axis=1
    )
    pair_cot = cot_back[slot_of_pair].astype(jnp.float32).reshape(tok_rows, topk)
    logit_grad = gate_prob * (pair_cot - jnp.sum(gate_prob * pair_cot, axis=1, keepdims=True))
    hits = routes[:, :, None] == jnp.arange(experts_all, dtype=jnp.int32)[None, None, :]
    column_grad = jnp.sum(jnp.where(hits, logit_grad[:, :, None], 0.0), axis=1)
    router_grad = jnp.dot(
        column_grad, router.astype(jnp.float32).T, precision=lax.Precision.HIGHEST
    )
    pulled = norm_gain * (expert_grad + router_grad)
    gram_image = inv_rms * pulled - xfull * inv_rms**3 * jnp.mean(
        pulled * xfull, axis=1, keepdims=True
    )
    return (tangent_image, gram_image)


MESH = pl.DeviceIdType.MESH


def nt_dot(left, right):
    return lax.dot_general(
        left, right, (((1,), (1,)), ((), ())), preferred_element_type=jnp.float32
    )


def nn_dot(left, right):
    return jnp.dot(left, right, preferred_element_type=jnp.float32)


def block_kernel(
    tok_ref, tan_ref, gain_ref, router_ref, routes_ref, wg_ref, wu_ref, wd_ref,
    image_ref, gram_ref,
    wgu, wd, rows, keep_a, keep_s, keep_h, mix, part, own_part, mid, far, landed,
    image_rows, grads, part2, own_part2, mid2, far2, landed2, prob_keep, inv_keep, router_pad,
    w_send, w_recv, w_own, m_send, m_recv, t_send, t_recv, a_send, a_recv, s_send, s_recv,
    z_send, z_recv,
):
    f32, bf = jnp.float32, jnp.bfloat16
    n_tok, width = tok_ref.shape
    slab, hid = wg_ref.shape[1], wg_ref.shape[2]
    half = hid // 2
    n_lane = 4 * n_tok
    n_exp = router_ref.shape[0]
    dp, ex = lax.axis_index("dp"), lax.axis_index("expert")
    y, x = dp // 2, dp % 2
    z, core = ex // 2, ex % 2
    x_index, y_index = y * 2 + 1 - x, (1 - y) * 2 + x
    d_index = (1 - y) * 2 + 1 - x
    x_peer, y_peer = (x_index, ex), (y_index, ex)
    mate = (dp, z * 2 + 1 - core)
    z_peers = [(dp, (z + dz) % 4 * 2 + core) for dz in range(1, 4)]
    at_x, at_own, at_y = 0, n_lane, 2 * n_lane

    def rows_of(base, dz):
        return pl.ds(pl.multiple_of(base + (z + dz) % 4 * n_tok, n_tok), n_tok)

    barrier = pltpu.get_barrier_semaphore()
    friends = z_peers + [x_peer, y_peer, mate]
    for friend in friends:
        pl.semaphore_signal(barrier, inc=1, device_id=friend, device_id_type=MESH)
    pl.semaphore_wait(barrier, len(friends))

    pending = []

    def push(src, dst, sems, where, device):
        copy = pltpu.make_async_remote_copy(
            src_ref=src, dst_ref=dst, send_sem=sems[0].at[where], recv_sem=sems[1].at[where],
            device_id=device, device_id_type=MESH,
        )
        copy.start()
        pending.append(copy)
        return copy

    def slab_of(index):
        return pl.ds(pl.multiple_of(index * slab, slab), slab)

    def weight_at(kind, l, index):
        if kind == 2:
            return wd.at[l, pl.ds(pl.multiple_of(core * half, half), half), slab_of(index)]
        first = pl.multiple_of(core * hid + kind * half, half)
        return wgu.at[l, slab_of(index), pl.ds(first, half)]

    def weight_src(kind, l, which):
        part_of = pl.ds(pl.multiple_of(which * half, half), half)
        if kind == 2:
            return wd_ref.at[l, part_of, :]
        return (wg_ref, wu_ref)[kind].at[l, :, part_of]

    direct, relayed, shared, local = {}, {}, {}, {}
    w_sems, m_sems, t_sems = (w_send, w_recv), (m_send, m_recv), (t_send, t_recv)
    a_sems, s_sems, z_sems = (a_send, a_recv), (s_send, s_recv), (z_send, z_recv)

    def start_weights(kind, l):
        mine = weight_at(kind, l, dp)
        for_x, for_y = (1 - x, x) if l == 0 else (y, 1 - y)
        for_me = x if l == 0 else y
        direct[kind, l] = [
            push(weight_src(kind, l, for_x), mine, w_sems, (kind, l, 0), x_peer),
            push(weight_src(kind, l, for_y), mine, w_sems, (kind, l, 1), y_peer),
        ]
        local[kind, l] = pltpu.make_async_copy(
            weight_src(kind, l, for_me), mine, w_own.at[kind, l]
        )
        local[kind, l].start()
        shared[kind, l] = [
            push(weight_src(kind, l, for_me), mine, m_sems, (kind, l, 0), mate)
        ]

    def share_weights(kind, l, slot, index):
        block = weight_at(kind, l, index)
        shared[kind, l].append(push(block, block, m_sems, (kind, l, slot), mate))

    def relay_weights(kind, l):
        block = weight_at(kind, l, (x_index, y_index)[l])
        direct[kind, l][l].wait_recv()
        relayed[kind, l] = push(block, block, w_sems, (kind, l, 2), (y_peer, x_peer)[l])
        share_weights(kind, l, 1, (x_index, y_index)[l])
        direct[kind, l][1 - l].wait_recv()
        share_weights(kind, l, 2, (x_index, y_index)[1 - l])

    def last_weights(kind, l):
        relayed[kind, l].wait_recv()
        share_weights(kind, l, 3, d_index)

    def need_weights(kind, l):
        local[kind, l].wait()
        for copy in shared[kind, l]:
            copy.wait_recv()

    start_weights(0, 0)

    router_pad[...] = jnp.zeros(router_pad.shape, bf)
    router_pad[0:n_exp, :] = router_ref[...]
    xfull = tok_ref[...].astype(f32)
    vfull = tan_ref[...].astype(f32)
    gain = gain_ref[...]
    inv_rms = lax.rsqrt(jnp.mean(xfull * xfull, axis=1, keepdims=True) + eps_value)
    normed = (gain * xfull * inv_rms).astype(bf)
    cross_term = jnp.mean(xfull * vfull, axis=1, keepdims=True)
    inv_cube = inv_rms * inv_rms * inv_rms
    normed_tan = (gain * (vfull * inv_rms - xfull * inv_cube * cross_term)).astype(bf)
    mine = rows_of(at_own, 0)
    rows[mine, 0:width] = normed
    rows[mine, width : 2 * width] = normed_tan
    logits = nt_dot(normed, router_pad[...])
    logit_tan = nt_dot(normed_tan, router_pad[...])
    ids = lax.broadcasted_iota(jnp.int32, (128, n_tok), 0)
    chosen_by = jnp.zeros((128, n_tok), f32)
    for k in range(routes_ref.shape[0]):
        chosen_by = chosen_by + jnp.where(ids == routes_ref[k : k + 1, :], 1.0, 0.0)
    unit = jnp.where(
        lax.broadcasted_iota(jnp.int32, (n_tok, n_tok), 0)
        == lax.broadcasted_iota(jnp.int32, (n_tok, n_tok), 1),
        1.0, 0.0,
    ).astype(bf)
    chosen = nt_dot(unit, chosen_by.astype(bf))
    exp_sel = jnp.where(chosen > 0.5, jnp.exp(logits), 0.0)
    gate_prob = exp_sel / jnp.sum(exp_sel, axis=1, keepdims=True)
    gate_tan = gate_prob * (
        logit_tan - jnp.sum(gate_prob * logit_tan, axis=1, keepdims=True)
    )
    rows[mine, 2 * width : 2 * width + 128] = (
        gate_prob + pltpu.roll(gate_tan, 64, 1)
    ).astype(bf)
    prob_keep[...] = gate_prob
    inv_keep[...] = jnp.broadcast_to(inv_rms, (n_tok, 128))

    def along_z(buf, base, sems, which):
        block = buf.at[rows_of(base, 0)]
        return [push(block, block, sems, (which, dz), z_peers[dz - 1]) for dz in (2, 1, 3)]

    from_x = push(rows.at[mine], rows.at[rows_of(at_x, 0)], t_sems, (0, 0), x_peer)
    from_y = push(rows.at[mine], rows.at[rows_of(at_y, 0)], t_sems, (2, 0), y_peer)
    token_copies = along_z(rows, at_own, t_sems, 1)
    pieces = [(0, 0), (1, 0), (0, 1), (1, 1), (2, 0), (2, 1)]
    for kind, l in pieces[1:]:
        start_weights(kind, l)
    from_x.wait_recv()
    token_copies += along_z(rows, at_x, t_sems, 0)
    from_y.wait_recv()
    token_copies += along_z(rows, at_y, t_sems, 2)
    for kind, l in pieces:
        relay_weights(kind, l)
    for kind, l in pieces[:4]:
        last_weights(kind, l)
    for copy in token_copies:
        copy.wait_recv()

    n_rows = 2 * n_lane
    wide_lanes = lax.broadcasted_iota(jnp.int32, (n_rows, 128), 1)

    for l in range(2):
        need_weights(0, l)
        need_weights(1, l)
        these = pl.ds(l * n_lane, n_rows)

        @pl.loop(0, 2)
        def _(k):
            cols = pl.ds(pl.multiple_of(k * hid, hid), hid)
            expert = (z * 2 + k) * 2 + l
            table = rows[these, 2 * width : 2 * width + 128].astype(f32)
            gate = jnp.sum(jnp.where(wide_lanes == expert, table, 0.0), axis=1, keepdims=True)
            tan = jnp.sum(
                jnp.where(wide_lanes == expert + 64, table, 0.0), axis=1, keepdims=True
            )
            pre = nn_dot(rows[these, 0:width], wgu[l, :, cols])
            dots = nn_dot(rows[these, width : 2 * width], wgu[l, :, cols])
            pre_gate, pre_up = pre[:, 0:half], pre[:, half:hid]
            gate_dot, up_dot = dots[:, 0:half], dots[:, half:hid]
            sig = jax.nn.sigmoid(pre_gate)
            silu = pre_gate * sig
            slope_up = sig * (1.0 + pre_gate * (1.0 - sig)) * pre_up
            hidden = silu * pre_up
            mixed = tan * hidden + gate * (slope_up * gate_dot + silu * up_dot)
            keep_a[l, k] = gate * slope_up
            keep_s[l, k] = gate * silu
            keep_h[l, k] = hidden
            mix[l, :, pl.ds(pl.multiple_of(k * half, half), half)] = mixed.astype(bf)

    for kind, l in pieces[4:]:
        last_weights(kind, l)

    def send_side(parts, far, turn, s):
        peer, base = ((x_peer, at_x), (y_peer, at_y))[s]
        return [
            push(
                parts.at[rows_of(base, dz)], far.at[s, rows_of(0, dz)],
                s_sems, (turn, s, dz), peer,
            )
            for dz in (2, 1, 3, 0)
        ]

    def send_home(compute, parts, own, mid, far, land, turn):
        compute(0)
        x_copies = send_side(parts, far, turn, 0)
        compute(1)
        y_copies = send_side(parts, far, turn, 1)
        copies = {}
        for i, dz in enumerate((2, 1, 3, 0)):
            x_copies[i].wait_recv()
            y_copies[i].wait_recv()
            at = rows_of(0, dz)
            total = own[at, :] + (far[0, at, :].astype(f32) + far[1, at, :].astype(f32))
            if dz:
                mid[dz] = total.astype(bf)
                copies[dz] = push(
                    mid.at[dz], land.at[z], z_sems, (turn, dz), z_peers[dz - 1]
                )
        for dz in (1, 3, 2):
            copies[dz].wait_recv()
            total = total + land[(z + 4 - dz) % 4].astype(f32)
        return total

    step = width // 4

    def place(parts, own, l, cols, term):
        if l == 0:
            parts[at_x : at_x + n_lane, cols] = term[0:n_lane].astype(bf)
            own[:, cols] = term[n_lane:n_rows]
        else:
            own[:, cols] = own[:, cols] + term[0:n_lane]
            parts[at_y : at_y + n_lane, cols] = term[n_lane:n_rows].astype(bf)

    def down(l):
        need_weights(2, l)

        @pl.loop(0, 4)
        def _(j):
            cols = pl.ds(pl.multiple_of(j * step, step), step)
            place(part, own_part, l, cols, nn_dot(mix[l], wd[l, :, cols]))

    image = send_home(down, part, own_part, mid, far, landed, 0)
    image_ref[...] = image
    image_rows[mine, :] = image.astype(bf)

    def gather_image():
        block = image_rows.at[mine]
        to_z = {dz: push(block, block, a_sems, (0, dz), z_peers[dz - 1]) for dz in (2, 1, 3)}
        sides = []

        def to_sides(dz):
            block = image_rows.at[rows_of(at_own, 4 - dz)]
            for s, (peer, base) in enumerate(((x_peer, at_x), (y_peer, at_y))):
                sides.append(
                    push(block, image_rows.at[rows_of(base, 4 - dz)], a_sems, (1 + s, dz), peer)
                )

        to_sides(0)
        for dz in (3, 1, 2):
            to_z[dz].wait_recv()
            to_sides(dz)
        for copy in sides:
            copy.wait_recv()

    gather_image()

    def backward(l):
        these = pl.ds(l * n_lane, n_rows)
        cots = jnp.zeros((n_rows, 128), f32)
        for k in range(2):
            back = nt_dot(image_rows[these, :], wd[l, k * half : (k + 1) * half, :])
            cot = jnp.sum(back * keep_h[l, k], axis=1, keepdims=True)
            cots = cots + jnp.where(wide_lanes == (z * 2 + k) * 2 + l, cot, 0.0)
            grads[l, :, k * hid : k * hid + half] = (back * keep_a[l, k]).astype(bf)
            grads[l, :, k * hid + half : (k + 1) * hid] = (back * keep_s[l, k]).astype(bf)
        place(part2, own_part2, l, slice(width, width + 128), cots)

        @pl.loop(0, 4)
        def _(j):
            cols = pl.ds(pl.multiple_of(j * step, step), step)
            place(part2, own_part2, l, cols, nt_dot(grads[l], wgu[l, cols, :]))

    total = send_home(backward, part2, own_part2, mid2, far2, landed2, 1)

    expert_grad = total[:, 0:width]
    cot = total[:, width : width + 128]
    prob = prob_keep[...]
    column_grad = prob * (cot - jnp.sum(prob * cot, axis=1, keepdims=True))
    high = column_grad.astype(bf)
    rest = column_grad - high.astype(f32)
    middle = rest.astype(bf)
    low = (rest - middle.astype(f32)).astype(bf)
    router = router_pad[...]
    router_grad = nn_dot(high, router) + (nn_dot(middle, router) + nn_dot(low, router))
    xfull = tok_ref[...].astype(f32)
    inv_rms = inv_keep[:, 0:1]
    pulled = gain_ref[...] * (expert_grad + router_grad)
    gram_ref[...] = inv_rms * pulled - xfull * (inv_rms * inv_rms * inv_rms) * jnp.mean(
        pulled * xfull, axis=1, keepdims=True
    )
    for copy in pending:
        copy.wait_send()


def on_device_dense(tokens, tangent, norm_gain, router, w_gate, w_up, w_down, routes):
    n_tok, width = tokens.shape
    hid = w_gate.shape[2]
    half = hid // 2
    n_lane = 4 * n_tok
    bf, f32 = jnp.bfloat16, jnp.float32
    vm = pl.BlockSpec(memory_space=pltpu.VMEM)
    hbm = pl.BlockSpec(memory_space=pl.ANY)
    out = jax.ShapeDtypeStruct((n_tok, width), f32)
    dma = pltpu.SemaphoreType.DMA
    keep = pltpu.VMEM((2, 2, 2 * n_lane, half), f32)

    def home(columns):
        return [
            pltpu.VMEM((3 * n_lane, columns), bf),
            pltpu.VMEM((n_lane, columns), f32),
            pltpu.VMEM((4, n_tok, columns), bf),
            pltpu.VMEM((2, n_lane, columns), bf),
            pltpu.VMEM((4, n_tok, columns), bf),
        ]

    image, gram = pl.pallas_call(
        block_kernel,
        out_shape=(out, out),
        in_specs=[vm] * 5 + [hbm] * 3,
        out_specs=(vm, vm),
        scratch_shapes=[
            pltpu.VMEM((2, width, 2 * hid), bf),
            pltpu.VMEM((2, hid, width), bf),
            pltpu.VMEM((3 * n_lane, 2 * width + 128), bf),
            keep, keep, keep,
            pltpu.VMEM((2, 2 * n_lane, hid), bf),
            *home(width),
            pltpu.VMEM((3 * n_lane, width), bf),
            pltpu.VMEM((2, 2 * n_lane, 2 * hid), bf),
            *home(width + 128),
            pltpu.VMEM((n_tok, 128), f32),
            pltpu.VMEM((n_tok, 128), f32),
            pltpu.VMEM((128, width), bf),
            dma((3, 2, 3)), dma((3, 2, 3)), dma((3, 2)),
            dma((3, 2, 4)), dma((3, 2, 4)),
            dma((3, 4)), dma((3, 4)), dma((3, 4)), dma((3, 4)),
            dma((2, 2, 4)), dma((2, 2, 4)), dma((2, 4)), dma((2, 4)),
        ],
        compiler_params=pltpu.CompilerParams(
            collective_id=0, has_side_effects=True, vmem_limit_bytes=60 * 2**20
        ),
        cost_estimate=pl.CostEstimate(
            flops=2 * 8 * 512 * width * hid, bytes_accessed=2**24, transcendentals=2**20
        ),
    )(tokens, tangent, norm_gain.reshape(1, width), router.T, routes.T, w_gate, w_up, w_down)
    return image, gram


def solution(mesh):
    in_specs = (
        P(("dp", "expert"), None),
        P(("dp", "expert"), None),
        P(),
        P(),
        P("expert", "dp", None),
        P("expert", "dp", None),
        P("expert", None, "dp"),
        P(("dp", "expert"), None),
    )
    out_specs = (P(("dp", "expert"), None), P(("dp", "expert"), None))
    body = on_device
    if mesh.shape["dp"] == 4 and mesh.shape["expert"] == 8:
        body = on_device_dense
    return jax.shard_map(
        body, mesh=mesh, in_specs=in_specs, out_specs=out_specs, check_vma=False
    )
```

```python
import jax
import jax.numpy as jnp
from jax import lax
from jax.experimental import pallas as pl
from jax.experimental.pallas import tpu as pltpu
from jax.sharding import PartitionSpec as P

eps_value = 1e-06


def pick_columns(table, routes):
    hits = routes[:, :, None] == jnp.arange(table.shape[1], dtype=jnp.int32)[None, None, :]
    return jnp.sum(jnp.where(hits, table[:, None, :], jnp.zeros((), table.dtype)), axis=2)


def on_device(tokens, tangent, norm_gain, router, w_gate, w_up, w_down, routes):
    tok_rows, topk = routes.shape
    model_width = tokens.shape[1]
    experts_all = router.shape[1]
    local_experts = w_gate.shape[0]
    groups = lax.axis_size("expert")
    capacity = 2 * tok_rows * topk // experts_all
    xfull = tokens.astype(jnp.float32)
    vfull = tangent.astype(jnp.float32)
    inv_rms = lax.rsqrt(jnp.mean(xfull * xfull, axis=1, keepdims=True) + eps_value)
    normed = (norm_gain * xfull * inv_rms).astype(jnp.bfloat16)
    cross_term = jnp.mean(xfull * vfull, axis=1, keepdims=True)
    normed_tan = (norm_gain * (vfull * inv_rms - xfull * inv_rms**3 * cross_term)).astype(
        jnp.bfloat16
    )
    logits = jnp.dot(normed, router, preferred_element_type=jnp.float32)
    logit_tan = jnp.dot(normed_tan, router, preferred_element_type=jnp.float32)
    selected = pick_columns(logits, routes)
    sel_tan = pick_columns(logit_tan, routes)
    exp_sel = jnp.exp(selected)
    gate_prob = exp_sel / jnp.sum(exp_sel, axis=1, keepdims=True)
    gate_tan = gate_prob * (sel_tan - jnp.sum(gate_prob * sel_tan, axis=1, keepdims=True))
    gate_b = gate_prob.astype(jnp.bfloat16)
    gate_tan_b = gate_tan.astype(jnp.bfloat16)
    pair_count = tok_rows * topk
    flat_ids = routes.reshape(-1)
    order = jnp.arange(pair_count, dtype=jnp.int32)
    earlier = (flat_ids[None, :] == flat_ids[:, None]) & (order[None, :] < order[:, None])
    slot_rank = jnp.sum(earlier.astype(jnp.int32), axis=1)
    slot_of_pair = flat_ids * capacity + slot_rank
    slot_hits = slot_of_pair[None, :] == jnp.arange(experts_all * capacity, dtype=jnp.int32)[:, None]
    slot_table = jnp.max(
        jnp.where(slot_hits, jnp.arange(pair_count, dtype=jnp.int32)[None, :], -1), axis=1
    )
    slot_valid = slot_table >= 0
    safe_pair = jnp.maximum(slot_table, 0)
    tok_idx = safe_pair // topk
    which_k = safe_pair % topk
    bf_zero = jnp.zeros((), jnp.bfloat16)
    send_rows = jnp.stack(
        (
            jnp.where(slot_valid[:, None], normed[tok_idx], bf_zero),
            jnp.where(slot_valid[:, None], normed_tan[tok_idx], bf_zero),
        )
    )
    send_rows = send_rows.reshape(2, groups, local_experts * capacity, model_width)
    send_gates = jnp.stack(
        (
            jnp.where(slot_valid, gate_b[tok_idx, which_k], bf_zero),
            jnp.where(slot_valid, gate_tan_b[tok_idx, which_k], bf_zero),
        )
    )
    send_gates = send_gates.reshape(2, groups, local_experts * capacity)
    recv_rows, recv_gates = (
        lax.all_to_all(send_rows, "expert", split_axis=1, concat_axis=1, tiled=True),
        lax.all_to_all(send_gates, "expert", split_axis=1, concat_axis=1, tiled=True),
    )
    slot_rows = recv_rows.reshape(2, groups, local_experts, capacity, model_width)
    recv_gates = recv_gates.reshape(2, groups, local_experts, capacity).astype(jnp.float32)
    gate_val = recv_gates[0][..., None]
    tan_val = recv_gates[1][..., None]
    gate_full, up_full, down_full = (
        lax.all_gather(w_gate, "dp", axis=1, tiled=True),
        lax.all_gather(w_up, "dp", axis=1, tiled=True),
        lax.all_gather(w_down, "dp", axis=2, tiled=True),
    )
    pre_both = jnp.einsum(
        "tslkd,ldf->tslkf", slot_rows, gate_full, preferred_element_type=jnp.float32
    )
    up_both = jnp.einsum("tslkd,ldf->tslkf", slot_rows, up_full, preferred_element_type=jnp.float32)
    pre_gate = pre_both[0]
    gate_dot = pre_both[1]
    pre_up = up_both[0]
    up_dot = up_both[1]
    sig_gate = jax.nn.sigmoid(pre_gate)
    silu_gate = pre_gate * sig_gate
    slope_gate = sig_gate * (1.0 + pre_gate * (1.0 - sig_gate))
    hidden = silu_gate * pre_up
    hidden_tan = slope_gate * gate_dot * pre_up + silu_gate * up_dot
    mixed_rows = (tan_val * hidden + gate_val * hidden_tan).astype(jnp.bfloat16)
    pair_image = jnp.einsum(
        "slkf,lfd->slkd", mixed_rows, down_full, preferred_element_type=jnp.float32
    )
    pair_send = pair_image.astype(jnp.bfloat16).reshape(
        groups, local_experts * capacity, model_width
    )
    pair_back = lax.all_to_all(pair_send, "expert", split_axis=0, concat_axis=0, tiled=True)
    pair_back = pair_back.reshape(experts_all * capacity, model_width)
    tangent_image = jnp.sum(
        pair_back[slot_of_pair].astype(jnp.float32).reshape(tok_rows, topk, model_width), axis=1
    )
    image_b = tangent_image.astype(jnp.bfloat16)
    send_cot = jnp.where(slot_valid[:, None], image_b[tok_idx], bf_zero).reshape(
        groups, local_experts * capacity, model_width
    )
    recv_cot = lax.all_to_all(send_cot, "expert", split_axis=0, concat_axis=0, tiled=True)
    recv_cot = recv_cot.reshape(groups, local_experts, capacity, model_width)
    back_hidden = jnp.einsum(
        "slkd,lfd->slkf", recv_cot, down_full, preferred_element_type=jnp.float32
    )
    gate_cot = jnp.sum(back_hidden * hidden, axis=3).astype(jnp.bfloat16)
    scaled = gate_val * back_hidden
    grad_gate = (scaled * pre_up * slope_gate).astype(jnp.bfloat16)
    grad_up = (scaled * silu_gate).astype(jnp.bfloat16)
    pair_grad = jnp.einsum(
        "slkf,ldf->slkd", grad_gate, gate_full, preferred_element_type=jnp.float32
    )
    pair_grad = pair_grad + jnp.einsum(
        "slkf,ldf->slkd", grad_up, up_full, preferred_element_type=jnp.float32
    )
    grad_send = pair_grad.astype(jnp.bfloat16).reshape(
        groups, local_experts * capacity, model_width
    )
    cot_send = gate_cot.reshape(groups, local_experts * capacity)
    grad_back, cot_back = (
        lax.all_to_all(grad_send, "expert", split_axis=0, concat_axis=0, tiled=True),
        lax.all_to_all(cot_send, "expert", split_axis=0, concat_axis=0, tiled=True),
    )
    grad_back = grad_back.reshape(experts_all * capacity, model_width)
    cot_back = cot_back.reshape(experts_all * capacity)
    expert_grad = jnp.sum(
        grad_back[slot_of_pair].astype(jnp.float32).reshape(tok_rows, topk, model_width), axis=1
    )
    pair_cot = cot_back[slot_of_pair].astype(jnp.float32).reshape(tok_rows, topk)
    logit_grad = gate_prob * (pair_cot - jnp.sum(gate_prob * pair_cot, axis=1, keepdims=True))
    hits = routes[:, :, None] == jnp.arange(experts_all, dtype=jnp.int32)[None, None, :]
    column_grad = jnp.sum(jnp.where(hits, logit_grad[:, :, None], 0.0), axis=1)
    router_grad = jnp.dot(
        column_grad, router.astype(jnp.float32).T, precision=lax.Precision.HIGHEST
    )
    pulled = norm_gain * (expert_grad + router_grad)
    gram_image = inv_rms * pulled - xfull * inv_rms**3 * jnp.mean(
        pulled * xfull, axis=1, keepdims=True
    )
    return (tangent_image, gram_image)


MESH = pl.DeviceIdType.MESH


def nt_dot(left, right):
    return lax.dot_general(
        left, right, (((1,), (1,)), ((), ())), preferred_element_type=jnp.float32
    )


def nn_dot(left, right):
    return jnp.dot(left, right, preferred_element_type=jnp.float32)


batches = 2


def block_kernel(
    tok_ref, tan_ref, gain_ref, router_ref, routes_ref, wg_ref, wu_ref, wd_ref,
    image_ref, gram_ref,
    wgu, wd, rows, keep_a, keep_s, keep_h, mix, part, own_part, mid, far, landed,
    image_rows, grads, part2, own_part2, mid2, far2, landed2, prob_keep, inv_keep, router_pad,
    w_send, w_recv, w_own, m_send, m_recv, t_send, t_recv, a_send, a_recv, s_send, s_recv,
    z_send, z_recv,
):
    f32, bf = jnp.float32, jnp.bfloat16
    n_tok, width = tok_ref.shape
    slab, hid = wg_ref.shape[1], wg_ref.shape[2]
    half = hid // 2
    n_sub = n_tok // batches
    n_lane = 4 * n_sub
    n_exp = router_ref.shape[0]
    dp, ex = lax.axis_index("dp"), lax.axis_index("expert")
    y, x = dp // 2, dp % 2
    z, core = ex // 2, ex % 2
    x_index, y_index = y * 2 + 1 - x, (1 - y) * 2 + x
    d_index = (1 - y) * 2 + 1 - x
    x_peer, y_peer = (x_index, ex), (y_index, ex)
    mate = (dp, z * 2 + 1 - core)
    z_peers = [(dp, (z + dz) % 4 * 2 + core) for dz in range(1, 4)]
    at_x, at_own, at_y = 0, n_lane, 2 * n_lane

    def rows_of(base, dz):
        return pl.ds(pl.multiple_of(base + (z + dz) % 4 * n_sub, n_sub), n_sub)

    def tokens_of(b):
        return slice(b * n_sub, (b + 1) * n_sub)

    barrier = pltpu.get_barrier_semaphore()
    friends = z_peers + [x_peer, y_peer, mate]
    for friend in friends:
        pl.semaphore_signal(barrier, inc=1, device_id=friend, device_id_type=MESH)
    pl.semaphore_wait(barrier, len(friends))

    pending = []

    def push(src, dst, sems, where, device):
        copy = pltpu.make_async_remote_copy(
            src_ref=src, dst_ref=dst, send_sem=sems[0].at[where], recv_sem=sems[1].at[where],
            device_id=device, device_id_type=MESH,
        )
        copy.start()
        pending.append(copy)
        return copy

    def slab_of(index):
        return pl.ds(pl.multiple_of(index * slab, slab), slab)

    def weight_at(kind, l, index):
        if kind == 2:
            return wd.at[l, pl.ds(pl.multiple_of(core * half, half), half), slab_of(index)]
        first = pl.multiple_of(core * hid + kind * half, half)
        return wgu.at[l, slab_of(index), pl.ds(first, half)]

    def weight_src(kind, l, which):
        part_of = pl.ds(pl.multiple_of(which * half, half), half)
        if kind == 2:
            return wd_ref.at[l, part_of, :]
        return (wg_ref, wu_ref)[kind].at[l, :, part_of]

    direct, relayed, shared, local = {}, {}, {}, {}
    w_sems, m_sems, t_sems = (w_send, w_recv), (m_send, m_recv), (t_send, t_recv)
    a_sems, s_sems, z_sems = (a_send, a_recv), (s_send, s_recv), (z_send, z_recv)

    def start_weights(kind, l):
        mine = weight_at(kind, l, dp)
        for_x, for_y = (1 - x, x) if l == 0 else (y, 1 - y)
        for_me = x if l == 0 else y
        direct[kind, l] = [
            push(weight_src(kind, l, for_x), mine, w_sems, (kind, l, 0), x_peer),
            push(weight_src(kind, l, for_y), mine, w_sems, (kind, l, 1), y_peer),
        ]
        local[kind, l] = pltpu.make_async_copy(
            weight_src(kind, l, for_me), mine, w_own.at[kind, l]
        )
        local[kind, l].start()
        shared[kind, l] = [
            push(weight_src(kind, l, for_me), mine, m_sems, (kind, l, 0), mate)
        ]

    def share_weights(kind, l, slot, index):
        block = weight_at(kind, l, index)
        shared[kind, l].append(push(block, block, m_sems, (kind, l, slot), mate))

    def relay_weights(kind, l):
        block = weight_at(kind, l, (x_index, y_index)[l])
        direct[kind, l][l].wait_recv()
        relayed[kind, l] = push(block, block, w_sems, (kind, l, 2), (y_peer, x_peer)[l])
        share_weights(kind, l, 1, (x_index, y_index)[l])
        direct[kind, l][1 - l].wait_recv()
        share_weights(kind, l, 2, (x_index, y_index)[1 - l])

    def last_weights(kind, l):
        relayed[kind, l].wait_recv()
        share_weights(kind, l, 3, d_index)

    def need_weights(kind, l):
        local[kind, l].wait()
        for copy in shared[kind, l]:
            copy.wait_recv()

    start_weights(0, 0)

    router_pad[...] = jnp.zeros(router_pad.shape, bf)
    router_pad[0:n_exp, :] = router_ref[...]
    xfull = tok_ref[...].astype(f32)
    vfull = tan_ref[...].astype(f32)
    gain = gain_ref[...]
    inv_rms = lax.rsqrt(jnp.mean(xfull * xfull, axis=1, keepdims=True) + eps_value)
    normed = (gain * xfull * inv_rms).astype(bf)
    cross_term = jnp.mean(xfull * vfull, axis=1, keepdims=True)
    inv_cube = inv_rms * inv_rms * inv_rms
    normed_tan = (gain * (vfull * inv_rms - xfull * inv_cube * cross_term)).astype(bf)
    mine = rows_of(at_own, 0)
    for b in range(batches):
        rows[b, mine, 0:width] = normed[tokens_of(b)]
        rows[b, mine, width : 2 * width] = normed_tan[tokens_of(b)]
    logits = nt_dot(normed, router_pad[...])
    logit_tan = nt_dot(normed_tan, router_pad[...])
    ids = lax.broadcasted_iota(jnp.int32, (128, n_tok), 0)
    chosen_by = jnp.zeros((128, n_tok), f32)
    for k in range(routes_ref.shape[0]):
        chosen_by = chosen_by + jnp.where(ids == routes_ref[k : k + 1, :], 1.0, 0.0)
    unit = jnp.where(
        lax.broadcasted_iota(jnp.int32, (n_tok, n_tok), 0)
        == lax.broadcasted_iota(jnp.int32, (n_tok, n_tok), 1),
        1.0, 0.0,
    ).astype(bf)
    chosen = nt_dot(unit, chosen_by.astype(bf))
    exp_sel = jnp.where(chosen > 0.5, jnp.exp(logits), 0.0)
    gate_prob = exp_sel / jnp.sum(exp_sel, axis=1, keepdims=True)
    gate_tan = gate_prob * (
        logit_tan - jnp.sum(gate_prob * logit_tan, axis=1, keepdims=True)
    )
    table = (gate_prob + pltpu.roll(gate_tan, 64, 1)).astype(bf)
    for b in range(batches):
        rows[b, mine, 2 * width : 2 * width + 128] = table[tokens_of(b)]
    prob_keep[...] = gate_prob
    inv_keep[...] = jnp.broadcast_to(inv_rms, (n_tok, 128))

    def along_z(buf, base, sems, which):
        block = buf.at[:, rows_of(base, 0)]
        return [push(block, block, sems, (which, dz), z_peers[dz - 1]) for dz in (2, 1, 3)]

    from_x = push(rows.at[:, mine], rows.at[:, rows_of(at_x, 0)], t_sems, (0, 0), x_peer)
    from_y = push(rows.at[:, mine], rows.at[:, rows_of(at_y, 0)], t_sems, (2, 0), y_peer)
    token_copies = along_z(rows, at_own, t_sems, 1)
    pieces = [(0, 0), (1, 0), (0, 1), (1, 1), (2, 0), (2, 1)]
    for kind, l in pieces[1:]:
        start_weights(kind, l)
    from_x.wait_recv()
    token_copies += along_z(rows, at_x, t_sems, 0)
    from_y.wait_recv()
    token_copies += along_z(rows, at_y, t_sems, 2)
    for kind, l in pieces:
        relay_weights(kind, l)
    for kind, l in pieces[:4]:
        last_weights(kind, l)
    for copy in token_copies:
        copy.wait_recv()

    n_rows = 2 * n_lane
    all_rows = batches * n_rows
    wide_lanes = lax.broadcasted_iota(jnp.int32, (all_rows, 128), 1)

    for l in range(2):
        need_weights(0, l)
        need_weights(1, l)
        these = slice(l * n_lane, l * n_lane + n_rows)

        @pl.loop(0, 2)
        def _(k):
            cols = pl.ds(pl.multiple_of(k * hid, hid), hid)
            expert = (z * 2 + k) * 2 + l
            table = rows[:, these, 2 * width : 2 * width + 128].reshape(all_rows, 128).astype(f32)
            gate = jnp.sum(jnp.where(wide_lanes == expert, table, 0.0), axis=1, keepdims=True)
            tan = jnp.sum(
                jnp.where(wide_lanes == expert + 64, table, 0.0), axis=1, keepdims=True
            )
            pre = nn_dot(rows[:, these, 0:width].reshape(all_rows, width), wgu[l, :, cols])
            dots = nn_dot(
                rows[:, these, width : 2 * width].reshape(all_rows, width), wgu[l, :, cols]
            )
            pre_gate, pre_up = pre[:, 0:half], pre[:, half:hid]
            gate_dot, up_dot = dots[:, 0:half], dots[:, half:hid]
            sig = jax.nn.sigmoid(pre_gate)
            silu = pre_gate * sig
            slope_up = sig * (1.0 + pre_gate * (1.0 - sig)) * pre_up
            hidden = silu * pre_up
            mixed = tan * hidden + gate * (slope_up * gate_dot + silu * up_dot)
            keep_a[l, k] = gate * slope_up
            keep_s[l, k] = gate * silu
            keep_h[l, k] = hidden
            mix[l, :, pl.ds(pl.multiple_of(k * half, half), half)] = mixed.astype(bf)

    for kind, l in pieces[4:]:
        last_weights(kind, l)

    step = width // 4
    turns = [
        (part, own_part, mid, far, landed), (part2, own_part2, mid2, far2, landed2)
    ]
    x_copies, y_copies, z_copies, totals = {}, {}, {}, {}

    def place(turn, b, l, cols, term):
        parts, own = turns[turn][0:2]
        if l == 0:
            parts[b, at_x : at_x + n_lane, cols] = term[0:n_lane].astype(bf)
            own[b, :, cols] = term[n_lane:n_rows]
        else:
            own[b, :, cols] = own[b, :, cols] + term[0:n_lane]
            parts[b, at_y : at_y + n_lane, cols] = term[n_lane:n_rows].astype(bf)

    def send_side(turn, b, s):
        parts, far = turns[turn][0], turns[turn][3]
        peer, base = ((x_peer, at_x), (y_peer, at_y))[s]
        copies = (x_copies, y_copies)[s]
        for dz in (2, 1, 3, 0):
            copies[turn, b, dz] = push(
                parts.at[b, rows_of(base, dz)], far.at[b, s, rows_of(0, dz)],
                s_sems, (turn, b, s, dz), peer,
            )

    def merge(turn, b, dz):
        parts, own, mid, far, land = turns[turn]
        x_copies[turn, b, dz].wait_recv()
        y_copies[turn, b, dz].wait_recv()
        at = rows_of(0, dz)
        total = own[b, at, :] + (far[b, 0, at, :].astype(f32) + far[b, 1, at, :].astype(f32))
        if dz:
            mid[b, dz] = total.astype(bf)
            z_copies[turn, b, dz] = push(
                mid.at[b, dz], land.at[b, z], z_sems, (turn, b, dz), z_peers[dz - 1]
            )
        else:
            own[b, at, :] = total

    def total_of(turn, b):
        own, land = turns[turn][1], turns[turn][4]
        total = own[b, rows_of(0, 0), :]
        for dz in (1, 3, 2):
            z_copies[turn, b, dz].wait_recv()
            total = total + land[b, (z + 4 - dz) % 4].astype(f32)
        return total

    def down(b, l):
        @pl.loop(0, 4)
        def _(j):
            cols = pl.ds(pl.multiple_of(j * step, step), step)
            left = mix[l, b * n_rows : (b + 1) * n_rows, :]
            place(0, b, l, cols, nn_dot(left, wd[l, :, cols]))

        send_side(0, b, l)

    to_z, sides = {}, {}

    def image_to_sides(b, dz):
        block = image_rows.at[b, rows_of(at_own, 4 - dz)]
        for s, (peer, base) in enumerate(((x_peer, at_x), (y_peer, at_y))):
            sides[b, s, dz] = push(
                block, image_rows.at[b, rows_of(base, 4 - dz)], a_sems, (b, 1 + s, dz), peer
            )

    def image_of(b):
        image = total_of(0, b)
        image_ref[tokens_of(b), :] = image
        image_rows[b, mine, :] = image.astype(bf)
        block = image_rows.at[b, mine]
        for dz in (2, 1, 3):
            to_z[b, dz] = push(block, block, a_sems, (b, 0, dz), z_peers[dz - 1])
        image_to_sides(b, 0)

    def image_on(b, dz):
        to_z[b, dz].wait_recv()
        image_to_sides(b, dz)

    def backward(b, l):
        for dz in range(4):
            sides[b, l, dz].wait_recv()
        these = slice(l * n_lane, l * n_lane + n_rows)
        kept = slice(b * n_rows, (b + 1) * n_rows)
        cots = jnp.zeros((n_rows, 128), f32)
        for k in range(2):
            back = nt_dot(image_rows[b, these, :], wd[l, k * half : (k + 1) * half, :])
            cot = jnp.sum(back * keep_h[l, k, kept], axis=1, keepdims=True)
            cots = cots + jnp.where(wide_lanes[0:n_rows] == (z * 2 + k) * 2 + l, cot, 0.0)
            grads[l, :, k * hid : k * hid + half] = (back * keep_a[l, k, kept]).astype(bf)
            grads[l, :, k * hid + half : (k + 1) * hid] = (back * keep_s[l, k, kept]).astype(bf)
        place(1, b, l, slice(width, width + 128), cots)

        @pl.loop(0, 4)
        def _(j):
            cols = pl.ds(pl.multiple_of(j * step, step), step)
            place(1, b, l, cols, nt_dot(grads[l], wgu[l, cols, :]))

        send_side(1, b, l)

    def gram_of(b):
        total = total_of(1, b)
        these = tokens_of(b)
        expert_grad = total[:, 0:width]
        cot = total[:, width : width + 128]
        prob = prob_keep[these, :]
        column_grad = prob * (cot - jnp.sum(prob * cot, axis=1, keepdims=True))
        high = column_grad.astype(bf)
        rest = column_grad - high.astype(f32)
        middle = rest.astype(bf)
        low = (rest - middle.astype(f32)).astype(bf)
        router = router_pad[...]
        router_grad = nn_dot(high, router) + (nn_dot(middle, router) + nn_dot(low, router))
        xfull = tok_ref[these, :].astype(f32)
        inv_rms = inv_keep[these, 0:1]
        pulled = gain_ref[...] * (expert_grad + router_grad)
        gram_ref[these, :] = inv_rms * pulled - xfull * (inv_rms * inv_rms * inv_rms) * jnp.mean(
            pulled * xfull, axis=1, keepdims=True
        )

    need_weights(2, 0)
    down(0, 0)
    need_weights(2, 1)
    down(0, 1)
    down(1, 0)
    down(1, 1)
    for b in range(batches):
        for dz in (2, 1, 3, 0):
            merge(0, b, dz)
    for b in range(batches):
        image_of(b)
    for dz in (3, 1, 2):
        image_on(0, dz)
    backward(0, 0)
    for dz in (3, 1, 2):
        image_on(1, dz)
    backward(0, 1)
    backward(1, 0)
    backward(1, 1)
    for b in range(batches):
        for dz in (2, 1, 3, 0):
            merge(1, b, dz)
    for b in range(batches):
        gram_of(b)
    for copy in pending:
        copy.wait_send()


def on_device_dense(tokens, tangent, norm_gain, router, w_gate, w_up, w_down, routes):
    n_tok, width = tokens.shape
    hid = w_gate.shape[2]
    half = hid // 2
    n_sub = n_tok // batches
    n_lane = 4 * n_sub
    n_rows = 2 * n_lane
    bf, f32 = jnp.bfloat16, jnp.float32
    vm = pl.BlockSpec(memory_space=pltpu.VMEM)
    hbm = pl.BlockSpec(memory_space=pl.ANY)
    out = jax.ShapeDtypeStruct((n_tok, width), f32)
    dma = pltpu.SemaphoreType.DMA
    keep = pltpu.VMEM((2, 2, batches * n_rows, half), f32)

    def home(columns):
        return [
            pltpu.VMEM((batches, 3 * n_lane, columns), bf),
            pltpu.VMEM((batches, n_lane, columns), f32),
            pltpu.VMEM((batches, 4, n_sub, columns), bf),
            pltpu.VMEM((batches, 2, n_lane, columns), bf),
            pltpu.VMEM((batches, 4, n_sub, columns), bf),
        ]

    image, gram = pl.pallas_call(
        block_kernel,
        out_shape=(out, out),
        in_specs=[vm] * 5 + [hbm] * 3,
        out_specs=(vm, vm),
        scratch_shapes=[
            pltpu.VMEM((2, width, 2 * hid), bf),
            pltpu.VMEM((2, hid, width), bf),
            pltpu.VMEM((batches, 3 * n_lane, 2 * width + 128), bf),
            keep, keep, keep,
            pltpu.VMEM((2, batches * n_rows, hid), bf),
            *home(width),
            pltpu.VMEM((batches, 3 * n_lane, width), bf),
            pltpu.VMEM((2, n_rows, 2 * hid), bf),
            *home(width + 128),
            pltpu.VMEM((n_tok, 128), f32),
            pltpu.VMEM((n_tok, 128), f32),
            pltpu.VMEM((128, width), bf),
            dma((3, 2, 3)), dma((3, 2, 3)), dma((3, 2)),
            dma((3, 2, 4)), dma((3, 2, 4)),
            dma((3, 4)), dma((3, 4)), dma((batches, 3, 4)), dma((batches, 3, 4)),
            dma((2, batches, 2, 4)), dma((2, batches, 2, 4)),
            dma((2, batches, 4)), dma((2, batches, 4)),
        ],
        compiler_params=pltpu.CompilerParams(
            collective_id=0, has_side_effects=True, vmem_limit_bytes=60 * 2**20
        ),
        cost_estimate=pl.CostEstimate(
            flops=2 * 8 * 512 * width * hid, bytes_accessed=2**24, transcendentals=2**20
        ),
    )(tokens, tangent, norm_gain.reshape(1, width), router.T, routes.T, w_gate, w_up, w_down)
    return image, gram


def solution(mesh):
    in_specs = (
        P(("dp", "expert"), None),
        P(("dp", "expert"), None),
        P(),
        P(),
        P("expert", "dp", None),
        P("expert", "dp", None),
        P("expert", None, "dp"),
        P(("dp", "expert"), None),
    )
    out_specs = (P(("dp", "expert"), None), P(("dp", "expert"), None))
    body = on_device
    if mesh.shape["dp"] == 4 and mesh.shape["expert"] == 8:
        body = on_device_dense
    return jax.shard_map(
        body, mesh=mesh, in_specs=in_specs, out_specs=out_specs, check_vma=False
    )
```

```python
import jax
import jax.numpy as jnp
from jax import lax
from jax.experimental import pallas as pl
from jax.experimental.pallas import tpu as pltpu
from jax.sharding import PartitionSpec as P

eps_value = 1e-06


def pick_columns(table, routes):
    hits = routes[:, :, None] == jnp.arange(table.shape[1], dtype=jnp.int32)[None, None, :]
    return jnp.sum(jnp.where(hits, table[:, None, :], jnp.zeros((), table.dtype)), axis=2)


def on_device(tokens, tangent, norm_gain, router, w_gate, w_up, w_down, routes):
    tok_rows, topk = routes.shape
    model_width = tokens.shape[1]
    experts_all = router.shape[1]
    local_experts = w_gate.shape[0]
    groups = lax.axis_size("expert")
    capacity = 2 * tok_rows * topk // experts_all
    xfull = tokens.astype(jnp.float32)
    vfull = tangent.astype(jnp.float32)
    inv_rms = lax.rsqrt(jnp.mean(xfull * xfull, axis=1, keepdims=True) + eps_value)
    normed = (norm_gain * xfull * inv_rms).astype(jnp.bfloat16)
    cross_term = jnp.mean(xfull * vfull, axis=1, keepdims=True)
    normed_tan = (norm_gain * (vfull * inv_rms - xfull * inv_rms**3 * cross_term)).astype(
        jnp.bfloat16
    )
    logits = jnp.dot(normed, router, preferred_element_type=jnp.float32)
    logit_tan = jnp.dot(normed_tan, router, preferred_element_type=jnp.float32)
    selected = pick_columns(logits, routes)
    sel_tan = pick_columns(logit_tan, routes)
    exp_sel = jnp.exp(selected)
    gate_prob = exp_sel / jnp.sum(exp_sel, axis=1, keepdims=True)
    gate_tan = gate_prob * (sel_tan - jnp.sum(gate_prob * sel_tan, axis=1, keepdims=True))
    gate_b = gate_prob.astype(jnp.bfloat16)
    gate_tan_b = gate_tan.astype(jnp.bfloat16)
    pair_count = tok_rows * topk
    flat_ids = routes.reshape(-1)
    order = jnp.arange(pair_count, dtype=jnp.int32)
    earlier = (flat_ids[None, :] == flat_ids[:, None]) & (order[None, :] < order[:, None])
    slot_rank = jnp.sum(earlier.astype(jnp.int32), axis=1)
    slot_of_pair = flat_ids * capacity + slot_rank
    slot_hits = slot_of_pair[None, :] == jnp.arange(experts_all * capacity, dtype=jnp.int32)[:, None]
    slot_table = jnp.max(
        jnp.where(slot_hits, jnp.arange(pair_count, dtype=jnp.int32)[None, :], -1), axis=1
    )
    slot_valid = slot_table >= 0
    safe_pair = jnp.maximum(slot_table, 0)
    tok_idx = safe_pair // topk
    which_k = safe_pair % topk
    bf_zero = jnp.zeros((), jnp.bfloat16)
    send_rows = jnp.stack(
        (
            jnp.where(slot_valid[:, None], normed[tok_idx], bf_zero),
            jnp.where(slot_valid[:, None], normed_tan[tok_idx], bf_zero),
        )
    )
    send_rows = send_rows.reshape(2, groups, local_experts * capacity, model_width)
    send_gates = jnp.stack(
        (
            jnp.where(slot_valid, gate_b[tok_idx, which_k], bf_zero),
            jnp.where(slot_valid, gate_tan_b[tok_idx, which_k], bf_zero),
        )
    )
    send_gates = send_gates.reshape(2, groups, local_experts * capacity)
    recv_rows, recv_gates = (
        lax.all_to_all(send_rows, "expert", split_axis=1, concat_axis=1, tiled=True),
        lax.all_to_all(send_gates, "expert", split_axis=1, concat_axis=1, tiled=True),
    )
    slot_rows = recv_rows.reshape(2, groups, local_experts, capacity, model_width)
    recv_gates = recv_gates.reshape(2, groups, local_experts, capacity).astype(jnp.float32)
    gate_val = recv_gates[0][..., None]
    tan_val = recv_gates[1][..., None]
    gate_full, up_full, down_full = (
        lax.all_gather(w_gate, "dp", axis=1, tiled=True),
        lax.all_gather(w_up, "dp", axis=1, tiled=True),
        lax.all_gather(w_down, "dp", axis=2, tiled=True),
    )
    pre_both = jnp.einsum(
        "tslkd,ldf->tslkf", slot_rows, gate_full, preferred_element_type=jnp.float32
    )
    up_both = jnp.einsum("tslkd,ldf->tslkf", slot_rows, up_full, preferred_element_type=jnp.float32)
    pre_gate = pre_both[0]
    gate_dot = pre_both[1]
    pre_up = up_both[0]
    up_dot = up_both[1]
    sig_gate = jax.nn.sigmoid(pre_gate)
    silu_gate = pre_gate * sig_gate
    slope_gate = sig_gate * (1.0 + pre_gate * (1.0 - sig_gate))
    hidden = silu_gate * pre_up
    hidden_tan = slope_gate * gate_dot * pre_up + silu_gate * up_dot
    mixed_rows = (tan_val * hidden + gate_val * hidden_tan).astype(jnp.bfloat16)
    pair_image = jnp.einsum(
        "slkf,lfd->slkd", mixed_rows, down_full, preferred_element_type=jnp.float32
    )
    pair_send = pair_image.astype(jnp.bfloat16).reshape(
        groups, local_experts * capacity, model_width
    )
    pair_back = lax.all_to_all(pair_send, "expert", split_axis=0, concat_axis=0, tiled=True)
    pair_back = pair_back.reshape(experts_all * capacity, model_width)
    tangent_image = jnp.sum(
        pair_back[slot_of_pair].astype(jnp.float32).reshape(tok_rows, topk, model_width), axis=1
    )
    image_b = tangent_image.astype(jnp.bfloat16)
    send_cot = jnp.where(slot_valid[:, None], image_b[tok_idx], bf_zero).reshape(
        groups, local_experts * capacity, model_width
    )
    recv_cot = lax.all_to_all(send_cot, "expert", split_axis=0, concat_axis=0, tiled=True)
    recv_cot = recv_cot.reshape(groups, local_experts, capacity, model_width)
    back_hidden = jnp.einsum(
        "slkd,lfd->slkf", recv_cot, down_full, preferred_element_type=jnp.float32
    )
    gate_cot = jnp.sum(back_hidden * hidden, axis=3).astype(jnp.bfloat16)
    scaled = gate_val * back_hidden
    grad_gate = (scaled * pre_up * slope_gate).astype(jnp.bfloat16)
    grad_up = (scaled * silu_gate).astype(jnp.bfloat16)
    pair_grad = jnp.einsum(
        "slkf,ldf->slkd", grad_gate, gate_full, preferred_element_type=jnp.float32
    )
    pair_grad = pair_grad + jnp.einsum(
        "slkf,ldf->slkd", grad_up, up_full, preferred_element_type=jnp.float32
    )
    grad_send = pair_grad.astype(jnp.bfloat16).reshape(
        groups, local_experts * capacity, model_width
    )
    cot_send = gate_cot.reshape(groups, local_experts * capacity)
    grad_back, cot_back = (
        lax.all_to_all(grad_send, "expert", split_axis=0, concat_axis=0, tiled=True),
        lax.all_to_all(cot_send, "expert", split_axis=0, concat_axis=0, tiled=True),
    )
    grad_back = grad_back.reshape(experts_all * capacity, model_width)
    cot_back = cot_back.reshape(experts_all * capacity)
    expert_grad = jnp.sum(
        grad_back[slot_of_pair].astype(jnp.float32).reshape(tok_rows, topk, model_width), axis=1
    )
    pair_cot = cot_back[slot_of_pair].astype(jnp.float32).reshape(tok_rows, topk)
    logit_grad = gate_prob * (pair_cot - jnp.sum(gate_prob * pair_cot, axis=1, keepdims=True))
    hits = routes[:, :, None] == jnp.arange(experts_all, dtype=jnp.int32)[None, None, :]
    column_grad = jnp.sum(jnp.where(hits, logit_grad[:, :, None], 0.0), axis=1)
    router_grad = jnp.dot(
        column_grad, router.astype(jnp.float32).T, precision=lax.Precision.HIGHEST
    )
    pulled = norm_gain * (expert_grad + router_grad)
    gram_image = inv_rms * pulled - xfull * inv_rms**3 * jnp.mean(
        pulled * xfull, axis=1, keepdims=True
    )
    return (tangent_image, gram_image)


MESH = pl.DeviceIdType.MESH


def nt_dot(left, right):
    return lax.dot_general(
        left, right, (((1,), (1,)), ((), ())), preferred_element_type=jnp.float32
    )


def nn_dot(left, right):
    return jnp.dot(left, right, preferred_element_type=jnp.float32)


batches = 2


def block_kernel(
    tok_ref, tan_ref, gain_ref, router_ref, routes_ref, wg_ref, wu_ref, wd_ref,
    image_ref, gram_ref,
    wgu, wgu_t, wd, rows, keep_a, keep_s, keep_h, mix, part, own_part, mid, far, landed,
    image_rows, grads, part2, own_part2, mid2, far2, landed2, prob_keep, inv_keep, router_pad,
    w_send, w_recv, w_own, m_send, m_recv, t_send, t_recv, a_send, a_recv, s_send, s_recv,
    z_send, z_recv,
):
    f32, bf = jnp.float32, jnp.bfloat16
    n_tok, width = tok_ref.shape
    slab, hid = wg_ref.shape[1], wg_ref.shape[2]
    half = hid // 2
    n_sub = n_tok // batches
    n_lane = 4 * n_sub
    n_exp = router_ref.shape[0]
    dp, ex = lax.axis_index("dp"), lax.axis_index("expert")
    y, x = dp // 2, dp % 2
    z, core = ex // 2, ex % 2
    x_index, y_index = y * 2 + 1 - x, (1 - y) * 2 + x
    d_index = (1 - y) * 2 + 1 - x
    x_peer, y_peer = (x_index, ex), (y_index, ex)
    mate = (dp, z * 2 + 1 - core)
    z_peers = [(dp, (z + dz) % 4 * 2 + core) for dz in range(1, 4)]
    at_x, at_own, at_y = 0, n_lane, 2 * n_lane

    def rows_of(base, dz):
        return pl.ds(pl.multiple_of(base + (z + dz) % 4 * n_sub, n_sub), n_sub)

    def tokens_of(b):
        return slice(b * n_sub, (b + 1) * n_sub)

    barrier = pltpu.get_barrier_semaphore()
    friends = z_peers + [x_peer, y_peer, mate]
    for friend in friends:
        pl.semaphore_signal(barrier, inc=1, device_id=friend, device_id_type=MESH)
    pl.semaphore_wait(barrier, len(friends))

    pending = []

    def push(src, dst, sems, where, device):
        copy = pltpu.make_async_remote_copy(
            src_ref=src, dst_ref=dst, send_sem=sems[0].at[where], recv_sem=sems[1].at[where],
            device_id=device, device_id_type=MESH,
        )
        copy.start()
        pending.append(copy)
        return copy

    def slab_of(index):
        return pl.ds(pl.multiple_of(index * slab, slab), slab)

    def weight_at(kind, l, index):
        if kind == 2:
            return wd.at[l, pl.ds(pl.multiple_of(core * half, half), half), slab_of(index)]
        first = pl.multiple_of(core * hid + kind * half, half)
        return wgu.at[l, slab_of(index), pl.ds(first, half)]

    def weight_src(kind, l, which):
        part_of = pl.ds(pl.multiple_of(which * half, half), half)
        if kind == 2:
            return wd_ref.at[l, part_of, :]
        return (wg_ref, wu_ref)[kind].at[l, :, part_of]

    direct, relayed, shared, local = {}, {}, {}, {}
    w_sems, m_sems, t_sems = (w_send, w_recv), (m_send, m_recv), (t_send, t_recv)
    a_sems, s_sems, z_sems = (a_send, a_recv), (s_send, s_recv), (z_send, z_recv)

    def start_weights(kind, l):
        mine = weight_at(kind, l, dp)
        for_x, for_y = (1 - x, x) if l == 0 else (y, 1 - y)
        for_me = x if l == 0 else y
        direct[kind, l] = [
            push(weight_src(kind, l, for_x), mine, w_sems, (kind, l, 0), x_peer),
            push(weight_src(kind, l, for_y), mine, w_sems, (kind, l, 1), y_peer),
        ]
        local[kind, l] = pltpu.make_async_copy(
            weight_src(kind, l, for_me), mine, w_own.at[kind, l]
        )
        local[kind, l].start()
        shared[kind, l] = [
            push(weight_src(kind, l, for_me), mine, m_sems, (kind, l, 0), mate)
        ]

    def share_weights(kind, l, slot, index):
        block = weight_at(kind, l, index)
        shared[kind, l].append(push(block, block, m_sems, (kind, l, slot), mate))

    def relay_weights(kind, l):
        block = weight_at(kind, l, (x_index, y_index)[l])
        direct[kind, l][l].wait_recv()
        relayed[kind, l] = push(block, block, w_sems, (kind, l, 2), (y_peer, x_peer)[l])
        share_weights(kind, l, 1, (x_index, y_index)[l])
        direct[kind, l][1 - l].wait_recv()
        share_weights(kind, l, 2, (x_index, y_index)[1 - l])

    def last_weights(kind, l):
        relayed[kind, l].wait_recv()
        share_weights(kind, l, 3, d_index)

    def need_weights(kind, l):
        local[kind, l].wait()
        for copy in shared[kind, l]:
            copy.wait_recv()

    start_weights(0, 0)

    router_pad[...] = jnp.zeros(router_pad.shape, bf)
    router_pad[0:n_exp, :] = router_ref[...]
    xfull = tok_ref[...].astype(f32)
    vfull = tan_ref[...].astype(f32)
    gain = gain_ref[...]
    inv_rms = lax.rsqrt(jnp.mean(xfull * xfull, axis=1, keepdims=True) + eps_value)
    normed = (gain * xfull * inv_rms).astype(bf)
    cross_term = jnp.mean(xfull * vfull, axis=1, keepdims=True)
    inv_cube = inv_rms * inv_rms * inv_rms
    normed_tan = (gain * (vfull * inv_rms - xfull * inv_cube * cross_term)).astype(bf)
    mine = rows_of(at_own, 0)
    for b in range(batches):
        rows[b, mine, 0:width] = normed[tokens_of(b)]
        rows[b, mine, width : 2 * width] = normed_tan[tokens_of(b)]
    logits = nt_dot(normed, router_pad[...])
    logit_tan = nt_dot(normed_tan, router_pad[...])
    ids = lax.broadcasted_iota(jnp.int32, (128, n_tok), 0)
    chosen_by = jnp.zeros((128, n_tok), f32)
    for k in range(routes_ref.shape[0]):
        chosen_by = chosen_by + jnp.where(ids == routes_ref[k : k + 1, :], 1.0, 0.0)
    unit = jnp.where(
        lax.broadcasted_iota(jnp.int32, (n_tok, n_tok), 0)
        == lax.broadcasted_iota(jnp.int32, (n_tok, n_tok), 1),
        1.0, 0.0,
    ).astype(bf)
    chosen = nt_dot(unit, chosen_by.astype(bf))
    exp_sel = jnp.where(chosen > 0.5, jnp.exp(logits), 0.0)
    gate_prob = exp_sel / jnp.sum(exp_sel, axis=1, keepdims=True)
    gate_tan = gate_prob * (
        logit_tan - jnp.sum(gate_prob * logit_tan, axis=1, keepdims=True)
    )
    table = (gate_prob + pltpu.roll(gate_tan, 64, 1)).astype(bf)
    for b in range(batches):
        rows[b, mine, 2 * width : 2 * width + 128] = table[tokens_of(b)]
    prob_keep[...] = gate_prob
    inv_keep[...] = jnp.broadcast_to(inv_rms, (n_tok, 128))

    def along_z(buf, base, sems, which):
        block = buf.at[:, rows_of(base, 0)]
        return [push(block, block, sems, (which, dz), z_peers[dz - 1]) for dz in (2, 1, 3)]

    from_x = push(rows.at[:, mine], rows.at[:, rows_of(at_x, 0)], t_sems, (0, 0), x_peer)
    from_y = push(rows.at[:, mine], rows.at[:, rows_of(at_y, 0)], t_sems, (2, 0), y_peer)
    token_copies = along_z(rows, at_own, t_sems, 1)
    pieces = [(0, 0), (1, 0), (0, 1), (1, 1), (2, 0), (2, 1)]
    start_weights(1, 0)
    from_x.wait_recv()
    token_copies += along_z(rows, at_x, t_sems, 0)
    from_y.wait_recv()
    token_copies += along_z(rows, at_y, t_sems, 2)

    def turn_weights(l):
        need_weights(0, l)
        need_weights(1, l)

        @pl.loop(0, 4)
        def _(j):
            at = pl.ds(pl.multiple_of(j * slab, slab), slab)
            wgu_t[l, :, at] = wgu[l, at, :].T

    for i, (kind, l) in enumerate(pieces):
        relay_weights(kind, l)
        if i + 2 < len(pieces):
            start_weights(*pieces[i + 2])
        if 1 <= i <= 4:
            last_weights(*pieces[i - 1])
        if i in (2, 4):
            turn_weights(i // 2 - 1)
    for copy in token_copies:
        copy.wait_recv()

    n_rows = 2 * n_lane
    all_rows = batches * n_rows
    wide_lanes = lax.broadcasted_iota(jnp.int32, (all_rows, 128), 1)

    for l in range(2):
        these = slice(l * n_lane, l * n_lane + n_rows)

        @pl.loop(0, 2)
        def _(k):
            cols = pl.ds(pl.multiple_of(k * hid, hid), hid)
            expert = (z * 2 + k) * 2 + l
            table = rows[:, these, 2 * width : 2 * width + 128].reshape(all_rows, 128).astype(f32)
            gate = jnp.sum(jnp.where(wide_lanes == expert, table, 0.0), axis=1, keepdims=True)
            tan = jnp.sum(
                jnp.where(wide_lanes == expert + 64, table, 0.0), axis=1, keepdims=True
            )
            pre = nn_dot(rows[:, these, 0:width].reshape(all_rows, width), wgu[l, :, cols])
            dots = nn_dot(
                rows[:, these, width : 2 * width].reshape(all_rows, width), wgu[l, :, cols]
            )
            pre_gate, pre_up = pre[:, 0:half], pre[:, half:hid]
            gate_dot, up_dot = dots[:, 0:half], dots[:, half:hid]
            sig = jax.nn.sigmoid(pre_gate)
            silu = pre_gate * sig
            slope_up = sig * (1.0 + pre_gate * (1.0 - sig)) * pre_up
            hidden = silu * pre_up
            mixed = tan * hidden + gate * (slope_up * gate_dot + silu * up_dot)
            keep_a[l, k] = gate * slope_up
            keep_s[l, k] = gate * silu
            keep_h[l, k] = hidden
            mix[l, :, pl.ds(pl.multiple_of(k * half, half), half)] = mixed.astype(bf)

        last_weights(2, l)

    turns = [
        (part, own_part, mid, far, landed), (part2, own_part2, mid2, far2, landed2)
    ]
    x_copies, y_copies, z_copies, totals = {}, {}, {}, {}

    def place(turn, b, l, cols, term):
        parts, own = turns[turn][0:2]
        if l == 0:
            parts[b, at_x : at_x + n_lane, cols] = term[0:n_lane].astype(bf)
            own[b, :, cols] = term[n_lane:n_rows]
        else:
            own[b, :, cols] = own[b, :, cols] + term[0:n_lane]
            parts[b, at_y : at_y + n_lane, cols] = term[n_lane:n_rows].astype(bf)

    def send_side(turn, b, s):
        parts, far = turns[turn][0], turns[turn][3]
        peer, base = ((x_peer, at_x), (y_peer, at_y))[s]
        copies = (x_copies, y_copies)[s]
        for dz in (2, 1, 3, 0):
            copies[turn, b, dz] = push(
                parts.at[b, rows_of(base, dz)], far.at[b, s, rows_of(0, dz)],
                s_sems, (turn, b, s, dz), peer,
            )

    def merge(turn, b, dz):
        parts, own, mid, far, land = turns[turn]
        x_copies[turn, b, dz].wait_recv()
        y_copies[turn, b, dz].wait_recv()
        at = rows_of(0, dz)
        total = own[b, at, :] + (far[b, 0, at, :].astype(f32) + far[b, 1, at, :].astype(f32))
        if dz:
            mid[b, dz] = total.astype(bf)
            z_copies[turn, b, dz] = push(
                mid.at[b, dz], land.at[b, z], z_sems, (turn, b, dz), z_peers[dz - 1]
            )
        else:
            own[b, at, :] = total

    def total_of(turn, b):
        own, land = turns[turn][1], turns[turn][4]
        total = own[b, rows_of(0, 0), :]
        for dz in (1, 3, 2):
            z_copies[turn, b, dz].wait_recv()
            total = total + land[b, (z + 4 - dz) % 4].astype(f32)
        return total

    def down(b, l):
        left = mix[l, b * n_rows : (b + 1) * n_rows, :]
        place(0, b, l, slice(0, width), nn_dot(left, wd[l]))
        send_side(0, b, l)

    to_z, sides = {}, {}

    def image_to_sides(b, dz):
        block = image_rows.at[b, rows_of(at_own, 4 - dz)]
        for s, (peer, base) in enumerate(((x_peer, at_x), (y_peer, at_y))):
            sides[b, s, dz] = push(
                block, image_rows.at[b, rows_of(base, 4 - dz)], a_sems, (b, 1 + s, dz), peer
            )

    def image_of(b):
        image = total_of(0, b)
        image_ref[tokens_of(b), :] = image
        image_rows[b, mine, :] = image.astype(bf)
        block = image_rows.at[b, mine]
        for dz in (2, 1, 3):
            to_z[b, dz] = push(block, block, a_sems, (b, 0, dz), z_peers[dz - 1])
        image_to_sides(b, 0)

    def image_on(b, dz):
        to_z[b, dz].wait_recv()
        image_to_sides(b, dz)

    def backward(b, l):
        for dz in range(4):
            sides[b, l, dz].wait_recv()
        these = slice(l * n_lane, l * n_lane + n_rows)
        kept = slice(b * n_rows, (b + 1) * n_rows)
        cots = jnp.zeros((n_rows, 128), f32)
        back_both = nt_dot(image_rows[b, these, :], wd[l])
        for k in range(2):
            back = back_both[:, k * half : (k + 1) * half]
            cot = jnp.sum(back * keep_h[l, k, kept], axis=1, keepdims=True)
            cots = cots + jnp.where(wide_lanes[0:n_rows] == (z * 2 + k) * 2 + l, cot, 0.0)
            grads[l, :, k * hid : k * hid + half] = (back * keep_a[l, k, kept]).astype(bf)
            grads[l, :, k * hid + half : (k + 1) * hid] = (back * keep_s[l, k, kept]).astype(bf)
        place(1, b, l, slice(width, width + 128), cots)
        place(1, b, l, slice(0, width), nn_dot(grads[l], wgu_t[l]))
        send_side(1, b, l)

    def gram_of(b):
        total = total_of(1, b)
        these = tokens_of(b)
        expert_grad = total[:, 0:width]
        cot = total[:, width : width + 128]
        prob = prob_keep[these, :]
        column_grad = prob * (cot - jnp.sum(prob * cot, axis=1, keepdims=True))
        high = column_grad.astype(bf)
        rest = column_grad - high.astype(f32)
        middle = rest.astype(bf)
        low = (rest - middle.astype(f32)).astype(bf)
        router = router_pad[...]
        router_grad = nn_dot(high, router) + (nn_dot(middle, router) + nn_dot(low, router))
        xfull = tok_ref[these, :].astype(f32)
        inv_rms = inv_keep[these, 0:1]
        pulled = gain_ref[...] * (expert_grad + router_grad)
        gram_ref[these, :] = inv_rms * pulled - xfull * (inv_rms * inv_rms * inv_rms) * jnp.mean(
            pulled * xfull, axis=1, keepdims=True
        )

    need_weights(2, 0)
    down(0,0)
    need_weights(2, 1)
    down(0,1)
    down(1,0)
    down(1,1)
    merge(0,0,2)
    merge(0,0,1)
    merge(0,0,3)
    merge(0,0,0)
    merge(0,1,2)
    merge(0,1,1)
    image_of(0)
    merge(0,1,3)
    merge(0,1,0)
    image_on(0,3)
    image_on(0,1)
    image_of(1)
    image_on(0,2)
    image_on(1,3)
    image_on(1,1)
    image_on(1,2)
    backward(0,0)
    backward(0,1)
    backward(1,0)
    backward(1,1)
    merge(1,0,2)
    merge(1,0,1)
    merge(1,0,3)
    merge(1,0,0)
    merge(1,1,2)
    merge(1,1,1)
    merge(1,1,3)
    merge(1,1,0)
    gram_of(0)
    gram_of(1)
    for copy in pending:
        copy.wait_send()


def on_device_dense(tokens, tangent, norm_gain, router, w_gate, w_up, w_down, routes):
    n_tok, width = tokens.shape
    hid = w_gate.shape[2]
    half = hid // 2
    n_sub = n_tok // batches
    n_lane = 4 * n_sub
    n_rows = 2 * n_lane
    bf, f32 = jnp.bfloat16, jnp.float32
    vm = pl.BlockSpec(memory_space=pltpu.VMEM)
    hbm = pl.BlockSpec(memory_space=pl.ANY)
    out = jax.ShapeDtypeStruct((n_tok, width), f32)
    dma = pltpu.SemaphoreType.DMA
    keep = pltpu.VMEM((2, 2, batches * n_rows, half), f32)

    def home(columns):
        return [
            pltpu.VMEM((batches, 3 * n_lane, columns), bf),
            pltpu.VMEM((batches, n_lane, columns), f32),
            pltpu.VMEM((batches, 4, n_sub, columns), bf),
            pltpu.VMEM((batches, 2, n_lane, columns), bf),
            pltpu.VMEM((batches, 4, n_sub, columns), bf),
        ]

    image, gram = pl.pallas_call(
        block_kernel,
        out_shape=(out, out),
        in_specs=[vm] * 5 + [hbm] * 3,
        out_specs=(vm, vm),
        scratch_shapes=[
            pltpu.VMEM((2, width, 2 * hid), bf),
            pltpu.VMEM((2, 2 * hid, width), bf),
            pltpu.VMEM((2, hid, width), bf),
            pltpu.VMEM((batches, 3 * n_lane, 2 * width + 128), bf),
            keep, keep, keep,
            pltpu.VMEM((2, batches * n_rows, hid), bf),
            *home(width),
            pltpu.VMEM((batches, 3 * n_lane, width), bf),
            pltpu.VMEM((2, n_rows, 2 * hid), bf),
            *home(width + 128),
            pltpu.VMEM((n_tok, 128), f32),
            pltpu.VMEM((n_tok, 128), f32),
            pltpu.VMEM((128, width), bf),
            dma((3, 2, 3)), dma((3, 2, 3)), dma((3, 2)),
            dma((3, 2, 4)), dma((3, 2, 4)),
            dma((3, 4)), dma((3, 4)), dma((batches, 3, 4)), dma((batches, 3, 4)),
            dma((2, batches, 2, 4)), dma((2, batches, 2, 4)),
            dma((2, batches, 4)), dma((2, batches, 4)),
        ],
        compiler_params=pltpu.CompilerParams(
            collective_id=0, has_side_effects=True, vmem_limit_bytes=60 * 2**20
        ),
        cost_estimate=pl.CostEstimate(
            flops=2 * 8 * 512 * width * hid, bytes_accessed=2**24, transcendentals=2**20
        ),
    )(tokens, tangent, norm_gain.reshape(1, width), router.T, routes.T, w_gate, w_up, w_down)
    return image, gram


def solution(mesh):
    in_specs = (
        P(("dp", "expert"), None),
        P(("dp", "expert"), None),
        P(),
        P(),
        P("expert", "dp", None),
        P("expert", "dp", None),
        P("expert", None, "dp"),
        P(("dp", "expert"), None),
    )
    out_specs = (P(("dp", "expert"), None), P(("dp", "expert"), None))
    body = on_device
    if mesh.shape["dp"] == 4 and mesh.shape["expert"] == 8:
        body = on_device_dense
    return jax.shard_map(
        body, mesh=mesh, in_specs=in_specs, out_specs=out_specs, check_vma=False
    )
```

```python
import functools

import jax
import jax.numpy as jnp
from jax import lax
from jax.experimental import pallas as pl
from jax.experimental.pallas import tpu as pltpu
from jax.sharding import PartitionSpec as P

eps_value = 1e-06


def pick_columns(table, routes):
    hits = routes[:, :, None] == jnp.arange(table.shape[1], dtype=jnp.int32)[None, None, :]
    return jnp.sum(jnp.where(hits, table[:, None, :], jnp.zeros((), table.dtype)), axis=2)


def on_device(tokens, tangent, norm_gain, router, w_gate, w_up, w_down, routes):
    tok_rows, topk = routes.shape
    model_width = tokens.shape[1]
    experts_all = router.shape[1]
    local_experts = w_gate.shape[0]
    groups = lax.axis_size("expert")
    capacity = 2 * tok_rows * topk // experts_all
    xfull = tokens.astype(jnp.float32)
    vfull = tangent.astype(jnp.float32)
    inv_rms = lax.rsqrt(jnp.mean(xfull * xfull, axis=1, keepdims=True) + eps_value)
    normed = (norm_gain * xfull * inv_rms).astype(jnp.bfloat16)
    cross_term = jnp.mean(xfull * vfull, axis=1, keepdims=True)
    normed_tan = (norm_gain * (vfull * inv_rms - xfull * inv_rms**3 * cross_term)).astype(
        jnp.bfloat16
    )
    logits = jnp.dot(normed, router, preferred_element_type=jnp.float32)
    logit_tan = jnp.dot(normed_tan, router, preferred_element_type=jnp.float32)
    selected = pick_columns(logits, routes)
    sel_tan = pick_columns(logit_tan, routes)
    exp_sel = jnp.exp(selected)
    gate_prob = exp_sel / jnp.sum(exp_sel, axis=1, keepdims=True)
    gate_tan = gate_prob * (sel_tan - jnp.sum(gate_prob * sel_tan, axis=1, keepdims=True))
    gate_b = gate_prob.astype(jnp.bfloat16)
    gate_tan_b = gate_tan.astype(jnp.bfloat16)
    pair_count = tok_rows * topk
    flat_ids = routes.reshape(-1)
    order = jnp.arange(pair_count, dtype=jnp.int32)
    earlier = (flat_ids[None, :] == flat_ids[:, None]) & (order[None, :] < order[:, None])
    slot_rank = jnp.sum(earlier.astype(jnp.int32), axis=1)
    slot_of_pair = flat_ids * capacity + slot_rank
    slot_hits = slot_of_pair[None, :] == jnp.arange(experts_all * capacity, dtype=jnp.int32)[:, None]
    slot_table = jnp.max(
        jnp.where(slot_hits, jnp.arange(pair_count, dtype=jnp.int32)[None, :], -1), axis=1
    )
    slot_valid = slot_table >= 0
    safe_pair = jnp.maximum(slot_table, 0)
    tok_idx = safe_pair // topk
    which_k = safe_pair % topk
    bf_zero = jnp.zeros((), jnp.bfloat16)
    send_rows = jnp.stack(
        (
            jnp.where(slot_valid[:, None], normed[tok_idx], bf_zero),
            jnp.where(slot_valid[:, None], normed_tan[tok_idx], bf_zero),
        )
    )
    send_rows = send_rows.reshape(2, groups, local_experts * capacity, model_width)
    send_gates = jnp.stack(
        (
            jnp.where(slot_valid, gate_b[tok_idx, which_k], bf_zero),
            jnp.where(slot_valid, gate_tan_b[tok_idx, which_k], bf_zero),
        )
    )
    send_gates = send_gates.reshape(2, groups, local_experts * capacity)
    recv_rows, recv_gates = (
        lax.all_to_all(send_rows, "expert", split_axis=1, concat_axis=1, tiled=True),
        lax.all_to_all(send_gates, "expert", split_axis=1, concat_axis=1, tiled=True),
    )
    slot_rows = recv_rows.reshape(2, groups, local_experts, capacity, model_width)
    recv_gates = recv_gates.reshape(2, groups, local_experts, capacity).astype(jnp.float32)
    gate_val = recv_gates[0][..., None]
    tan_val = recv_gates[1][..., None]
    gate_full, up_full, down_full = (
        lax.all_gather(w_gate, "dp", axis=1, tiled=True),
        lax.all_gather(w_up, "dp", axis=1, tiled=True),
        lax.all_gather(w_down, "dp", axis=2, tiled=True),
    )
    pre_both = jnp.einsum(
        "tslkd,ldf->tslkf", slot_rows, gate_full, preferred_element_type=jnp.float32
    )
    up_both = jnp.einsum("tslkd,ldf->tslkf", slot_rows, up_full, preferred_element_type=jnp.float32)
    pre_gate = pre_both[0]
    gate_dot = pre_both[1]
    pre_up = up_both[0]
    up_dot = up_both[1]
    sig_gate = jax.nn.sigmoid(pre_gate)
    silu_gate = pre_gate * sig_gate
    slope_gate = sig_gate * (1.0 + pre_gate * (1.0 - sig_gate))
    hidden = silu_gate * pre_up
    hidden_tan = slope_gate * gate_dot * pre_up + silu_gate * up_dot
    mixed_rows = (tan_val * hidden + gate_val * hidden_tan).astype(jnp.bfloat16)
    pair_image = jnp.einsum(
        "slkf,lfd->slkd", mixed_rows, down_full, preferred_element_type=jnp.float32
    )
    pair_send = pair_image.astype(jnp.bfloat16).reshape(
        groups, local_experts * capacity, model_width
    )
    pair_back = lax.all_to_all(pair_send, "expert", split_axis=0, concat_axis=0, tiled=True)
    pair_back = pair_back.reshape(experts_all * capacity, model_width)
    tangent_image = jnp.sum(
        pair_back[slot_of_pair].astype(jnp.float32).reshape(tok_rows, topk, model_width), axis=1
    )
    image_b = tangent_image.astype(jnp.bfloat16)
    send_cot = jnp.where(slot_valid[:, None], image_b[tok_idx], bf_zero).reshape(
        groups, local_experts * capacity, model_width
    )
    recv_cot = lax.all_to_all(send_cot, "expert", split_axis=0, concat_axis=0, tiled=True)
    recv_cot = recv_cot.reshape(groups, local_experts, capacity, model_width)
    back_hidden = jnp.einsum(
        "slkd,lfd->slkf", recv_cot, down_full, preferred_element_type=jnp.float32
    )
    gate_cot = jnp.sum(back_hidden * hidden, axis=3).astype(jnp.bfloat16)
    scaled = gate_val * back_hidden
    grad_gate = (scaled * pre_up * slope_gate).astype(jnp.bfloat16)
    grad_up = (scaled * silu_gate).astype(jnp.bfloat16)
    pair_grad = jnp.einsum(
        "slkf,ldf->slkd", grad_gate, gate_full, preferred_element_type=jnp.float32
    )
    pair_grad = pair_grad + jnp.einsum(
        "slkf,ldf->slkd", grad_up, up_full, preferred_element_type=jnp.float32
    )
    grad_send = pair_grad.astype(jnp.bfloat16).reshape(
        groups, local_experts * capacity, model_width
    )
    cot_send = gate_cot.reshape(groups, local_experts * capacity)
    grad_back, cot_back = (
        lax.all_to_all(grad_send, "expert", split_axis=0, concat_axis=0, tiled=True),
        lax.all_to_all(cot_send, "expert", split_axis=0, concat_axis=0, tiled=True),
    )
    grad_back = grad_back.reshape(experts_all * capacity, model_width)
    cot_back = cot_back.reshape(experts_all * capacity)
    expert_grad = jnp.sum(
        grad_back[slot_of_pair].astype(jnp.float32).reshape(tok_rows, topk, model_width), axis=1
    )
    pair_cot = cot_back[slot_of_pair].astype(jnp.float32).reshape(tok_rows, topk)
    logit_grad = gate_prob * (pair_cot - jnp.sum(gate_prob * pair_cot, axis=1, keepdims=True))
    hits = routes[:, :, None] == jnp.arange(experts_all, dtype=jnp.int32)[None, None, :]
    column_grad = jnp.sum(jnp.where(hits, logit_grad[:, :, None], 0.0), axis=1)
    router_grad = jnp.dot(
        column_grad, router.astype(jnp.float32).T, precision=lax.Precision.HIGHEST
    )
    pulled = norm_gain * (expert_grad + router_grad)
    gram_image = inv_rms * pulled - xfull * inv_rms**3 * jnp.mean(
        pulled * xfull, axis=1, keepdims=True
    )
    return (tangent_image, gram_image)


MESH = pl.DeviceIdType.MESH


def nt_dot(left, right):
    return lax.dot_general(
        left, right, (((1,), (1,)), ((), ())), preferred_element_type=jnp.float32
    )


def nn_dot(left, right):
    return jnp.dot(left, right, preferred_element_type=jnp.float32)


batches = 2


def block_kernel(
    tok_ref, tan_ref, gain_ref, router_ref, routes_ref, wg_ref, wu_ref, wd_ref,
    both_ref,
    wgu, wgu_t, wd, rows, keep_a, keep_s, keep_h, mix, part, own_part, mid, far, landed,
    image_rows, grads, part2, own_part2, mid2, far2, landed2, prob_keep, inv_keep, router_pad,
    w_send, w_recv, w_own, m_send, m_recv, t_send, t_recv, a_send, a_recv, s_send, s_recv,
    z_send, z_recv,
):
    f32, bf = jnp.float32, jnp.bfloat16
    n_tok, width = tok_ref.shape
    slab, hid = wg_ref.shape[1], wg_ref.shape[2]
    half = hid // 2
    n_sub = n_tok // batches
    n_lane = 4 * n_sub
    n_exp = router_ref.shape[0]
    dp, ex = lax.axis_index("dp"), lax.axis_index("expert")
    y, x = dp // 2, dp % 2
    z, core = ex // 2, ex % 2
    x_index, y_index = y * 2 + 1 - x, (1 - y) * 2 + x
    d_index = (1 - y) * 2 + 1 - x
    x_peer, y_peer = (x_index, ex), (y_index, ex)
    mate = (dp, z * 2 + 1 - core)
    z_peers = [(dp, (z + dz) % 4 * 2 + core) for dz in range(1, 4)]
    at_x, at_own, at_y = 0, n_lane, 2 * n_lane

    def rows_of(base, dz):
        return pl.ds(pl.multiple_of(base + (z + dz) % 4 * n_sub, n_sub), n_sub)

    def tokens_of(b):
        return slice(b * n_sub, (b + 1) * n_sub)

    barrier = pltpu.get_barrier_semaphore()
    friends = [
        (x_peer, None), (y_peer, None), (mate, None), (z_peers[0], z < 3), (z_peers[2], z > 0)
    ]

    def greet(friend):
        pl.semaphore_signal(barrier, inc=1, device_id=friend, device_id_type=MESH)

    for friend, cond in friends:
        if cond is None:
            greet(friend)
        else:
            pl.when(cond)(functools.partial(greet, friend))
    inner = jnp.where(z > 0, 1, 0) * jnp.where(z < 3, 1, 0)
    pl.semaphore_wait(barrier, 4 + inner)

    pending = []

    def push(src, dst, sems, where, device, cond=None):
        copy = pltpu.make_async_remote_copy(
            src_ref=src, dst_ref=dst, send_sem=sems[0].at[where], recv_sem=sems[1].at[where],
            device_id=device, device_id_type=MESH,
        )
        if cond is None:
            copy.start()
        else:
            pl.when(cond)(copy.start)
        pending.append((copy, cond))
        return copy

    def slab_of(index):
        return pl.ds(pl.multiple_of(index * slab, slab), slab)

    def weight_at(kind, l, index):
        if kind == 2:
            return wd.at[l, pl.ds(pl.multiple_of(core * half, half), half), slab_of(index)]
        first = pl.multiple_of(core * hid + kind * half, half)
        return wgu.at[l, slab_of(index), pl.ds(first, half)]

    def weight_src(kind, l, which):
        part_of = pl.ds(pl.multiple_of(which * half, half), half)
        if kind == 2:
            return wd_ref.at[l, part_of, :]
        return (wg_ref, wu_ref)[kind].at[l, :, part_of]

    direct, relayed, shared, local = {}, {}, {}, {}
    w_sems, m_sems, t_sems = (w_send, w_recv), (m_send, m_recv), (t_send, t_recv)
    a_sems, s_sems, z_sems = (a_send, a_recv), (s_send, s_recv), (z_send, z_recv)

    def start_weights(kind):
        for p, l in ((0, 0), (1, 1), (0, 1), (1, 0)):
            for_x, for_y = (1 - x, x) if l == 0 else (y, 1 - y)
            direct[kind, l, p] = push(
                weight_src(kind, l, (for_x, for_y)[p]), weight_at(kind, l, dp),
                w_sems, (kind, l, p), (x_peer, y_peer)[p],
            )
        for l in range(2):
            for_me = (x, y)[l]
            mine = weight_at(kind, l, dp)
            local[kind, l] = pltpu.make_async_copy(
                weight_src(kind, l, for_me), mine, w_own.at[kind, l]
            )
            local[kind, l].start()
            shared[kind, l] = [
                push(weight_src(kind, l, for_me), mine, m_sems, (kind, l, 0), mate)
            ]

    def share_weights(kind, l, slot, index):
        block = weight_at(kind, l, index)
        shared[kind, l].append(push(block, block, m_sems, (kind, l, slot), mate))

    def relay_weights(kind):
        for l in range(2):
            index = (x_index, y_index)[l]
            block = weight_at(kind, l, index)
            direct[kind, l, l].wait_recv()
            relayed[kind, l] = push(block, block, w_sems, (kind, l, 2), (y_peer, x_peer)[l])
            share_weights(kind, l, 1, index)

    def side_weights(kind):
        for l in range(2):
            direct[kind, l, 1 - l].wait_recv()
            share_weights(kind, l, 2, (x_index, y_index)[1 - l])

    def last_weights(kind, l):
        relayed[kind, l].wait_recv()
        share_weights(kind, l, 3, d_index)

    def need_weights(kind, l):
        local[kind, l].wait()
        for copy in shared[kind, l]:
            copy.wait_recv()

    start_weights(0)

    router_pad[...] = jnp.zeros(router_pad.shape, bf)
    router_pad[0:n_exp, :] = router_ref[...]
    xfull = tok_ref[...].astype(f32)
    vfull = tan_ref[...].astype(f32)
    gain = gain_ref[...]
    inv_rms = lax.rsqrt(jnp.mean(xfull * xfull, axis=1, keepdims=True) + eps_value)
    normed = (gain * xfull * inv_rms).astype(bf)
    cross_term = jnp.mean(xfull * vfull, axis=1, keepdims=True)
    inv_cube = inv_rms * inv_rms * inv_rms
    normed_tan = (gain * (vfull * inv_rms - xfull * inv_cube * cross_term)).astype(bf)
    mine = rows_of(at_own, 0)
    for b in range(batches):
        rows[b, mine, 0:width] = normed[tokens_of(b)]
        rows[b, mine, width : 2 * width] = normed_tan[tokens_of(b)]
    logits = nt_dot(normed, router_pad[...])
    logit_tan = nt_dot(normed_tan, router_pad[...])
    ids = lax.broadcasted_iota(jnp.int32, (128, n_tok), 0)
    chosen_by = jnp.zeros((128, n_tok), f32)
    for k in range(routes_ref.shape[0]):
        chosen_by = chosen_by + jnp.where(ids == routes_ref[k : k + 1, :], 1.0, 0.0)
    unit = jnp.where(
        lax.broadcasted_iota(jnp.int32, (n_tok, n_tok), 0)
        == lax.broadcasted_iota(jnp.int32, (n_tok, n_tok), 1),
        1.0, 0.0,
    ).astype(bf)
    chosen = nt_dot(unit, chosen_by.astype(bf))
    exp_sel = jnp.where(chosen > 0.5, jnp.exp(logits), 0.0)
    gate_prob = exp_sel / jnp.sum(exp_sel, axis=1, keepdims=True)
    gate_tan = gate_prob * (
        logit_tan - jnp.sum(gate_prob * logit_tan, axis=1, keepdims=True)
    )
    table = (gate_prob + pltpu.roll(gate_tan, 64, 1)).astype(bf)
    for b in range(batches):
        rows[b, mine, 2 * width : 2 * width + 128] = table[tokens_of(b)]
    prob_keep[...] = gate_prob
    inv_keep[...] = jnp.broadcast_to(inv_rms, (n_tok, 128))

    ups, downs = {}, {}
    bases = (at_x, at_own, at_y)

    def has_up(j):
        return jnp.logical_and(z < 3, z >= j)

    def has_down(j):
        return jnp.logical_and(z > 0, z + j <= 3)

    def chain(which, j):
        if j:
            pl.when(z >= j)(ups[which, j - 1].wait_recv)
            pl.when(z + j <= 3)(downs[which, j - 1].wait_recv)
        if j < 3:
            above = rows.at[:, rows_of(bases[which], 4 - j)]
            below = rows.at[:, rows_of(bases[which], j)]
            ups[which, j] = push(above, above, t_sems, (which, 0, j), z_peers[0], has_up(j))
            downs[which, j] = push(below, below, t_sems, (which, 1, j), z_peers[2], has_down(j))

    from_x = push(rows.at[:, mine], rows.at[:, rows_of(at_x, 0)], t_sems, (0, 2, 0), x_peer)
    from_y = push(rows.at[:, mine], rows.at[:, rows_of(at_y, 0)], t_sems, (2, 2, 0), y_peer)
    chain(1, 0)
    start_weights(1)
    from_x.wait_recv()
    chain(0, 0)
    from_y.wait_recv()
    chain(2, 0)
    relay_weights(0)
    for which in (1, 0, 2):
        chain(which, 1)
    side_weights(0)
    relay_weights(1)
    start_weights(2)
    for which in (1, 0, 2):
        chain(which, 2)
    side_weights(1)
    for kind in range(2):
        for l in range(2):
            last_weights(kind, l)

    def turn_weights(l):
        need_weights(0, l)
        need_weights(1, l)

        @pl.loop(0, 4)
        def _(j):
            at = pl.ds(pl.multiple_of(j * slab, slab), slab)
            wgu_t[l, :, at] = wgu[l, at, :].T

    turn_weights(0)
    turn_weights(1)
    relay_weights(2)
    side_weights(2)
    for which in (1, 0, 2):
        chain(which, 3)

    n_rows = 2 * n_lane
    all_rows = batches * n_rows
    wide_lanes = lax.broadcasted_iota(jnp.int32, (all_rows, 128), 1)

    for l in range(2):
        these = slice(l * n_lane, l * n_lane + n_rows)

        @pl.loop(0, 2)
        def _(k):
            cols = pl.ds(pl.multiple_of(k * hid, hid), hid)
            expert = (z * 2 + k) * 2 + l
            table = rows[:, these, 2 * width : 2 * width + 128].reshape(all_rows, 128).astype(f32)
            gate = jnp.sum(jnp.where(wide_lanes == expert, table, 0.0), axis=1, keepdims=True)
            tan = jnp.sum(
                jnp.where(wide_lanes == expert + 64, table, 0.0), axis=1, keepdims=True
            )
            pre = nn_dot(rows[:, these, 0:width].reshape(all_rows, width), wgu[l, :, cols])
            dots = nn_dot(
                rows[:, these, width : 2 * width].reshape(all_rows, width), wgu[l, :, cols]
            )
            pre_gate, pre_up = pre[:, 0:half], pre[:, half:hid]
            gate_dot, up_dot = dots[:, 0:half], dots[:, half:hid]
            sig = jax.nn.sigmoid(pre_gate)
            silu = pre_gate * sig
            slope_up = sig * (1.0 + pre_gate * (1.0 - sig)) * pre_up
            hidden = silu * pre_up
            mixed = tan * hidden + gate * (slope_up * gate_dot + silu * up_dot)
            keep_a[l, k] = gate * slope_up
            keep_s[l, k] = gate * silu
            keep_h[l, k] = hidden
            mix[l, :, pl.ds(pl.multiple_of(k * half, half), half)] = mixed.astype(bf)

    turns = [
        (part, own_part, mid, far, landed), (part2, own_part2, mid2, far2, landed2)
    ]
    x_copies, y_copies, z_copies, totals = {}, {}, {}, {}

    def place(turn, b, l, cols, term):
        parts, own = turns[turn][0:2]
        if l == 0:
            parts[b, at_x : at_x + n_lane, cols] = term[0:n_lane].astype(bf)
            own[b, :, cols] = term[n_lane:n_rows]
        else:
            own[b, :, cols] = own[b, :, cols] + term[0:n_lane]
            parts[b, at_y : at_y + n_lane, cols] = term[n_lane:n_rows].astype(bf)

    def send_side(turn, b, s):
        parts, far = turns[turn][0], turns[turn][3]
        peer, base = ((x_peer, at_x), (y_peer, at_y))[s]
        copies = (x_copies, y_copies)[s]
        for dz in (2, 1, 3, 0):
            copies[turn, b, dz] = push(
                parts.at[b, rows_of(base, dz)], far.at[b, s, rows_of(0, dz)],
                s_sems, (turn, b, s, dz), peer,
            )

    def merge(turn, b, dz):
        parts, own, mid, far, land = turns[turn]
        x_copies[turn, b, dz].wait_recv()
        y_copies[turn, b, dz].wait_recv()
        at = rows_of(0, dz)
        total = own[b, at, :] + (far[b, 0, at, :].astype(f32) + far[b, 1, at, :].astype(f32))
        if dz:
            mid[b, dz] = total.astype(bf)
            z_copies[turn, b, dz] = push(
                mid.at[b, dz], land.at[b, z], z_sems, (turn, b, dz), z_peers[dz - 1]
            )
        else:
            own[b, at, :] = total

    def total_of(turn, b):
        own, land = turns[turn][1], turns[turn][4]
        total = own[b, rows_of(0, 0), :]
        for dz in (1, 3, 2):
            z_copies[turn, b, dz].wait_recv()
            total = total + land[b, (z + 4 - dz) % 4].astype(f32)
        return total

    def down(b, l):
        left = mix[l, b * n_rows : (b + 1) * n_rows, :]
        place(0, b, l, slice(0, width), nn_dot(left, wd[l]))
        send_side(0, b, l)

    to_z, sides = {}, {}

    def image_to_sides(b, dz):
        block = image_rows.at[b, rows_of(at_own, 4 - dz)]
        for s, (peer, base) in enumerate(((x_peer, at_x), (y_peer, at_y))):
            sides[b, s, dz] = push(
                block, image_rows.at[b, rows_of(base, 4 - dz)], a_sems, (b, 1 + s, dz), peer
            )

    def image_of(b):
        image = total_of(0, b)
        both_ref[tokens_of(b), 0:width] = image
        image_rows[b, mine, :] = image.astype(bf)
        block = image_rows.at[b, mine]
        for dz in (2, 1, 3):
            to_z[b, dz] = push(block, block, a_sems, (b, 0, dz), z_peers[dz - 1])
        image_to_sides(b, 0)

    def image_on(b, dz):
        to_z[b, dz].wait_recv()
        image_to_sides(b, dz)

    def backward(b, l):
        for dz in range(4):
            sides[b, l, dz].wait_recv()
        these = slice(l * n_lane, l * n_lane + n_rows)
        kept = slice(b * n_rows, (b + 1) * n_rows)
        cots = jnp.zeros((n_rows, 128), f32)
        back_both = nt_dot(image_rows[b, these, :], wd[l])
        for k in range(2):
            back = back_both[:, k * half : (k + 1) * half]
            cot = jnp.sum(back * keep_h[l, k, kept], axis=1, keepdims=True)
            cots = cots + jnp.where(wide_lanes[0:n_rows] == (z * 2 + k) * 2 + l, cot, 0.0)
            grads[l, :, k * hid : k * hid + half] = (back * keep_a[l, k, kept]).astype(bf)
            grads[l, :, k * hid + half : (k + 1) * hid] = (back * keep_s[l, k, kept]).astype(bf)
        place(1, b, l, slice(width, width + 128), cots)
        place(1, b, l, slice(0, width), nn_dot(grads[l], wgu_t[l]))
        send_side(1, b, l)

    def gram_of(b):
        total = total_of(1, b)
        these = tokens_of(b)
        expert_grad = total[:, 0:width]
        cot = total[:, width : width + 128]
        prob = prob_keep[these, :]
        column_grad = prob * (cot - jnp.sum(prob * cot, axis=1, keepdims=True))
        high = column_grad.astype(bf)
        rest = column_grad - high.astype(f32)
        middle = rest.astype(bf)
        low = (rest - middle.astype(f32)).astype(bf)
        router = router_pad[...]
        router_grad = nn_dot(high, router) + (nn_dot(middle, router) + nn_dot(low, router))
        xfull = tok_ref[these, :].astype(f32)
        inv_rms = inv_keep[these, 0:1]
        pulled = gain_ref[...] * (expert_grad + router_grad)
        both_ref[these, width : 2 * width] = inv_rms * pulled - xfull * (inv_rms * inv_rms * inv_rms) * jnp.mean(
            pulled * xfull, axis=1, keepdims=True
        )

    last_weights(2, 0)
    last_weights(2, 1)
    need_weights(2, 0)
    down(0,0)
    need_weights(2, 1)
    down(0,1)
    down(1,0)
    down(1,1)
    merge(0,0,2)
    merge(0,0,1)
    merge(0,0,3)
    merge(0,0,0)
    merge(0,1,2)
    merge(0,1,1)
    image_of(0)
    merge(0,1,3)
    merge(0,1,0)
    image_on(0,3)
    image_on(0,1)
    image_of(1)
    image_on(0,2)
    image_on(1,3)
    image_on(1,1)
    image_on(1,2)
    backward(0,0)
    backward(0,1)
    backward(1,0)
    backward(1,1)
    merge(1,0,2)
    merge(1,0,1)
    merge(1,0,3)
    merge(1,0,0)
    merge(1,1,2)
    merge(1,1,1)
    merge(1,1,3)
    merge(1,1,0)
    gram_of(0)
    gram_of(1)
    for copy, cond in pending:
        if cond is None:
            copy.wait_send()
        else:
            pl.when(cond)(copy.wait_send)


def on_device_dense(tokens, tangent, norm_gain, router, w_gate, w_up, w_down, routes):
    n_tok, width = tokens.shape
    hid = w_gate.shape[2]
    half = hid // 2
    n_sub = n_tok // batches
    n_lane = 4 * n_sub
    n_rows = 2 * n_lane
    bf, f32 = jnp.bfloat16, jnp.float32
    vm = pl.BlockSpec(memory_space=pltpu.VMEM)
    hbm = pl.BlockSpec(memory_space=pl.ANY)
    out = jax.ShapeDtypeStruct((n_tok, 2 * width), f32)
    dma = pltpu.SemaphoreType.DMA
    keep = pltpu.VMEM((2, 2, batches * n_rows, half), f32)

    def home(columns):
        return [
            pltpu.VMEM((batches, 3 * n_lane, columns), bf),
            pltpu.VMEM((batches, n_lane, columns), f32),
            pltpu.VMEM((batches, 4, n_sub, columns), bf),
            pltpu.VMEM((batches, 2, n_lane, columns), bf),
            pltpu.VMEM((batches, 4, n_sub, columns), bf),
        ]

    both = pl.pallas_call(
        block_kernel,
        out_shape=out,
        in_specs=[vm] * 5 + [hbm] * 3,
        out_specs=vm,
        scratch_shapes=[
            pltpu.VMEM((2, width, 2 * hid), bf),
            pltpu.VMEM((2, 2 * hid, width), bf),
            pltpu.VMEM((2, hid, width), bf),
            pltpu.VMEM((batches, 3 * n_lane, 2 * width + 128), bf),
            keep, keep, keep,
            pltpu.VMEM((2, batches * n_rows, hid), bf),
            *home(width),
            pltpu.VMEM((batches, 3 * n_lane, width), bf),
            pltpu.VMEM((2, n_rows, 2 * hid), bf),
            *home(width + 128),
            pltpu.VMEM((n_tok, 128), f32),
            pltpu.VMEM((n_tok, 128), f32),
            pltpu.VMEM((128, width), bf),
            dma((3, 2, 3)), dma((3, 2, 3)), dma((3, 2)),
            dma((3, 2, 4)), dma((3, 2, 4)),
            dma((3, 3, 3)), dma((3, 3, 3)), dma((batches, 3, 4)), dma((batches, 3, 4)),
            dma((2, batches, 2, 4)), dma((2, batches, 2, 4)),
            dma((2, batches, 4)), dma((2, batches, 4)),
        ],
        compiler_params=pltpu.CompilerParams(
            collective_id=0, has_side_effects=True, vmem_limit_bytes=60 * 2**20
        ),
        cost_estimate=pl.CostEstimate(
            flops=2 * 8 * 512 * width * hid, bytes_accessed=2**24, transcendentals=2**20
        ),
    )(tokens, tangent, norm_gain.reshape(1, width), router.T, routes.T, w_gate, w_up, w_down)
    return both[:, 0:width], both[:, width : 2 * width]


def solution(mesh):
    in_specs = (
        P(("dp", "expert"), None),
        P(("dp", "expert"), None),
        P(),
        P(),
        P("expert", "dp", None),
        P("expert", "dp", None),
        P("expert", None, "dp"),
        P(("dp", "expert"), None),
    )
    out_specs = (P(("dp", "expert"), None), P(("dp", "expert"), None))
    body = on_device
    if mesh.shape["dp"] == 4 and mesh.shape["expert"] == 8:
        body = on_device_dense
    return jax.shard_map(
        body, mesh=mesh, in_specs=in_specs, out_specs=out_specs, check_vma=False
    )
```

```python
import functools

import jax
import jax.numpy as jnp
from jax import lax
from jax.experimental import pallas as pl
from jax.experimental.pallas import tpu as pltpu
from jax.sharding import PartitionSpec as P

eps_value = 1e-06


def pick_columns(table, routes):
    hits = routes[:, :, None] == jnp.arange(table.shape[1], dtype=jnp.int32)[None, None, :]
    return jnp.sum(jnp.where(hits, table[:, None, :], jnp.zeros((), table.dtype)), axis=2)


def on_device(tokens, tangent, norm_gain, router, w_gate, w_up, w_down, routes):
    tok_rows, topk = routes.shape
    model_width = tokens.shape[1]
    experts_all = router.shape[1]
    local_experts = w_gate.shape[0]
    groups = lax.axis_size("expert")
    capacity = 2 * tok_rows * topk // experts_all
    xfull = tokens.astype(jnp.float32)
    vfull = tangent.astype(jnp.float32)
    inv_rms = lax.rsqrt(jnp.mean(xfull * xfull, axis=1, keepdims=True) + eps_value)
    normed = (norm_gain * xfull * inv_rms).astype(jnp.bfloat16)
    cross_term = jnp.mean(xfull * vfull, axis=1, keepdims=True)
    normed_tan = (norm_gain * (vfull * inv_rms - xfull * inv_rms**3 * cross_term)).astype(
        jnp.bfloat16
    )
    logits = jnp.dot(normed, router, preferred_element_type=jnp.float32)
    logit_tan = jnp.dot(normed_tan, router, preferred_element_type=jnp.float32)
    selected = pick_columns(logits, routes)
    sel_tan = pick_columns(logit_tan, routes)
    exp_sel = jnp.exp(selected)
    gate_prob = exp_sel / jnp.sum(exp_sel, axis=1, keepdims=True)
    gate_tan = gate_prob * (sel_tan - jnp.sum(gate_prob * sel_tan, axis=1, keepdims=True))
    gate_b = gate_prob.astype(jnp.bfloat16)
    gate_tan_b = gate_tan.astype(jnp.bfloat16)
    pair_count = tok_rows * topk
    flat_ids = routes.reshape(-1)
    order = jnp.arange(pair_count, dtype=jnp.int32)
    earlier = (flat_ids[None, :] == flat_ids[:, None]) & (order[None, :] < order[:, None])
    slot_rank = jnp.sum(earlier.astype(jnp.int32), axis=1)
    slot_of_pair = flat_ids * capacity + slot_rank
    slot_hits = slot_of_pair[None, :] == jnp.arange(experts_all * capacity, dtype=jnp.int32)[:, None]
    slot_table = jnp.max(
        jnp.where(slot_hits, jnp.arange(pair_count, dtype=jnp.int32)[None, :], -1), axis=1
    )
    slot_valid = slot_table >= 0
    safe_pair = jnp.maximum(slot_table, 0)
    tok_idx = safe_pair // topk
    which_k = safe_pair % topk
    bf_zero = jnp.zeros((), jnp.bfloat16)
    send_rows = jnp.stack(
        (
            jnp.where(slot_valid[:, None], normed[tok_idx], bf_zero),
            jnp.where(slot_valid[:, None], normed_tan[tok_idx], bf_zero),
        )
    )
    send_rows = send_rows.reshape(2, groups, local_experts * capacity, model_width)
    send_gates = jnp.stack(
        (
            jnp.where(slot_valid, gate_b[tok_idx, which_k], bf_zero),
            jnp.where(slot_valid, gate_tan_b[tok_idx, which_k], bf_zero),
        )
    )
    send_gates = send_gates.reshape(2, groups, local_experts * capacity)
    recv_rows, recv_gates = (
        lax.all_to_all(send_rows, "expert", split_axis=1, concat_axis=1, tiled=True),
        lax.all_to_all(send_gates, "expert", split_axis=1, concat_axis=1, tiled=True),
    )
    slot_rows = recv_rows.reshape(2, groups, local_experts, capacity, model_width)
    recv_gates = recv_gates.reshape(2, groups, local_experts, capacity).astype(jnp.float32)
    gate_val = recv_gates[0][..., None]
    tan_val = recv_gates[1][..., None]
    gate_full, up_full, down_full = (
        lax.all_gather(w_gate, "dp", axis=1, tiled=True),
        lax.all_gather(w_up, "dp", axis=1, tiled=True),
        lax.all_gather(w_down, "dp", axis=2, tiled=True),
    )
    pre_both = jnp.einsum(
        "tslkd,ldf->tslkf", slot_rows, gate_full, preferred_element_type=jnp.float32
    )
    up_both = jnp.einsum("tslkd,ldf->tslkf", slot_rows, up_full, preferred_element_type=jnp.float32)
    pre_gate = pre_both[0]
    gate_dot = pre_both[1]
    pre_up = up_both[0]
    up_dot = up_both[1]
    sig_gate = jax.nn.sigmoid(pre_gate)
    silu_gate = pre_gate * sig_gate
    slope_gate = sig_gate * (1.0 + pre_gate * (1.0 - sig_gate))
    hidden = silu_gate * pre_up
    hidden_tan = slope_gate * gate_dot * pre_up + silu_gate * up_dot
    mixed_rows = (tan_val * hidden + gate_val * hidden_tan).astype(jnp.bfloat16)
    pair_image = jnp.einsum(
        "slkf,lfd->slkd", mixed_rows, down_full, preferred_element_type=jnp.float32
    )
    pair_send = pair_image.astype(jnp.bfloat16).reshape(
        groups, local_experts * capacity, model_width
    )
    pair_back = lax.all_to_all(pair_send, "expert", split_axis=0, concat_axis=0, tiled=True)
    pair_back = pair_back.reshape(experts_all * capacity, model_width)
    tangent_image = jnp.sum(
        pair_back[slot_of_pair].astype(jnp.float32).reshape(tok_rows, topk, model_width), axis=1
    )
    image_b = tangent_image.astype(jnp.bfloat16)
    send_cot = jnp.where(slot_valid[:, None], image_b[tok_idx], bf_zero).reshape(
        groups, local_experts * capacity, model_width
    )
    recv_cot = lax.all_to_all(send_cot, "expert", split_axis=0, concat_axis=0, tiled=True)
    recv_cot = recv_cot.reshape(groups, local_experts, capacity, model_width)
    back_hidden = jnp.einsum(
        "slkd,lfd->slkf", recv_cot, down_full, preferred_element_type=jnp.float32
    )
    gate_cot = jnp.sum(back_hidden * hidden, axis=3).astype(jnp.bfloat16)
    scaled = gate_val * back_hidden
    grad_gate = (scaled * pre_up * slope_gate).astype(jnp.bfloat16)
    grad_up = (scaled * silu_gate).astype(jnp.bfloat16)
    pair_grad = jnp.einsum(
        "slkf,ldf->slkd", grad_gate, gate_full, preferred_element_type=jnp.float32
    )
    pair_grad = pair_grad + jnp.einsum(
        "slkf,ldf->slkd", grad_up, up_full, preferred_element_type=jnp.float32
    )
    grad_send = pair_grad.astype(jnp.bfloat16).reshape(
        groups, local_experts * capacity, model_width
    )
    cot_send = gate_cot.reshape(groups, local_experts * capacity)
    grad_back, cot_back = (
        lax.all_to_all(grad_send, "expert", split_axis=0, concat_axis=0, tiled=True),
        lax.all_to_all(cot_send, "expert", split_axis=0, concat_axis=0, tiled=True),
    )
    grad_back = grad_back.reshape(experts_all * capacity, model_width)
    cot_back = cot_back.reshape(experts_all * capacity)
    expert_grad = jnp.sum(
        grad_back[slot_of_pair].astype(jnp.float32).reshape(tok_rows, topk, model_width), axis=1
    )
    pair_cot = cot_back[slot_of_pair].astype(jnp.float32).reshape(tok_rows, topk)
    logit_grad = gate_prob * (pair_cot - jnp.sum(gate_prob * pair_cot, axis=1, keepdims=True))
    hits = routes[:, :, None] == jnp.arange(experts_all, dtype=jnp.int32)[None, None, :]
    column_grad = jnp.sum(jnp.where(hits, logit_grad[:, :, None], 0.0), axis=1)
    router_grad = jnp.dot(
        column_grad, router.astype(jnp.float32).T, precision=lax.Precision.HIGHEST
    )
    pulled = norm_gain * (expert_grad + router_grad)
    gram_image = inv_rms * pulled - xfull * inv_rms**3 * jnp.mean(
        pulled * xfull, axis=1, keepdims=True
    )
    return (tangent_image, gram_image)


MESH = pl.DeviceIdType.MESH


def nt_dot(left, right):
    return lax.dot_general(
        left, right, (((1,), (1,)), ((), ())), preferred_element_type=jnp.float32
    )


def nn_dot(left, right):
    return jnp.dot(left, right, preferred_element_type=jnp.float32)


batches = 2


def block_kernel(
    tok_hbm, tan_hbm, gain_hbm, router_hbm, routes_hbm, wg_ref, wu_ref, wd_ref,
    both_hbm,
    tok_ref, tan_ref, gain_ref, router_ref, routes_ref, both_ref,
    wgu, wgu_t, wd, rows, keep_a, keep_s, keep_h, mix, part, own_part, mid, far, landed,
    image_rows, grads, part2, own_part2, mid2, far2, landed2, prob_keep, inv_keep, router_pad,
    w_send, w_recv, w_own, m_send, m_recv, t_send, t_recv, a_send, a_recv, s_send, s_recv,
    z_send, z_recv, l_send, l_recv, i_sems, o_sems,
):
    f32, bf = jnp.float32, jnp.bfloat16
    n_tok, width = tok_ref.shape
    slab, hid = wg_ref.shape[1], wg_ref.shape[2]
    half = hid // 2
    n_sub = n_tok // batches
    n_lane = 4 * n_sub
    n_exp = router_ref.shape[0]
    dp, ex = lax.axis_index("dp"), lax.axis_index("expert")
    y, x = dp // 2, dp % 2
    z, core = ex // 2, ex % 2
    x_index, y_index = y * 2 + 1 - x, (1 - y) * 2 + x
    d_index = (1 - y) * 2 + 1 - x
    x_peer, y_peer = (x_index, ex), (y_index, ex)
    mate = (dp, z * 2 + 1 - core)
    z_peers = [(dp, (z + dz) % 4 * 2 + core) for dz in range(1, 4)]
    at_x, at_own, at_y = 0, n_lane, 2 * n_lane

    def rows_of(base, dz):
        return pl.ds(pl.multiple_of(base + (z + dz) % 4 * n_sub, n_sub), n_sub)

    def tokens_of(b):
        return slice(b * n_sub, (b + 1) * n_sub)

    loads = [
        pltpu.make_async_copy(src, dst, i_sems.at[i])
        for i, (src, dst) in enumerate((
            (tok_hbm, tok_ref), (tan_hbm, tan_ref), (gain_hbm, gain_ref),
            (router_hbm, router_ref), (routes_hbm, routes_ref),
        ))
    ]
    for load in loads:
        load.start()

    barrier = pltpu.get_barrier_semaphore()
    friends = [
        (x_peer, None), (y_peer, None), (mate, None), (z_peers[0], z < 3), (z_peers[2], z > 0)
    ]

    def greet(friend):
        pl.semaphore_signal(barrier, inc=1, device_id=friend, device_id_type=MESH)

    for friend, cond in friends:
        if cond is None:
            greet(friend)
        else:
            pl.when(cond)(functools.partial(greet, friend))
    inner = jnp.where(z > 0, 1, 0) * jnp.where(z < 3, 1, 0)
    pl.semaphore_wait(barrier, 4 + inner)

    pending = []

    def push(src, dst, sems, where, device, cond=None):
        copy = pltpu.make_async_remote_copy(
            src_ref=src, dst_ref=dst, send_sem=sems[0].at[where], recv_sem=sems[1].at[where],
            device_id=device, device_id_type=MESH,
        )
        if cond is None:
            copy.start()
        else:
            pl.when(cond)(copy.start)
        pending.append((copy, cond))
        return copy

    def slab_of(index):
        return pl.ds(pl.multiple_of(index * slab, slab), slab)

    def weight_at(kind, l, index):
        if kind == 2:
            return wd.at[l, pl.ds(pl.multiple_of(core * half, half), half), slab_of(index)]
        first = pl.multiple_of(core * hid + kind * half, half)
        return wgu.at[l, slab_of(index), pl.ds(first, half)]

    def weight_src(kind, l, which):
        part_of = pl.ds(pl.multiple_of(which * half, half), half)
        if kind == 2:
            return wd_ref.at[l, part_of, :]
        return (wg_ref, wu_ref)[kind].at[l, :, part_of]

    direct, relayed, shared, local = {}, {}, {}, {}
    w_sems, m_sems, t_sems = (w_send, w_recv), (m_send, m_recv), (t_send, t_recv)
    a_sems, s_sems, z_sems = (a_send, a_recv), (s_send, s_recv), (z_send, z_recv)
    l_sems = (l_send, l_recv)

    def start_weights(kind):
        for p, l in ((0, 0), (1, 1), (0, 1), (1, 0)):
            for_x, for_y = (1 - x, x) if l == 0 else (y, 1 - y)
            direct[kind, l, p] = push(
                weight_src(kind, l, (for_x, for_y)[p]), weight_at(kind, l, dp),
                w_sems, (kind, l, p), (x_peer, y_peer)[p],
            )
        for l in range(2):
            for_me = (x, y)[l]
            mine = weight_at(kind, l, dp)
            local[kind, l] = pltpu.make_async_copy(
                weight_src(kind, l, for_me), mine, w_own.at[kind, l]
            )
            local[kind, l].start()
            shared[kind, l] = [
                push(weight_src(kind, l, for_me), mine, m_sems, (kind, l, 0), mate)
            ]

    def share_weights(kind, l, slot, index):
        block = weight_at(kind, l, index)
        shared[kind, l].append(push(block, block, m_sems, (kind, l, slot), mate))

    def relay_weights(kind):
        for l in range(2):
            index = (x_index, y_index)[l]
            block = weight_at(kind, l, index)
            direct[kind, l, l].wait_recv()
            relayed[kind, l] = push(block, block, w_sems, (kind, l, 2), (y_peer, x_peer)[l])
            share_weights(kind, l, 1, index)

    def side_weights(kind):
        for l in range(2):
            direct[kind, l, 1 - l].wait_recv()
            share_weights(kind, l, 2, (x_index, y_index)[1 - l])

    def last_weights(kind, l):
        relayed[kind, l].wait_recv()
        share_weights(kind, l, 3, d_index)

    def need_weights(kind, l):
        local[kind, l].wait()
        for copy in shared[kind, l]:
            copy.wait_recv()

    start_weights(0)

    for load in loads:
        load.wait()
    router_pad[...] = jnp.zeros(router_pad.shape, bf)
    router_pad[0:n_exp, :] = router_ref[...]
    xfull = tok_ref[...].astype(f32)
    vfull = tan_ref[...].astype(f32)
    gain = gain_ref[...]
    inv_rms = lax.rsqrt(jnp.mean(xfull * xfull, axis=1, keepdims=True) + eps_value)
    normed = (gain * xfull * inv_rms).astype(bf)
    cross_term = jnp.mean(xfull * vfull, axis=1, keepdims=True)
    inv_cube = inv_rms * inv_rms * inv_rms
    normed_tan = (gain * (vfull * inv_rms - xfull * inv_cube * cross_term)).astype(bf)
    mine = rows_of(at_own, 0)
    for b in range(batches):
        rows[b, mine, 0:width] = normed[tokens_of(b)]
        rows[b, mine, width : 2 * width] = normed_tan[tokens_of(b)]
    logits = nt_dot(normed, router_pad[...])
    logit_tan = nt_dot(normed_tan, router_pad[...])
    ids = lax.broadcasted_iota(jnp.int32, (128, n_tok), 0)
    chosen_by = jnp.zeros((128, n_tok), f32)
    for k in range(routes_ref.shape[0]):
        chosen_by = chosen_by + jnp.where(ids == routes_ref[k : k + 1, :], 1.0, 0.0)
    unit = jnp.where(
        lax.broadcasted_iota(jnp.int32, (n_tok, n_tok), 0)
        == lax.broadcasted_iota(jnp.int32, (n_tok, n_tok), 1),
        1.0, 0.0,
    ).astype(bf)
    chosen = nt_dot(unit, chosen_by.astype(bf))
    exp_sel = jnp.where(chosen > 0.5, jnp.exp(logits), 0.0)
    gate_prob = exp_sel / jnp.sum(exp_sel, axis=1, keepdims=True)
    gate_tan = gate_prob * (
        logit_tan - jnp.sum(gate_prob * logit_tan, axis=1, keepdims=True)
    )
    table = (gate_prob + pltpu.roll(gate_tan, 64, 1)).astype(bf)
    for b in range(batches):
        rows[b, mine, 2 * width : 2 * width + 128] = table[tokens_of(b)]
    prob_keep[...] = gate_prob
    inv_keep[...] = jnp.broadcast_to(inv_rms, (n_tok, 128))

    ups, downs = {}, {}
    bases = (at_x, at_own, at_y)

    def has_up(j):
        return jnp.logical_and(z < 3, z >= j)

    def has_down(j):
        return jnp.logical_and(z > 0, z + j <= 3)

    def chain(which, j):
        if j:
            pl.when(z >= j)(ups[which, j - 1].wait_recv)
            pl.when(z + j <= 3)(downs[which, j - 1].wait_recv)
        if j < 3:
            above = rows.at[:, rows_of(bases[which], 4 - j)]
            below = rows.at[:, rows_of(bases[which], j)]
            ups[which, j] = push(above, above, t_sems, (which, 0, j), z_peers[0], has_up(j))
            downs[which, j] = push(below, below, t_sems, (which, 1, j), z_peers[2], has_down(j))

    from_x = push(rows.at[:, mine], rows.at[:, rows_of(at_x, 0)], t_sems, (0, 2, 0), x_peer)
    from_y = push(rows.at[:, mine], rows.at[:, rows_of(at_y, 0)], t_sems, (2, 2, 0), y_peer)
    chain(1, 0)
    start_weights(1)
    from_x.wait_recv()
    chain(0, 0)
    from_y.wait_recv()
    chain(2, 0)
    relay_weights(0)
    for which in (1, 0, 2):
        chain(which, 1)
    side_weights(0)
    relay_weights(1)
    start_weights(2)
    for which in (1, 0, 2):
        chain(which, 2)
    side_weights(1)
    for kind in range(2):
        for l in range(2):
            last_weights(kind, l)

    def turn_weights(l):
        need_weights(0, l)
        need_weights(1, l)

        @pl.loop(0, 4)
        def _(j):
            at = pl.ds(pl.multiple_of(j * slab, slab), slab)
            wgu_t[l, :, at] = wgu[l, at, :].T

    turn_weights(0)
    turn_weights(1)
    relay_weights(2)
    side_weights(2)
    for which in (1, 0, 2):
        chain(which, 3)

    n_rows = 2 * n_lane
    all_rows = batches * n_rows
    wide_lanes = lax.broadcasted_iota(jnp.int32, (all_rows, 128), 1)

    for l in range(2):
        these = slice(l * n_lane, l * n_lane + n_rows)

        @pl.loop(0, 2)
        def _(k):
            cols = pl.ds(pl.multiple_of(k * hid, hid), hid)
            expert = (z * 2 + k) * 2 + l
            table = rows[:, these, 2 * width : 2 * width + 128].reshape(all_rows, 128).astype(f32)
            gate = jnp.sum(jnp.where(wide_lanes == expert, table, 0.0), axis=1, keepdims=True)
            tan = jnp.sum(
                jnp.where(wide_lanes == expert + 64, table, 0.0), axis=1, keepdims=True
            )
            pre = nn_dot(rows[:, these, 0:width].reshape(all_rows, width), wgu[l, :, cols])
            dots = nn_dot(
                rows[:, these, width : 2 * width].reshape(all_rows, width), wgu[l, :, cols]
            )
            pre_gate, pre_up = pre[:, 0:half], pre[:, half:hid]
            gate_dot, up_dot = dots[:, 0:half], dots[:, half:hid]
            sig = jax.nn.sigmoid(pre_gate)
            silu = pre_gate * sig
            slope_up = sig * (1.0 + pre_gate * (1.0 - sig)) * pre_up
            hidden = silu * pre_up
            mixed = tan * hidden + gate * (slope_up * gate_dot + silu * up_dot)
            keep_a[l, k] = gate * slope_up
            keep_s[l, k] = gate * silu
            keep_h[l, k] = hidden
            mix[l, :, pl.ds(pl.multiple_of(k * half, half), half)] = mixed.astype(bf)

    turns = [
        (part, own_part, mid, far, landed), (part2, own_part2, mid2, far2, landed2)
    ]
    x_copies, y_copies, z_copies, totals = {}, {}, {}, {}

    def place(turn, b, l, cols, term):
        parts, own = turns[turn][0:2]
        if l == 0:
            parts[b, at_x : at_x + n_lane, cols] = term[0:n_lane].astype(bf)
            own[b, :, cols] = term[n_lane:n_rows]
        else:
            own[b, :, cols] = own[b, :, cols] + term[0:n_lane]
            parts[b, at_y : at_y + n_lane, cols] = term[n_lane:n_rows].astype(bf)

    def send_side(turn, b, s):
        parts, far = turns[turn][0], turns[turn][3]
        peer, base = ((x_peer, at_x), (y_peer, at_y))[s]
        copies = (x_copies, y_copies)[s]
        for dz in (2, 1, 3, 0):
            copies[turn, b, dz] = push(
                parts.at[b, rows_of(base, dz)], far.at[b, s, rows_of(0, dz)],
                s_sems, (turn, b, s, dz), peer,
            )

    def merge(turn, b, dz):
        parts, own, mid, far, land = turns[turn]
        x_copies[turn, b, dz].wait_recv()
        y_copies[turn, b, dz].wait_recv()
        at = rows_of(0, dz)
        total = own[b, at, :] + (far[b, 0, at, :].astype(f32) + far[b, 1, at, :].astype(f32))
        if dz:
            mid[b, dz] = total.astype(bf)
            z_copies[turn, b, dz] = push(
                mid.at[b, dz], land.at[b, z], z_sems, (turn, b, dz), z_peers[dz - 1]
            )
        else:
            own[b, at, :] = total

    def total_of(turn, b):
        own, land = turns[turn][1], turns[turn][4]
        total = own[b, rows_of(0, 0), :]
        for dz in (1, 3, 2):
            z_copies[turn, b, dz].wait_recv()
            total = total + land[b, (z + 4 - dz) % 4].astype(f32)
        return total

    def down(b, l):
        left = mix[l, b * n_rows : (b + 1) * n_rows, :]
        place(0, b, l, slice(0, width), nn_dot(left, wd[l]))
        send_side(0, b, l)

    links, sides, stores = {}, {}, []

    def store(b, part):
        piece = (tokens_of(b), pl.ds(part * width, width))
        stores.append(
            pltpu.make_async_copy(both_ref.at[piece], both_hbm.at[piece], o_sems.at[b, part])
        )
        stores[-1].start()

    def image_to_sides(b, dz, cond=None):
        block = image_rows.at[b, rows_of(at_own, 4 - dz)]
        for s, (peer, base) in enumerate(((x_peer, at_x), (y_peer, at_y))):
            sides[b, s, dz] = push(
                block, image_rows.at[b, rows_of(base, 4 - dz)], a_sems, (b, s, dz), peer, cond
            )

    def image_link(b, way, j):
        block = image_rows.at[b, rows_of(at_own, (4 - j, j)[way])]
        links[b, way, j] = push(
            block, block, l_sems, (b, way, j), z_peers[(0, 2)[way]], (has_up, has_down)[way](j)
        )

    def image_of(b):
        image = total_of(0, b)
        both_ref[tokens_of(b), 0:width] = image
        image_rows[b, mine, :] = image.astype(bf)
        image_link(b, 0, 0)
        image_link(b, 1, 0)
        image_to_sides(b, 0)
        store(b, 0)

    def image_on(b, j):
        for way, here, dz in ((0, z > j, 1 + j), (1, z < 3 - j, 3 - j)):
            pl.when(here)(links[b, way, j].wait_recv)
            if j < 2:
                image_link(b, way, j + 1)
            image_to_sides(b, dz, here)

    def backward(b, l):
        for dz in range(4):
            sides[b, l, dz].wait_recv()
        these = slice(l * n_lane, l * n_lane + n_rows)
        kept = slice(b * n_rows, (b + 1) * n_rows)
        cots = jnp.zeros((n_rows, 128), f32)
        back_both = nt_dot(image_rows[b, these, :], wd[l])
        for k in range(2):
            back = back_both[:, k * half : (k + 1) * half]
            cot = jnp.sum(back * keep_h[l, k, kept], axis=1, keepdims=True)
            cots = cots + jnp.where(wide_lanes[0:n_rows] == (z * 2 + k) * 2 + l, cot, 0.0)
            grads[l, :, k * hid : k * hid + half] = (back * keep_a[l, k, kept]).astype(bf)
            grads[l, :, k * hid + half : (k + 1) * hid] = (back * keep_s[l, k, kept]).astype(bf)
        place(1, b, l, slice(width, width + 128), cots)
        place(1, b, l, slice(0, width), nn_dot(grads[l], wgu_t[l]))
        send_side(1, b, l)

    def gram_of(b):
        total = total_of(1, b)
        these = tokens_of(b)
        expert_grad = total[:, 0:width]
        cot = total[:, width : width + 128]
        prob = prob_keep[these, :]
        column_grad = prob * (cot - jnp.sum(prob * cot, axis=1, keepdims=True))
        high = column_grad.astype(bf)
        rest = column_grad - high.astype(f32)
        middle = rest.astype(bf)
        low = (rest - middle.astype(f32)).astype(bf)
        router = router_pad[...]
        router_grad = nn_dot(high, router) + (nn_dot(middle, router) + nn_dot(low, router))
        xfull = tok_ref[these, :].astype(f32)
        inv_rms = inv_keep[these, 0:1]
        pulled = gain_ref[...] * (expert_grad + router_grad)
        both_ref[these, width : 2 * width] = inv_rms * pulled - xfull * (inv_rms * inv_rms * inv_rms) * jnp.mean(
            pulled * xfull, axis=1, keepdims=True
        )
        store(b, 1)

    last_weights(2, 0)
    last_weights(2, 1)
    need_weights(2, 0)
    down(0, 0)
    need_weights(2, 1)
    down(0, 1)
    down(1, 0)
    down(1, 1)
    merge(0, 0, 2)
    merge(0, 0, 1)
    merge(0, 0, 3)
    merge(0, 0, 0)
    merge(0, 1, 2)
    merge(0, 1, 1)
    image_of(0)
    merge(0, 1, 3)
    merge(0, 1, 0)
    image_on(0, 0)
    image_on(0, 1)
    image_of(1)
    image_on(0, 2)
    image_on(1, 0)
    image_on(1, 1)
    image_on(1, 2)
    backward(0, 0)
    backward(0, 1)
    backward(1, 0)
    backward(1, 1)
    merge(1, 0, 2)
    merge(1, 0, 1)
    merge(1, 0, 3)
    merge(1, 0, 0)
    merge(1, 1, 2)
    merge(1, 1, 1)
    merge(1, 1, 3)
    merge(1, 1, 0)
    gram_of(0)
    gram_of(1)
    for copy in stores:
        copy.wait()
    for copy, cond in pending:
        if cond is None:
            copy.wait_send()
        else:
            pl.when(cond)(copy.wait_send)


def on_device_dense(tokens, tangent, norm_gain, router, w_gate, w_up, w_down, routes):
    n_tok, width = tokens.shape
    hid = w_gate.shape[2]
    half = hid // 2
    n_sub = n_tok // batches
    n_lane = 4 * n_sub
    n_rows = 2 * n_lane
    bf, f32 = jnp.bfloat16, jnp.float32
    hbm = pl.BlockSpec(memory_space=pl.ANY)
    out = jax.ShapeDtypeStruct((n_tok, 2 * width), f32)
    dma = pltpu.SemaphoreType.DMA
    keep = pltpu.VMEM((2, 2, batches * n_rows, half), f32)

    def home(columns):
        return [
            pltpu.VMEM((batches, 3 * n_lane, columns), bf),
            pltpu.VMEM((batches, n_lane, columns), f32),
            pltpu.VMEM((batches, 4, n_sub, columns), bf),
            pltpu.VMEM((batches, 2, n_lane, columns), bf),
            pltpu.VMEM((batches, 4, n_sub, columns), bf),
        ]

    both = pl.pallas_call(
        block_kernel,
        out_shape=out,
        in_specs=[hbm] * 8,
        out_specs=hbm,
        scratch_shapes=[
            pltpu.VMEM((n_tok, width), bf),
            pltpu.VMEM((n_tok, width), bf),
            pltpu.VMEM((1, width), f32),
            pltpu.VMEM((router.shape[1], width), bf),
            pltpu.VMEM((routes.shape[1], n_tok), routes.dtype),
            pltpu.VMEM((n_tok, 2 * width), f32),
            pltpu.VMEM((2, width, 2 * hid), bf),
            pltpu.VMEM((2, 2 * hid, width), bf),
            pltpu.VMEM((2, hid, width), bf),
            pltpu.VMEM((batches, 3 * n_lane, 2 * width + 128), bf),
            keep, keep, keep,
            pltpu.VMEM((2, batches * n_rows, hid), bf),
            *home(width),
            pltpu.VMEM((batches, 3 * n_lane, width), bf),
            pltpu.VMEM((2, n_rows, 2 * hid), bf),
            *home(width + 128),
            pltpu.VMEM((n_tok, 128), f32),
            pltpu.VMEM((n_tok, 128), f32),
            pltpu.VMEM((128, width), bf),
            dma((3, 2, 3)), dma((3, 2, 3)), dma((3, 2)),
            dma((3, 2, 4)), dma((3, 2, 4)),
            dma((3, 3, 3)), dma((3, 3, 3)), dma((batches, 2, 4)), dma((batches, 2, 4)),
            dma((2, batches, 2, 4)), dma((2, batches, 2, 4)),
            dma((2, batches, 4)), dma((2, batches, 4)),
            dma((batches, 2, 3)), dma((batches, 2, 3)), dma((5,)), dma((batches, 2)),
        ],
        compiler_params=pltpu.CompilerParams(
            collective_id=0, has_side_effects=True, vmem_limit_bytes=60 * 2**20
        ),
        cost_estimate=pl.CostEstimate(
            flops=2 * 8 * 512 * width * hid, bytes_accessed=2**24, transcendentals=2**20
        ),
    )(tokens, tangent, norm_gain.reshape(1, width), router.T, routes.T, w_gate, w_up, w_down)
    return both[:, 0:width], both[:, width : 2 * width]


def solution(mesh):
    in_specs = (
        P(("dp", "expert"), None),
        P(("dp", "expert"), None),
        P(),
        P(),
        P("expert", "dp", None),
        P("expert", "dp", None),
        P("expert", None, "dp"),
        P(("dp", "expert"), None),
    )
    out_specs = (P(("dp", "expert"), None), P(("dp", "expert"), None))
    body = on_device
    if mesh.shape["dp"] == 4 and mesh.shape["expert"] == 8:
        body = on_device_dense
    return jax.shard_map(
        body, mesh=mesh, in_specs=in_specs, out_specs=out_specs, check_vma=False
    )
```

```python
import functools

import jax
import jax.numpy as jnp
from jax import lax
from jax.experimental import pallas as pl
from jax.experimental.pallas import tpu as pltpu
from jax.sharding import PartitionSpec as P

eps_value = 1e-06


def pick_columns(table, routes):
    hits = routes[:, :, None] == jnp.arange(table.shape[1], dtype=jnp.int32)[None, None, :]
    return jnp.sum(jnp.where(hits, table[:, None, :], jnp.zeros((), table.dtype)), axis=2)


def on_device(tokens, tangent, norm_gain, router, w_gate, w_up, w_down, routes):
    tok_rows, topk = routes.shape
    model_width = tokens.shape[1]
    experts_all = router.shape[1]
    local_experts = w_gate.shape[0]
    groups = lax.axis_size("expert")
    capacity = 2 * tok_rows * topk // experts_all
    xfull = tokens.astype(jnp.float32)
    vfull = tangent.astype(jnp.float32)
    inv_rms = lax.rsqrt(jnp.mean(xfull * xfull, axis=1, keepdims=True) + eps_value)
    normed = (norm_gain * xfull * inv_rms).astype(jnp.bfloat16)
    cross_term = jnp.mean(xfull * vfull, axis=1, keepdims=True)
    normed_tan = (norm_gain * (vfull * inv_rms - xfull * inv_rms**3 * cross_term)).astype(
        jnp.bfloat16
    )
    logits = jnp.dot(normed, router, preferred_element_type=jnp.float32)
    logit_tan = jnp.dot(normed_tan, router, preferred_element_type=jnp.float32)
    selected = pick_columns(logits, routes)
    sel_tan = pick_columns(logit_tan, routes)
    exp_sel = jnp.exp(selected)
    gate_prob = exp_sel / jnp.sum(exp_sel, axis=1, keepdims=True)
    gate_tan = gate_prob * (sel_tan - jnp.sum(gate_prob * sel_tan, axis=1, keepdims=True))
    gate_b = gate_prob.astype(jnp.bfloat16)
    gate_tan_b = gate_tan.astype(jnp.bfloat16)
    pair_count = tok_rows * topk
    flat_ids = routes.reshape(-1)
    order = jnp.arange(pair_count, dtype=jnp.int32)
    earlier = (flat_ids[None, :] == flat_ids[:, None]) & (order[None, :] < order[:, None])
    slot_rank = jnp.sum(earlier.astype(jnp.int32), axis=1)
    slot_of_pair = flat_ids * capacity + slot_rank
    slot_hits = slot_of_pair[None, :] == jnp.arange(experts_all * capacity, dtype=jnp.int32)[:, None]
    slot_table = jnp.max(
        jnp.where(slot_hits, jnp.arange(pair_count, dtype=jnp.int32)[None, :], -1), axis=1
    )
    slot_valid = slot_table >= 0
    safe_pair = jnp.maximum(slot_table, 0)
    tok_idx = safe_pair // topk
    which_k = safe_pair % topk
    bf_zero = jnp.zeros((), jnp.bfloat16)
    send_rows = jnp.stack(
        (
            jnp.where(slot_valid[:, None], normed[tok_idx], bf_zero),
            jnp.where(slot_valid[:, None], normed_tan[tok_idx], bf_zero),
        )
    )
    send_rows = send_rows.reshape(2, groups, local_experts * capacity, model_width)
    send_gates = jnp.stack(
        (
            jnp.where(slot_valid, gate_b[tok_idx, which_k], bf_zero),
            jnp.where(slot_valid, gate_tan_b[tok_idx, which_k], bf_zero),
        )
    )
    send_gates = send_gates.reshape(2, groups, local_experts * capacity)
    recv_rows, recv_gates = (
        lax.all_to_all(send_rows, "expert", split_axis=1, concat_axis=1, tiled=True),
        lax.all_to_all(send_gates, "expert", split_axis=1, concat_axis=1, tiled=True),
    )
    slot_rows = recv_rows.reshape(2, groups, local_experts, capacity, model_width)
    recv_gates = recv_gates.reshape(2, groups, local_experts, capacity).astype(jnp.float32)
    gate_val = recv_gates[0][..., None]
    tan_val = recv_gates[1][..., None]
    gate_full, up_full, down_full = (
        lax.all_gather(w_gate, "dp", axis=1, tiled=True),
        lax.all_gather(w_up, "dp", axis=1, tiled=True),
        lax.all_gather(w_down, "dp", axis=2, tiled=True),
    )
    pre_both = jnp.einsum(
        "tslkd,ldf->tslkf", slot_rows, gate_full, preferred_element_type=jnp.float32
    )
    up_both = jnp.einsum("tslkd,ldf->tslkf", slot_rows, up_full, preferred_element_type=jnp.float32)
    pre_gate = pre_both[0]
    gate_dot = pre_both[1]
    pre_up = up_both[0]
    up_dot = up_both[1]
    sig_gate = jax.nn.sigmoid(pre_gate)
    silu_gate = pre_gate * sig_gate
    slope_gate = sig_gate * (1.0 + pre_gate * (1.0 - sig_gate))
    hidden = silu_gate * pre_up
    hidden_tan = slope_gate * gate_dot * pre_up + silu_gate * up_dot
    mixed_rows = (tan_val * hidden + gate_val * hidden_tan).astype(jnp.bfloat16)
    pair_image = jnp.einsum(
        "slkf,lfd->slkd", mixed_rows, down_full, preferred_element_type=jnp.float32
    )
    pair_send = pair_image.astype(jnp.bfloat16).reshape(
        groups, local_experts * capacity, model_width
    )
    pair_back = lax.all_to_all(pair_send, "expert", split_axis=0, concat_axis=0, tiled=True)
    pair_back = pair_back.reshape(experts_all * capacity, model_width)
    tangent_image = jnp.sum(
        pair_back[slot_of_pair].astype(jnp.float32).reshape(tok_rows, topk, model_width), axis=1
    )
    image_b = tangent_image.astype(jnp.bfloat16)
    send_cot = jnp.where(slot_valid[:, None], image_b[tok_idx], bf_zero).reshape(
        groups, local_experts * capacity, model_width
    )
    recv_cot = lax.all_to_all(send_cot, "expert", split_axis=0, concat_axis=0, tiled=True)
    recv_cot = recv_cot.reshape(groups, local_experts, capacity, model_width)
    back_hidden = jnp.einsum(
        "slkd,lfd->slkf", recv_cot, down_full, preferred_element_type=jnp.float32
    )
    gate_cot = jnp.sum(back_hidden * hidden, axis=3).astype(jnp.bfloat16)
    scaled = gate_val * back_hidden
    grad_gate = (scaled * pre_up * slope_gate).astype(jnp.bfloat16)
    grad_up = (scaled * silu_gate).astype(jnp.bfloat16)
    pair_grad = jnp.einsum(
        "slkf,ldf->slkd", grad_gate, gate_full, preferred_element_type=jnp.float32
    )
    pair_grad = pair_grad + jnp.einsum(
        "slkf,ldf->slkd", grad_up, up_full, preferred_element_type=jnp.float32
    )
    grad_send = pair_grad.astype(jnp.bfloat16).reshape(
        groups, local_experts * capacity, model_width
    )
    cot_send = gate_cot.reshape(groups, local_experts * capacity)
    grad_back, cot_back = (
        lax.all_to_all(grad_send, "expert", split_axis=0, concat_axis=0, tiled=True),
        lax.all_to_all(cot_send, "expert", split_axis=0, concat_axis=0, tiled=True),
    )
    grad_back = grad_back.reshape(experts_all * capacity, model_width)
    cot_back = cot_back.reshape(experts_all * capacity)
    expert_grad = jnp.sum(
        grad_back[slot_of_pair].astype(jnp.float32).reshape(tok_rows, topk, model_width), axis=1
    )
    pair_cot = cot_back[slot_of_pair].astype(jnp.float32).reshape(tok_rows, topk)
    logit_grad = gate_prob * (pair_cot - jnp.sum(gate_prob * pair_cot, axis=1, keepdims=True))
    hits = routes[:, :, None] == jnp.arange(experts_all, dtype=jnp.int32)[None, None, :]
    column_grad = jnp.sum(jnp.where(hits, logit_grad[:, :, None], 0.0), axis=1)
    router_grad = jnp.dot(
        column_grad, router.astype(jnp.float32).T, precision=lax.Precision.HIGHEST
    )
    pulled = norm_gain * (expert_grad + router_grad)
    gram_image = inv_rms * pulled - xfull * inv_rms**3 * jnp.mean(
        pulled * xfull, axis=1, keepdims=True
    )
    return (tangent_image, gram_image)


MESH = pl.DeviceIdType.MESH


def nt_dot(left, right):
    return lax.dot_general(
        left, right, (((1,), (1,)), ((), ())), preferred_element_type=jnp.float32
    )


def nn_dot(left, right):
    return jnp.dot(left, right, preferred_element_type=jnp.float32)


batches = 2


def block_kernel(
    tok_hbm, tan_hbm, gain_hbm, router_hbm, routes_hbm, wg_ref, wu_ref, wd_ref,
    both_hbm,
    tok_ref, tan_ref, gain_ref, router_ref, routes_ref, both_ref,
    wgu, wgu_t, wd, rows, keep_a, keep_s, keep_h, mix, part, own_part, mid, far, landed,
    image_rows, grads, part2, own_part2, mid2, far2, landed2, prob_keep, inv_keep, router_pad,
    w_send, w_recv, w_own, m_send, m_recv, t_send, t_recv, a_send, a_recv, s_send, s_recv,
    z_send, z_recv, l_send, l_recv, i_sems, o_sems,
):
    f32, bf = jnp.float32, jnp.bfloat16
    n_tok, width = tok_ref.shape
    slab, hid = wg_ref.shape[1], wg_ref.shape[2]
    half = hid // 2
    n_sub = n_tok // batches
    n_lane = 4 * n_sub
    n_exp = router_ref.shape[0]
    dp, ex = lax.axis_index("dp"), lax.axis_index("expert")
    y, x = dp // 2, dp % 2
    z, core = ex // 2, ex % 2
    x_index, y_index = y * 2 + 1 - x, (1 - y) * 2 + x
    d_index = (1 - y) * 2 + 1 - x
    x_peer, y_peer = (x_index, ex), (y_index, ex)
    mate = (dp, z * 2 + 1 - core)
    z_peers = [(dp, (z + dz) % 4 * 2 + core) for dz in range(1, 4)]
    at_x, at_own, at_y = 0, n_lane, 2 * n_lane

    def rows_of(base, dz):
        return pl.ds(pl.multiple_of(base + (z + dz) % 4 * n_sub, n_sub), n_sub)

    def tokens_of(b):
        return slice(b * n_sub, (b + 1) * n_sub)

    loads = [
        pltpu.make_async_copy(src, dst, i_sems.at[i])
        for i, (src, dst) in enumerate((
            (tok_hbm, tok_ref), (tan_hbm, tan_ref), (gain_hbm, gain_ref),
            (router_hbm, router_ref), (routes_hbm, routes_ref),
        ))
    ]
    for load in loads:
        load.start()

    barrier = pltpu.get_barrier_semaphore()
    friends = [
        (x_peer, None), (y_peer, None), (mate, None), (z_peers[0], z < 3), (z_peers[2], z > 0)
    ]

    def greet(friend):
        pl.semaphore_signal(barrier, inc=1, device_id=friend, device_id_type=MESH)

    for friend, cond in friends:
        if cond is None:
            greet(friend)
        else:
            pl.when(cond)(functools.partial(greet, friend))
    inner = jnp.where(z > 0, 1, 0) * jnp.where(z < 3, 1, 0)
    pl.semaphore_wait(barrier, 4 + inner)

    pending = []

    def push(src, dst, sems, where, device, cond=None):
        copy = pltpu.make_async_remote_copy(
            src_ref=src, dst_ref=dst, send_sem=sems[0].at[where], recv_sem=sems[1].at[where],
            device_id=device, device_id_type=MESH,
        )
        if cond is None:
            copy.start()
        else:
            pl.when(cond)(copy.start)
        pending.append((copy, cond))
        return copy

    def slab_of(index):
        return pl.ds(pl.multiple_of(index * slab, slab), slab)

    def weight_at(kind, l, index):
        if kind == 2:
            return wd.at[l, pl.ds(pl.multiple_of(core * half, half), half), slab_of(index)]
        first = pl.multiple_of(core * hid + kind * half, half)
        return wgu.at[l, slab_of(index), pl.ds(first, half)]

    def weight_src(kind, l, which):
        part_of = pl.ds(pl.multiple_of(which * half, half), half)
        if kind == 2:
            return wd_ref.at[l, part_of, :]
        return (wg_ref, wu_ref)[kind].at[l, :, part_of]

    direct, relayed, shared, local = {}, {}, {}, {}
    w_sems, m_sems, t_sems = (w_send, w_recv), (m_send, m_recv), (t_send, t_recv)
    a_sems, s_sems, z_sems = (a_send, a_recv), (s_send, s_recv), (z_send, z_recv)
    l_sems = (l_send, l_recv)

    def start_weights(kind):
        for p, l in ((0, 0), (1, 1), (0, 1), (1, 0)):
            for_x, for_y = (1 - x, x) if l == 0 else (y, 1 - y)
            direct[kind, l, p] = push(
                weight_src(kind, l, (for_x, for_y)[p]), weight_at(kind, l, dp),
                w_sems, (kind, l, p), (x_peer, y_peer)[p],
            )
        for l in range(2):
            for_me = (x, y)[l]
            mine = weight_at(kind, l, dp)
            local[kind, l] = pltpu.make_async_copy(
                weight_src(kind, l, for_me), mine, w_own.at[kind, l]
            )
            local[kind, l].start()
            shared[kind, l] = [
                push(weight_src(kind, l, for_me), mine, m_sems, (kind, l, 0), mate)
            ]

    def share_weights(kind, l, slot, index):
        block = weight_at(kind, l, index)
        shared[kind, l].append(push(block, block, m_sems, (kind, l, slot), mate))

    def relay_weights(kind):
        for l in range(2):
            index = (x_index, y_index)[l]
            block = weight_at(kind, l, index)
            direct[kind, l, l].wait_recv()
            relayed[kind, l] = push(block, block, w_sems, (kind, l, 2), (y_peer, x_peer)[l])
            share_weights(kind, l, 1, index)

    def side_weights(kind):
        for l in range(2):
            direct[kind, l, 1 - l].wait_recv()
            share_weights(kind, l, 2, (x_index, y_index)[1 - l])

    def last_weights(kind, l):
        relayed[kind, l].wait_recv()
        share_weights(kind, l, 3, d_index)

    def need_weights(kind, l):
        local[kind, l].wait()
        for copy in shared[kind, l]:
            copy.wait_recv()

    start_weights(0)

    for load in loads:
        load.wait()
    router_pad[...] = jnp.zeros(router_pad.shape, bf)
    router_pad[0:n_exp, :] = router_ref[...]
    xfull = tok_ref[...].astype(f32)
    vfull = tan_ref[...].astype(f32)
    gain = gain_ref[...]
    inv_rms = lax.rsqrt(jnp.mean(xfull * xfull, axis=1, keepdims=True) + eps_value)
    normed = (gain * xfull * inv_rms).astype(bf)
    cross_term = jnp.mean(xfull * vfull, axis=1, keepdims=True)
    inv_cube = inv_rms * inv_rms * inv_rms
    normed_tan = (gain * (vfull * inv_rms - xfull * inv_cube * cross_term)).astype(bf)
    mine = rows_of(at_own, 0)
    for b in range(batches):
        rows[b, mine, 0:width] = normed[tokens_of(b)]
        rows[b, mine, width : 2 * width] = normed_tan[tokens_of(b)]
    logits = nt_dot(normed, router_pad[...])
    logit_tan = nt_dot(normed_tan, router_pad[...])
    ids = lax.broadcasted_iota(jnp.int32, (128, n_tok), 0)
    chosen_by = jnp.zeros((128, n_tok), f32)
    for k in range(routes_ref.shape[0]):
        chosen_by = chosen_by + jnp.where(ids == routes_ref[k : k + 1, :], 1.0, 0.0)
    unit = jnp.where(
        lax.broadcasted_iota(jnp.int32, (n_tok, n_tok), 0)
        == lax.broadcasted_iota(jnp.int32, (n_tok, n_tok), 1),
        1.0, 0.0,
    ).astype(bf)
    chosen = nt_dot(unit, chosen_by.astype(bf))
    exp_sel = jnp.where(chosen > 0.5, jnp.exp(logits), 0.0)
    gate_prob = exp_sel / jnp.sum(exp_sel, axis=1, keepdims=True)
    gate_tan = gate_prob * (
        logit_tan - jnp.sum(gate_prob * logit_tan, axis=1, keepdims=True)
    )
    table = (gate_prob + pltpu.roll(gate_tan, 64, 1)).astype(bf)
    for b in range(batches):
        rows[b, mine, 2 * width : 2 * width + 128] = table[tokens_of(b)]
    prob_keep[...] = gate_prob
    inv_keep[...] = jnp.broadcast_to(inv_rms, (n_tok, 128))

    ups, downs = {}, {}
    bases = (at_x, at_own, at_y)

    def has_up(j):
        return jnp.logical_and(z < 3, z >= j)

    def has_down(j):
        return jnp.logical_and(z > 0, z + j <= 3)

    def chain(which, j):
        if j:
            pl.when(z >= j)(ups[which, j - 1].wait_recv)
            pl.when(z + j <= 3)(downs[which, j - 1].wait_recv)
        if j < 3:
            above = rows.at[:, rows_of(bases[which], 4 - j)]
            below = rows.at[:, rows_of(bases[which], j)]
            ups[which, j] = push(above, above, t_sems, (which, 0, j), z_peers[0], has_up(j))
            downs[which, j] = push(below, below, t_sems, (which, 1, j), z_peers[2], has_down(j))

    from_x = push(rows.at[:, mine], rows.at[:, rows_of(at_x, 0)], t_sems, (0, 2, 0), x_peer)
    from_y = push(rows.at[:, mine], rows.at[:, rows_of(at_y, 0)], t_sems, (2, 2, 0), y_peer)
    chain(1, 0)
    start_weights(1)
    from_x.wait_recv()
    chain(0, 0)
    from_y.wait_recv()
    chain(2, 0)
    relay_weights(0)
    for which in (1, 0, 2):
        chain(which, 1)
    side_weights(0)
    relay_weights(1)
    start_weights(2)
    for which in (1, 0, 2):
        chain(which, 2)
    side_weights(1)
    for kind in range(2):
        for l in range(2):
            last_weights(kind, l)

    def turn_weights(l):
        need_weights(0, l)
        need_weights(1, l)

        @pl.loop(0, 4)
        def _(j):
            at = pl.ds(pl.multiple_of(j * slab, slab), slab)
            wgu_t[l, :, at] = wgu[l, at, :].T

    turn_weights(0)
    turn_weights(1)
    relay_weights(2)
    side_weights(2)
    for which in (1, 0, 2):
        chain(which, 3)

    n_rows = 2 * n_lane
    all_rows = batches * n_rows
    wide_lanes = lax.broadcasted_iota(jnp.int32, (all_rows, 128), 1)

    for l in range(2):
        these = slice(l * n_lane, l * n_lane + n_rows)

        @pl.loop(0, 2)
        def _(k):
            cols = pl.ds(pl.multiple_of(k * hid, hid), hid)
            expert = (z * 2 + k) * 2 + l
            table = rows[:, these, 2 * width : 2 * width + 128].reshape(all_rows, 128).astype(f32)
            gate = jnp.sum(jnp.where(wide_lanes == expert, table, 0.0), axis=1, keepdims=True)
            tan = jnp.sum(
                jnp.where(wide_lanes == expert + 64, table, 0.0), axis=1, keepdims=True
            )
            pre = nn_dot(rows[:, these, 0:width].reshape(all_rows, width), wgu[l, :, cols])
            dots = nn_dot(
                rows[:, these, width : 2 * width].reshape(all_rows, width), wgu[l, :, cols]
            )
            pre_gate, pre_up = pre[:, 0:half], pre[:, half:hid]
            gate_dot, up_dot = dots[:, 0:half], dots[:, half:hid]
            sig = jax.nn.sigmoid(pre_gate)
            silu = pre_gate * sig
            slope_up = sig * (1.0 + pre_gate * (1.0 - sig)) * pre_up
            hidden = silu * pre_up
            mixed = tan * hidden + gate * (slope_up * gate_dot + silu * up_dot)
            keep_a[l, k] = gate * slope_up
            keep_s[l, k] = gate * silu
            keep_h[l, k] = hidden
            mix[l, :, pl.ds(pl.multiple_of(k * half, half), half)] = mixed.astype(bf)

    turns = [
        (part, own_part, mid, far, landed), (part2, own_part2, mid2, far2, landed2)
    ]
    x_copies, y_copies, z_copies, totals = {}, {}, {}, {}

    def place(turn, b, l, cols, term):
        parts, own = turns[turn][0:2]
        if l == 0:
            parts[b, at_x : at_x + n_lane, cols] = term[0:n_lane].astype(bf)
            own[b, :, cols] = term[n_lane:n_rows]
        else:
            own[b, :, cols] = own[b, :, cols] + term[0:n_lane]
            parts[b, at_y : at_y + n_lane, cols] = term[n_lane:n_rows].astype(bf)

    def send_side(turn, b, s):
        parts, far = turns[turn][0], turns[turn][3]
        peer, base = ((x_peer, at_x), (y_peer, at_y))[s]
        copies = (x_copies, y_copies)[s]
        for dz in (2, 1, 3, 0):
            copies[turn, b, dz] = push(
                parts.at[b, rows_of(base, dz)], far.at[b, s, rows_of(0, dz)],
                s_sems, (turn, b, s, dz), peer,
            )

    def merge(turn, b, dz):
        parts, own, mid, far, land = turns[turn]
        x_copies[turn, b, dz].wait_recv()
        y_copies[turn, b, dz].wait_recv()
        at = rows_of(0, dz)
        total = own[b, at, :] + (far[b, 0, at, :].astype(f32) + far[b, 1, at, :].astype(f32))
        if dz:
            mid[b, dz] = total.astype(bf)
            z_copies[turn, b, dz] = push(
                mid.at[b, dz], land.at[b, z], z_sems, (turn, b, dz), z_peers[dz - 1]
            )
        else:
            own[b, at, :] = total

    def total_of(turn, b):
        own, land = turns[turn][1], turns[turn][4]
        total = own[b, rows_of(0, 0), :]
        for dz in (1, 3, 2):
            z_copies[turn, b, dz].wait_recv()
            total = total + land[b, (z + 4 - dz) % 4].astype(f32)
        return total

    def down(b, l):
        left = mix[l, b * n_rows : (b + 1) * n_rows, :]
        place(0, b, l, slice(0, width), nn_dot(left, wd[l]))
        send_side(0, b, l)

    links, sides, stores = {}, {}, []

    def store(b, part):
        piece = (tokens_of(b), pl.ds(part * width, width))
        stores.append(
            pltpu.make_async_copy(both_ref.at[piece], both_hbm.at[piece], o_sems.at[b, part])
        )
        stores[-1].start()

    def image_to_sides(b, dz, cond=None):
        block = image_rows.at[b, rows_of(at_own, 4 - dz)]
        for s, (peer, base) in enumerate(((x_peer, at_x), (y_peer, at_y))):
            sides[b, s, dz] = push(
                block, image_rows.at[b, rows_of(base, 4 - dz)], a_sems, (b, s, dz), peer, cond
            )

    def image_link(b, way, j):
        block = image_rows.at[b, rows_of(at_own, (4 - j, j)[way])]
        links[b, way, j] = push(
            block, block, l_sems, (b, way, j), z_peers[(0, 2)[way]], (has_up, has_down)[way](j)
        )

    def image_of(b):
        image = total_of(0, b)
        both_ref[tokens_of(b), 0:width] = image
        image_rows[b, mine, :] = image.astype(bf)
        image_link(b, 0, 0)
        image_link(b, 1, 0)
        image_to_sides(b, 0)
        store(b, 0)

    def image_on(b, j):
        for way, here, dz in ((0, z > j, 1 + j), (1, z < 3 - j, 3 - j)):
            pl.when(here)(links[b, way, j].wait_recv)
            if j < 2:
                image_link(b, way, j + 1)
            image_to_sides(b, dz, here)

    def backward(b, l):
        for dz in range(4):
            sides[b, l, dz].wait_recv()
        these = slice(l * n_lane, l * n_lane + n_rows)
        kept = slice(b * n_rows, (b + 1) * n_rows)
        cots = jnp.zeros((n_rows, 128), f32)
        back_both = nt_dot(image_rows[b, these, :], wd[l])
        for k in range(2):
            back = back_both[:, k * half : (k + 1) * half]
            cot = jnp.sum(back * keep_h[l, k, kept], axis=1, keepdims=True)
            cots = cots + jnp.where(wide_lanes[0:n_rows] == (z * 2 + k) * 2 + l, cot, 0.0)
            grads[l, :, k * hid : k * hid + half] = (back * keep_a[l, k, kept]).astype(bf)
            grads[l, :, k * hid + half : (k + 1) * hid] = (back * keep_s[l, k, kept]).astype(bf)
        place(1, b, l, slice(width, width + 128), cots)
        place(1, b, l, slice(0, width), nn_dot(grads[l], wgu_t[l]))
        send_side(1, b, l)

    def gram_of(b):
        total = total_of(1, b)
        these = tokens_of(b)
        expert_grad = total[:, 0:width]
        cot = total[:, width : width + 128]
        prob = prob_keep[these, :]
        column_grad = prob * (cot - jnp.sum(prob * cot, axis=1, keepdims=True))
        high = column_grad.astype(bf)
        rest = column_grad - high.astype(f32)
        middle = rest.astype(bf)
        low = (rest - middle.astype(f32)).astype(bf)
        router = router_pad[...]
        router_grad = nn_dot(high, router) + (nn_dot(middle, router) + nn_dot(low, router))
        xfull = tok_ref[these, :].astype(f32)
        inv_rms = inv_keep[these, 0:1]
        pulled = gain_ref[...] * (expert_grad + router_grad)
        both_ref[these, width : 2 * width] = inv_rms * pulled - xfull * (inv_rms * inv_rms * inv_rms) * jnp.mean(
            pulled * xfull, axis=1, keepdims=True
        )
        store(b, 1)

    last_weights(2, 0)
    last_weights(2, 1)
    need_weights(2, 0)
    down(0, 0)
    need_weights(2, 1)
    down(0, 1)
    down(1, 0)
    down(1, 1)
    merge(0, 0, 2)
    merge(0, 0, 1)
    merge(0, 0, 3)
    merge(0, 0, 0)
    merge(0, 1, 2)
    image_of(0)
    merge(0, 1, 1)
    merge(0, 1, 3)
    image_on(0, 0)
    merge(0, 1, 0)
    image_of(1)
    image_on(0, 1)
    image_on(1, 0)
    image_on(0, 2)
    image_on(1, 1)
    image_on(1, 2)
    backward(0, 0)
    backward(0, 1)
    backward(1, 0)
    backward(1, 1)
    merge(1, 0, 2)
    merge(1, 0, 1)
    merge(1, 0, 3)
    merge(1, 0, 0)
    merge(1, 1, 2)
    merge(1, 1, 1)
    merge(1, 1, 3)
    merge(1, 1, 0)
    gram_of(0)
    gram_of(1)
    for copy in stores:
        copy.wait()
    for copy, cond in pending:
        if cond is None:
            copy.wait_send()
        else:
            pl.when(cond)(copy.wait_send)


def on_device_dense(tokens, tangent, norm_gain, router, w_gate, w_up, w_down, routes):
    n_tok, width = tokens.shape
    hid = w_gate.shape[2]
    half = hid // 2
    n_sub = n_tok // batches
    n_lane = 4 * n_sub
    n_rows = 2 * n_lane
    bf, f32 = jnp.bfloat16, jnp.float32
    hbm = pl.BlockSpec(memory_space=pl.ANY)
    out = jax.ShapeDtypeStruct((n_tok, 2 * width), f32)
    dma = pltpu.SemaphoreType.DMA
    keep = pltpu.VMEM((2, 2, batches * n_rows, half), f32)

    def home(columns):
        return [
            pltpu.VMEM((batches, 3 * n_lane, columns), bf),
            pltpu.VMEM((batches, n_lane, columns), f32),
            pltpu.VMEM((batches, 4, n_sub, columns), bf),
            pltpu.VMEM((batches, 2, n_lane, columns), bf),
            pltpu.VMEM((batches, 4, n_sub, columns), bf),
        ]

    both = pl.pallas_call(
        block_kernel,
        out_shape=out,
        in_specs=[hbm] * 8,
        out_specs=hbm,
        scratch_shapes=[
            pltpu.VMEM((n_tok, width), bf),
            pltpu.VMEM((n_tok, width), bf),
            pltpu.VMEM((1, width), f32),
            pltpu.VMEM((router.shape[1], width), bf),
            pltpu.VMEM((routes.shape[1], n_tok), routes.dtype),
            pltpu.VMEM((n_tok, 2 * width), f32),
            pltpu.VMEM((2, width, 2 * hid), bf),
            pltpu.VMEM((2, 2 * hid, width), bf),
            pltpu.VMEM((2, hid, width), bf),
            pltpu.VMEM((batches, 3 * n_lane, 2 * width + 128), bf),
            keep, keep, keep,
            pltpu.VMEM((2, batches * n_rows, hid), bf),
            *home(width),
            pltpu.VMEM((batches, 3 * n_lane, width), bf),
            pltpu.VMEM((2, n_rows, 2 * hid), bf),
            *home(width + 128),
            pltpu.VMEM((n_tok, 128), f32),
            pltpu.VMEM((n_tok, 128), f32),
            pltpu.VMEM((128, width), bf),
            dma((3, 2, 3)), dma((3, 2, 3)), dma((3, 2)),
            dma((3, 2, 4)), dma((3, 2, 4)),
            dma((3, 3, 3)), dma((3, 3, 3)), dma((batches, 2, 4)), dma((batches, 2, 4)),
            dma((2, batches, 2, 4)), dma((2, batches, 2, 4)),
            dma((2, batches, 4)), dma((2, batches, 4)),
            dma((batches, 2, 3)), dma((batches, 2, 3)), dma((5,)), dma((batches, 2)),
        ],
        compiler_params=pltpu.CompilerParams(
            collective_id=0, has_side_effects=True, vmem_limit_bytes=60 * 2**20
        ),
        cost_estimate=pl.CostEstimate(
            flops=2 * 8 * 512 * width * hid, bytes_accessed=2**24, transcendentals=2**20
        ),
    )(tokens, tangent, norm_gain.reshape(1, width), router.T, routes.T, w_gate, w_up, w_down)
    return both[:, 0:width], both[:, width : 2 * width]


def solution(mesh):
    in_specs = (
        P(("dp", "expert"), None),
        P(("dp", "expert"), None),
        P(),
        P(),
        P("expert", "dp", None),
        P("expert", "dp", None),
        P("expert", None, "dp"),
        P(("dp", "expert"), None),
    )
    out_specs = (P(("dp", "expert"), None), P(("dp", "expert"), None))
    body = on_device
    if mesh.shape["dp"] == 4 and mesh.shape["expert"] == 8:
        body = on_device_dense
    return jax.shard_map(
        body, mesh=mesh, in_specs=in_specs, out_specs=out_specs, check_vma=False
    )
```

```python
import functools

import jax
import jax.numpy as jnp
from jax import lax
from jax.experimental import pallas as pl
from jax.experimental.pallas import tpu as pltpu
from jax.sharding import PartitionSpec as P

eps_value = 1e-06


def pick_columns(table, routes):
    hits = routes[:, :, None] == jnp.arange(table.shape[1], dtype=jnp.int32)[None, None, :]
    return jnp.sum(jnp.where(hits, table[:, None, :], jnp.zeros((), table.dtype)), axis=2)


def on_device(tokens, tangent, norm_gain, router, w_gate, w_up, w_down, routes):
    tok_rows, topk = routes.shape
    model_width = tokens.shape[1]
    experts_all = router.shape[1]
    local_experts = w_gate.shape[0]
    groups = lax.axis_size("expert")
    capacity = 2 * tok_rows * topk // experts_all
    xfull = tokens.astype(jnp.float32)
    vfull = tangent.astype(jnp.float32)
    inv_rms = lax.rsqrt(jnp.mean(xfull * xfull, axis=1, keepdims=True) + eps_value)
    normed = (norm_gain * xfull * inv_rms).astype(jnp.bfloat16)
    cross_term = jnp.mean(xfull * vfull, axis=1, keepdims=True)
    normed_tan = (norm_gain * (vfull * inv_rms - xfull * inv_rms**3 * cross_term)).astype(
        jnp.bfloat16
    )
    logits = jnp.dot(normed, router, preferred_element_type=jnp.float32)
    logit_tan = jnp.dot(normed_tan, router, preferred_element_type=jnp.float32)
    selected = pick_columns(logits, routes)
    sel_tan = pick_columns(logit_tan, routes)
    exp_sel = jnp.exp(selected)
    gate_prob = exp_sel / jnp.sum(exp_sel, axis=1, keepdims=True)
    gate_tan = gate_prob * (sel_tan - jnp.sum(gate_prob * sel_tan, axis=1, keepdims=True))
    gate_b = gate_prob.astype(jnp.bfloat16)
    gate_tan_b = gate_tan.astype(jnp.bfloat16)
    pair_count = tok_rows * topk
    flat_ids = routes.reshape(-1)
    order = jnp.arange(pair_count, dtype=jnp.int32)
    earlier = (flat_ids[None, :] == flat_ids[:, None]) & (order[None, :] < order[:, None])
    slot_rank = jnp.sum(earlier.astype(jnp.int32), axis=1)
    slot_of_pair = flat_ids * capacity + slot_rank
    slot_hits = slot_of_pair[None, :] == jnp.arange(experts_all * capacity, dtype=jnp.int32)[:, None]
    slot_table = jnp.max(
        jnp.where(slot_hits, jnp.arange(pair_count, dtype=jnp.int32)[None, :], -1), axis=1
    )
    slot_valid = slot_table >= 0
    safe_pair = jnp.maximum(slot_table, 0)
    tok_idx = safe_pair // topk
    which_k = safe_pair % topk
    bf_zero = jnp.zeros((), jnp.bfloat16)
    send_rows = jnp.stack(
        (
            jnp.where(slot_valid[:, None], normed[tok_idx], bf_zero),
            jnp.where(slot_valid[:, None], normed_tan[tok_idx], bf_zero),
        )
    )
    send_rows = send_rows.reshape(2, groups, local_experts * capacity, model_width)
    send_gates = jnp.stack(
        (
            jnp.where(slot_valid, gate_b[tok_idx, which_k], bf_zero),
            jnp.where(slot_valid, gate_tan_b[tok_idx, which_k], bf_zero),
        )
    )
    send_gates = send_gates.reshape(2, groups, local_experts * capacity)
    recv_rows, recv_gates = (
        lax.all_to_all(send_rows, "expert", split_axis=1, concat_axis=1, tiled=True),
        lax.all_to_all(send_gates, "expert", split_axis=1, concat_axis=1, tiled=True),
    )
    slot_rows = recv_rows.reshape(2, groups, local_experts, capacity, model_width)
    recv_gates = recv_gates.reshape(2, groups, local_experts, capacity).astype(jnp.float32)
    gate_val = recv_gates[0][..., None]
    tan_val = recv_gates[1][..., None]
    gate_full, up_full, down_full = (
        lax.all_gather(w_gate, "dp", axis=1, tiled=True),
        lax.all_gather(w_up, "dp", axis=1, tiled=True),
        lax.all_gather(w_down, "dp", axis=2, tiled=True),
    )
    pre_both = jnp.einsum(
        "tslkd,ldf->tslkf", slot_rows, gate_full, preferred_element_type=jnp.float32
    )
    up_both = jnp.einsum("tslkd,ldf->tslkf", slot_rows, up_full, preferred_element_type=jnp.float32)
    pre_gate = pre_both[0]
    gate_dot = pre_both[1]
    pre_up = up_both[0]
    up_dot = up_both[1]
    sig_gate = jax.nn.sigmoid(pre_gate)
    silu_gate = pre_gate * sig_gate
    slope_gate = sig_gate * (1.0 + pre_gate * (1.0 - sig_gate))
    hidden = silu_gate * pre_up
    hidden_tan = slope_gate * gate_dot * pre_up + silu_gate * up_dot
    mixed_rows = (tan_val * hidden + gate_val * hidden_tan).astype(jnp.bfloat16)
    pair_image = jnp.einsum(
        "slkf,lfd->slkd", mixed_rows, down_full, preferred_element_type=jnp.float32
    )
    pair_send = pair_image.astype(jnp.bfloat16).reshape(
        groups, local_experts * capacity, model_width
    )
    pair_back = lax.all_to_all(pair_send, "expert", split_axis=0, concat_axis=0, tiled=True)
    pair_back = pair_back.reshape(experts_all * capacity, model_width)
    tangent_image = jnp.sum(
        pair_back[slot_of_pair].astype(jnp.float32).reshape(tok_rows, topk, model_width), axis=1
    )
    image_b = tangent_image.astype(jnp.bfloat16)
    send_cot = jnp.where(slot_valid[:, None], image_b[tok_idx], bf_zero).reshape(
        groups, local_experts * capacity, model_width
    )
    recv_cot = lax.all_to_all(send_cot, "expert", split_axis=0, concat_axis=0, tiled=True)
    recv_cot = recv_cot.reshape(groups, local_experts, capacity, model_width)
    back_hidden = jnp.einsum(
        "slkd,lfd->slkf", recv_cot, down_full, preferred_element_type=jnp.float32
    )
    gate_cot = jnp.sum(back_hidden * hidden, axis=3).astype(jnp.bfloat16)
    scaled = gate_val * back_hidden
    grad_gate = (scaled * pre_up * slope_gate).astype(jnp.bfloat16)
    grad_up = (scaled * silu_gate).astype(jnp.bfloat16)
    pair_grad = jnp.einsum(
        "slkf,ldf->slkd", grad_gate, gate_full, preferred_element_type=jnp.float32
    )
    pair_grad = pair_grad + jnp.einsum(
        "slkf,ldf->slkd", grad_up, up_full, preferred_element_type=jnp.float32
    )
    grad_send = pair_grad.astype(jnp.bfloat16).reshape(
        groups, local_experts * capacity, model_width
    )
    cot_send = gate_cot.reshape(groups, local_experts * capacity)
    grad_back, cot_back = (
        lax.all_to_all(grad_send, "expert", split_axis=0, concat_axis=0, tiled=True),
        lax.all_to_all(cot_send, "expert", split_axis=0, concat_axis=0, tiled=True),
    )
    grad_back = grad_back.reshape(experts_all * capacity, model_width)
    cot_back = cot_back.reshape(experts_all * capacity)
    expert_grad = jnp.sum(
        grad_back[slot_of_pair].astype(jnp.float32).reshape(tok_rows, topk, model_width), axis=1
    )
    pair_cot = cot_back[slot_of_pair].astype(jnp.float32).reshape(tok_rows, topk)
    logit_grad = gate_prob * (pair_cot - jnp.sum(gate_prob * pair_cot, axis=1, keepdims=True))
    hits = routes[:, :, None] == jnp.arange(experts_all, dtype=jnp.int32)[None, None, :]
    column_grad = jnp.sum(jnp.where(hits, logit_grad[:, :, None], 0.0), axis=1)
    router_grad = jnp.dot(
        column_grad, router.astype(jnp.float32).T, precision=lax.Precision.HIGHEST
    )
    pulled = norm_gain * (expert_grad + router_grad)
    gram_image = inv_rms * pulled - xfull * inv_rms**3 * jnp.mean(
        pulled * xfull, axis=1, keepdims=True
    )
    return (tangent_image, gram_image)


MESH = pl.DeviceIdType.MESH


def nt_dot(left, right):
    return lax.dot_general(
        left, right, (((1,), (1,)), ((), ())), preferred_element_type=jnp.float32
    )


def nn_dot(left, right):
    return jnp.dot(left, right, preferred_element_type=jnp.float32)


batches = 2


def block_kernel(
    tok_hbm, tan_hbm, gain_hbm, router_hbm, routes_hbm, wg_ref, wu_ref, wd_ref,
    both_hbm,
    tok_ref, tan_ref, gain_ref, router_ref, routes_ref, both_ref,
    wgu, wgu_t, wd, rows, keep_a, keep_s, keep_h, mix, part, own_part, mid, far, landed,
    image_rows, grads, part2, own_part2, mid2, far2, landed2, prob_keep, inv_keep, router_pad,
    w_send, w_recv, w_own, m_send, m_recv, t_send, t_recv, a_send, a_recv, s_send, s_recv,
    z_send, z_recv, l_send, l_recv, i_sems, o_sems,
):
    f32, bf = jnp.float32, jnp.bfloat16
    n_tok, width = tok_ref.shape
    slab, hid = wg_ref.shape[1], wg_ref.shape[2]
    half = hid // 2
    n_sub = n_tok // batches
    n_lane = 4 * n_sub
    n_exp = router_ref.shape[0]
    dp, ex = lax.axis_index("dp"), lax.axis_index("expert")
    y, x = dp // 2, dp % 2
    z, core = ex // 2, ex % 2
    x_index, y_index = y * 2 + 1 - x, (1 - y) * 2 + x
    d_index = (1 - y) * 2 + 1 - x
    x_peer, y_peer = (x_index, ex), (y_index, ex)
    mate = (dp, z * 2 + 1 - core)
    z_peers = [(dp, (z + dz) % 4 * 2 + core) for dz in range(1, 4)]
    at_x, at_own, at_y = 0, n_lane, 2 * n_lane

    def rows_of(base, dz):
        return pl.ds(pl.multiple_of(base + (z + dz) % 4 * n_sub, n_sub), n_sub)

    def tokens_of(b):
        return slice(b * n_sub, (b + 1) * n_sub)

    loads = [
        pltpu.make_async_copy(src, dst, i_sems.at[i])
        for i, (src, dst) in enumerate((
            (tok_hbm, tok_ref), (tan_hbm, tan_ref), (gain_hbm, gain_ref),
            (router_hbm, router_ref), (routes_hbm, routes_ref),
        ))
    ]
    for load in loads:
        load.start()

    barrier = pltpu.get_barrier_semaphore()
    friends = [
        (x_peer, None), (y_peer, None), (mate, None), (z_peers[0], z < 3), (z_peers[2], z > 0)
    ]

    def greet(friend):
        pl.semaphore_signal(barrier, inc=1, device_id=friend, device_id_type=MESH)

    for friend, cond in friends:
        if cond is None:
            greet(friend)
        else:
            pl.when(cond)(functools.partial(greet, friend))
    inner = jnp.where(z > 0, 1, 0) * jnp.where(z < 3, 1, 0)
    pl.semaphore_wait(barrier, 4 + inner)

    pending = []

    def push(src, dst, sems, where, device, cond=None):
        copy = pltpu.make_async_remote_copy(
            src_ref=src, dst_ref=dst, send_sem=sems[0].at[where], recv_sem=sems[1].at[where],
            device_id=device, device_id_type=MESH,
        )
        if cond is None:
            copy.start()
        else:
            pl.when(cond)(copy.start)
        pending.append((copy, cond))
        return copy

    def slab_of(index):
        return pl.ds(pl.multiple_of(index * slab, slab), slab)

    def weight_at(kind, l, index):
        if kind == 2:
            return wd.at[l, pl.ds(pl.multiple_of(core * half, half), half), slab_of(index)]
        first = pl.multiple_of(core * hid + kind * half, half)
        return wgu.at[l, slab_of(index), pl.ds(first, half)]

    def weight_src(kind, l, which):
        part_of = pl.ds(pl.multiple_of(which * half, half), half)
        if kind == 2:
            return wd_ref.at[l, part_of, :]
        return (wg_ref, wu_ref)[kind].at[l, :, part_of]

    direct, relayed, shared, local = {}, {}, {}, {}
    w_sems, m_sems, t_sems = (w_send, w_recv), (m_send, m_recv), (t_send, t_recv)
    a_sems, s_sems, z_sems = (a_send, a_recv), (s_send, s_recv), (z_send, z_recv)
    l_sems = (l_send, l_recv)

    def start_weights(kind):
        for p, l in ((0, 0), (1, 1), (0, 1), (1, 0)):
            for_x, for_y = (1 - x, x) if l == 0 else (y, 1 - y)
            direct[kind, l, p] = push(
                weight_src(kind, l, (for_x, for_y)[p]), weight_at(kind, l, dp),
                w_sems, (kind, l, p), (x_peer, y_peer)[p],
            )
        for l in range(2):
            for_me = (x, y)[l]
            mine = weight_at(kind, l, dp)
            local[kind, l] = pltpu.make_async_copy(
                weight_src(kind, l, for_me), mine, w_own.at[kind, l]
            )
            local[kind, l].start()
            shared[kind, l] = [
                push(weight_src(kind, l, for_me), mine, m_sems, (kind, l, 0), mate)
            ]

    def share_weights(kind, l, slot, index):
        block = weight_at(kind, l, index)
        shared[kind, l].append(push(block, block, m_sems, (kind, l, slot), mate))

    def relay_weights(kind):
        for l in range(2):
            index = (x_index, y_index)[l]
            block = weight_at(kind, l, index)
            direct[kind, l, l].wait_recv()
            relayed[kind, l] = push(block, block, w_sems, (kind, l, 2), (y_peer, x_peer)[l])
            share_weights(kind, l, 1, index)

    def side_weights(kind):
        for l in range(2):
            direct[kind, l, 1 - l].wait_recv()
            share_weights(kind, l, 2, (x_index, y_index)[1 - l])

    def last_weights(kind, l):
        relayed[kind, l].wait_recv()
        share_weights(kind, l, 3, d_index)

    def need_weights(kind, l):
        local[kind, l].wait()
        for copy in shared[kind, l]:
            copy.wait_recv()

    start_weights(0)

    for load in loads:
        load.wait()
    router_pad[...] = jnp.zeros(router_pad.shape, bf)
    router_pad[0:n_exp, :] = router_ref[...]
    xfull = tok_ref[...].astype(f32)
    vfull = tan_ref[...].astype(f32)
    gain = gain_ref[...]
    inv_rms = lax.rsqrt(jnp.mean(xfull * xfull, axis=1, keepdims=True) + eps_value)
    normed = (gain * xfull * inv_rms).astype(bf)
    cross_term = jnp.mean(xfull * vfull, axis=1, keepdims=True)
    inv_cube = inv_rms * inv_rms * inv_rms
    normed_tan = (gain * (vfull * inv_rms - xfull * inv_cube * cross_term)).astype(bf)
    mine = rows_of(at_own, 0)
    for b in range(batches):
        rows[b, mine, 0:width] = normed[tokens_of(b)]
        rows[b, mine, width : 2 * width] = normed_tan[tokens_of(b)]
    logits = nt_dot(normed, router_pad[...])
    logit_tan = nt_dot(normed_tan, router_pad[...])
    ids = lax.broadcasted_iota(jnp.int32, (128, n_tok), 0)
    chosen_by = jnp.zeros((128, n_tok), f32)
    for k in range(routes_ref.shape[0]):
        chosen_by = chosen_by + jnp.where(ids == routes_ref[k : k + 1, :], 1.0, 0.0)
    unit = jnp.where(
        lax.broadcasted_iota(jnp.int32, (n_tok, n_tok), 0)
        == lax.broadcasted_iota(jnp.int32, (n_tok, n_tok), 1),
        1.0, 0.0,
    ).astype(bf)
    chosen = nt_dot(unit, chosen_by.astype(bf))
    exp_sel = jnp.where(chosen > 0.5, jnp.exp(logits), 0.0)
    gate_prob = exp_sel / jnp.sum(exp_sel, axis=1, keepdims=True)
    gate_tan = gate_prob * (
        logit_tan - jnp.sum(gate_prob * logit_tan, axis=1, keepdims=True)
    )
    table = (gate_prob + pltpu.roll(gate_tan, 64, 1)).astype(bf)
    for b in range(batches):
        rows[b, mine, 2 * width : 2 * width + 128] = table[tokens_of(b)]
    prob_keep[...] = gate_prob
    inv_keep[...] = jnp.broadcast_to(inv_rms, (n_tok, 128))

    ups, downs = {}, {}
    bases = (at_x, at_own, at_y)

    def has_up(j):
        return jnp.logical_and(z < 3, z >= j)

    def has_down(j):
        return jnp.logical_and(z > 0, z + j <= 3)

    def chain(which, j):
        if j:
            pl.when(z >= j)(ups[which, j - 1].wait_recv)
            pl.when(z + j <= 3)(downs[which, j - 1].wait_recv)
        if j < 3:
            above = rows.at[:, rows_of(bases[which], 4 - j)]
            below = rows.at[:, rows_of(bases[which], j)]
            ups[which, j] = push(above, above, t_sems, (which, 0, j), z_peers[0], has_up(j))
            downs[which, j] = push(below, below, t_sems, (which, 1, j), z_peers[2], has_down(j))

    from_x = push(rows.at[:, mine], rows.at[:, rows_of(at_x, 0)], t_sems, (0, 2, 0), x_peer)
    from_y = push(rows.at[:, mine], rows.at[:, rows_of(at_y, 0)], t_sems, (2, 2, 0), y_peer)
    chain(1, 0)
    start_weights(1)
    from_x.wait_recv()
    chain(0, 0)
    from_y.wait_recv()
    chain(2, 0)
    relay_weights(0)
    for which in (1, 0, 2):
        chain(which, 1)
    side_weights(0)
    relay_weights(1)
    start_weights(2)
    for which in (1, 0, 2):
        chain(which, 2)
    side_weights(1)
    for kind in range(2):
        for l in range(2):
            last_weights(kind, l)

    def turn_weights(l):
        need_weights(0, l)
        need_weights(1, l)

        @pl.loop(0, 4)
        def _(j):
            at = pl.ds(pl.multiple_of(j * slab, slab), slab)
            wgu_t[l, :, at] = wgu[l, at, :].T

    turn_weights(0)
    turn_weights(1)
    relay_weights(2)
    side_weights(2)
    for which in (1, 0, 2):
        chain(which, 3)

    n_rows = 2 * n_lane
    all_rows = batches * n_rows
    wide_lanes = lax.broadcasted_iota(jnp.int32, (all_rows, 128), 1)

    for l in range(2):
        these = slice(l * n_lane, l * n_lane + n_rows)

        @pl.loop(0, 2)
        def _(k):
            cols = pl.ds(pl.multiple_of(k * hid, hid), hid)
            expert = (z * 2 + k) * 2 + l
            table = rows[:, these, 2 * width : 2 * width + 128].reshape(all_rows, 128).astype(f32)
            gate = jnp.sum(jnp.where(wide_lanes == expert, table, 0.0), axis=1, keepdims=True)
            tan = jnp.sum(
                jnp.where(wide_lanes == expert + 64, table, 0.0), axis=1, keepdims=True
            )
            pre = nn_dot(rows[:, these, 0:width].reshape(all_rows, width), wgu[l, :, cols])
            dots = nn_dot(
                rows[:, these, width : 2 * width].reshape(all_rows, width), wgu[l, :, cols]
            )
            pre_gate, pre_up = pre[:, 0:half], pre[:, half:hid]
            gate_dot, up_dot = dots[:, 0:half], dots[:, half:hid]
            sig = jax.nn.sigmoid(pre_gate)
            silu = pre_gate * sig
            slope_up = sig * (1.0 + pre_gate * (1.0 - sig)) * pre_up
            hidden = silu * pre_up
            mixed = tan * hidden + gate * (slope_up * gate_dot + silu * up_dot)
            keep_a[l, k] = gate * slope_up
            keep_s[l, k] = gate * silu
            keep_h[l, k] = hidden
            mix[l, :, pl.ds(pl.multiple_of(k * half, half), half)] = mixed.astype(bf)

    turns = [
        (part, own_part, mid, far, landed), (part2, own_part2, mid2, far2, landed2)
    ]
    x_copies, y_copies = {}, {}

    def by_z(a, b, c, d):
        return jnp.where(z < 2, jnp.where(z < 1, a, b), jnp.where(z < 3, c, d))

    far_first = {0: 0, 2: by_z(3, 2, 2, 1), 1: by_z(2, 1, 3, 2), 3: by_z(1, 3, 1, 3)}

    def place(turn, b, l, cols, term):
        parts, own = turns[turn][0:2]
        if l == 0:
            parts[b, at_x : at_x + n_lane, cols] = term[0:n_lane].astype(bf)
            own[b, :, cols] = term[n_lane:n_rows]
        else:
            own[b, :, cols] = own[b, :, cols] + term[0:n_lane]
            parts[b, at_y : at_y + n_lane, cols] = term[n_lane:n_rows].astype(bf)

    def send_side(turn, b, s):
        parts, far = turns[turn][0], turns[turn][3]
        peer, base = ((x_peer, at_x), (y_peer, at_y))[s]
        copies = (x_copies, y_copies)[s]
        for turn_no in (2, 1, 3, 0):
            dz = far_first[turn_no]
            copies[turn, b, turn_no] = push(
                parts.at[b, rows_of(base, dz)], far.at[b, s, rows_of(0, dz)],
                s_sems, (turn, b, s, dz), peer,
            )

    def merge(turn, b, turn_no):
        parts, own, mid, far, land = turns[turn]
        dz = far_first[turn_no]
        x_copies[turn, b, turn_no].wait_recv()
        y_copies[turn, b, turn_no].wait_recv()
        at = rows_of(0, dz)
        total = own[b, at, :] + (far[b, 0, at, :].astype(f32) + far[b, 1, at, :].astype(f32))
        if turn_no:
            mid[b, turn_no] = total.astype(bf)
            push(
                mid.at[b, turn_no], land.at[b, z], z_sems, (turn, b, dz),
                (dp, (z + dz) % 4 * 2 + core),
            )
        else:
            own[b, at, :] = total

    def total_of(turn, b):
        own, mid, land = turns[turn][1], turns[turn][2], turns[turn][4]
        total = own[b, rows_of(0, 0), :]
        for dz in (1, 3, 2):
            pltpu.make_async_remote_copy(
                src_ref=mid.at[b, dz], dst_ref=land.at[b, (z + 4 - dz) % 4],
                send_sem=z_send.at[turn, b, dz], recv_sem=z_recv.at[turn, b, dz],
                device_id=z_peers[dz - 1], device_id_type=MESH,
            ).wait_recv()
            total = total + land[b, (z + 4 - dz) % 4].astype(f32)
        return total

    def down(b, l):
        left = mix[l, b * n_rows : (b + 1) * n_rows, :]
        place(0, b, l, slice(0, width), nn_dot(left, wd[l]))
        send_side(0, b, l)

    links, sides, stores = {}, {}, []

    def store(b, part):
        piece = (tokens_of(b), pl.ds(part * width, width))
        stores.append(
            pltpu.make_async_copy(both_ref.at[piece], both_hbm.at[piece], o_sems.at[b, part])
        )
        stores[-1].start()

    def image_to_sides(b, dz, cond=None):
        block = image_rows.at[b, rows_of(at_own, 4 - dz)]
        for s, (peer, base) in enumerate(((x_peer, at_x), (y_peer, at_y))):
            sides[b, s, dz] = push(
                block, image_rows.at[b, rows_of(base, 4 - dz)], a_sems, (b, s, dz), peer, cond
            )

    def image_link(b, way, j):
        block = image_rows.at[b, rows_of(at_own, (4 - j, j)[way])]
        links[b, way, j] = push(
            block, block, l_sems, (b, way, j), z_peers[(0, 2)[way]], (has_up, has_down)[way](j)
        )

    def image_of(b):
        image = total_of(0, b)
        both_ref[tokens_of(b), 0:width] = image
        image_rows[b, mine, :] = image.astype(bf)
        image_link(b, 0, 0)
        image_link(b, 1, 0)
        image_to_sides(b, 0)
        store(b, 0)

    def image_on(b, j):
        for way, here, dz in ((0, z > j, 1 + j), (1, z < 3 - j, 3 - j)):
            pl.when(here)(links[b, way, j].wait_recv)
            if j < 2:
                image_link(b, way, j + 1)
            image_to_sides(b, dz, here)

    def backward(b, l):
        for dz in range(4):
            sides[b, l, dz].wait_recv()
        these = slice(l * n_lane, l * n_lane + n_rows)
        kept = slice(b * n_rows, (b + 1) * n_rows)
        cots = jnp.zeros((n_rows, 128), f32)
        back_both = nt_dot(image_rows[b, these, :], wd[l])
        for k in range(2):
            back = back_both[:, k * half : (k + 1) * half]
            cot = jnp.sum(back * keep_h[l, k, kept], axis=1, keepdims=True)
            cots = cots + jnp.where(wide_lanes[0:n_rows] == (z * 2 + k) * 2 + l, cot, 0.0)
            grads[l, :, k * hid : k * hid + half] = (back * keep_a[l, k, kept]).astype(bf)
            grads[l, :, k * hid + half : (k + 1) * hid] = (back * keep_s[l, k, kept]).astype(bf)
        place(1, b, l, slice(width, width + 128), cots)
        place(1, b, l, slice(0, width), nn_dot(grads[l], wgu_t[l]))
        send_side(1, b, l)

    def gram_of(b):
        total = total_of(1, b)
        these = tokens_of(b)
        expert_grad = total[:, 0:width]
        cot = total[:, width : width + 128]
        prob = prob_keep[these, :]
        column_grad = prob * (cot - jnp.sum(prob * cot, axis=1, keepdims=True))
        high = column_grad.astype(bf)
        rest = column_grad - high.astype(f32)
        middle = rest.astype(bf)
        low = (rest - middle.astype(f32)).astype(bf)
        router = router_pad[...]
        router_grad = nn_dot(high, router) + (nn_dot(middle, router) + nn_dot(low, router))
        xfull = tok_ref[these, :].astype(f32)
        inv_rms = inv_keep[these, 0:1]
        pulled = gain_ref[...] * (expert_grad + router_grad)
        both_ref[these, width : 2 * width] = inv_rms * pulled - xfull * (inv_rms * inv_rms * inv_rms) * jnp.mean(
            pulled * xfull, axis=1, keepdims=True
        )
        store(b, 1)

    last_weights(2, 0)
    last_weights(2, 1)
    need_weights(2, 0)
    down(0, 0)
    need_weights(2, 1)
    down(0, 1)
    down(1, 0)
    down(1, 1)
    merge(0, 0, 2)
    merge(0, 0, 1)
    merge(0, 0, 3)
    merge(0, 0, 0)
    merge(0, 1, 2)
    image_of(0)
    merge(0, 1, 1)
    merge(0, 1, 3)
    image_on(0, 0)
    merge(0, 1, 0)
    image_of(1)
    image_on(0, 1)
    image_on(1, 0)
    image_on(0, 2)
    image_on(1, 1)
    image_on(1, 2)
    backward(0, 0)
    backward(0, 1)
    backward(1, 0)
    backward(1, 1)
    merge(1, 0, 2)
    merge(1, 0, 1)
    merge(1, 0, 3)
    merge(1, 0, 0)
    merge(1, 1, 2)
    merge(1, 1, 1)
    merge(1, 1, 3)
    merge(1, 1, 0)
    gram_of(0)
    gram_of(1)
    for copy in stores:
        copy.wait()
    for copy, cond in pending:
        if cond is None:
            copy.wait_send()
        else:
            pl.when(cond)(copy.wait_send)


def on_device_dense(tokens, tangent, norm_gain, router, w_gate, w_up, w_down, routes):
    n_tok, width = tokens.shape
    hid = w_gate.shape[2]
    half = hid // 2
    n_sub = n_tok // batches
    n_lane = 4 * n_sub
    n_rows = 2 * n_lane
    bf, f32 = jnp.bfloat16, jnp.float32
    hbm = pl.BlockSpec(memory_space=pl.ANY)
    out = jax.ShapeDtypeStruct((n_tok, 2 * width), f32)
    dma = pltpu.SemaphoreType.DMA
    keep = pltpu.VMEM((2, 2, batches * n_rows, half), f32)

    def home(columns):
        return [
            pltpu.VMEM((batches, 3 * n_lane, columns), bf),
            pltpu.VMEM((batches, n_lane, columns), f32),
            pltpu.VMEM((batches, 4, n_sub, columns), bf),
            pltpu.VMEM((batches, 2, n_lane, columns), bf),
            pltpu.VMEM((batches, 4, n_sub, columns), bf),
        ]

    both = pl.pallas_call(
        block_kernel,
        out_shape=out,
        in_specs=[hbm] * 8,
        out_specs=hbm,
        scratch_shapes=[
            pltpu.VMEM((n_tok, width), bf),
            pltpu.VMEM((n_tok, width), bf),
            pltpu.VMEM((1, width), f32),
            pltpu.VMEM((router.shape[1], width), bf),
            pltpu.VMEM((routes.shape[1], n_tok), routes.dtype),
            pltpu.VMEM((n_tok, 2 * width), f32),
            pltpu.VMEM((2, width, 2 * hid), bf),
            pltpu.VMEM((2, 2 * hid, width), bf),
            pltpu.VMEM((2, hid, width), bf),
            pltpu.VMEM((batches, 3 * n_lane, 2 * width + 128), bf),
            keep, keep, keep,
            pltpu.VMEM((2, batches * n_rows, hid), bf),
            *home(width),
            pltpu.VMEM((batches, 3 * n_lane, width), bf),
            pltpu.VMEM((2, n_rows, 2 * hid), bf),
            *home(width + 128),
            pltpu.VMEM((n_tok, 128), f32),
            pltpu.VMEM((n_tok, 128), f32),
            pltpu.VMEM((128, width), bf),
            dma((3, 2, 3)), dma((3, 2, 3)), dma((3, 2)),
            dma((3, 2, 4)), dma((3, 2, 4)),
            dma((3, 3, 3)), dma((3, 3, 3)), dma((batches, 2, 4)), dma((batches, 2, 4)),
            dma((2, batches, 2, 4)), dma((2, batches, 2, 4)),
            dma((2, batches, 4)), dma((2, batches, 4)),
            dma((batches, 2, 3)), dma((batches, 2, 3)), dma((5,)), dma((batches, 2)),
        ],
        compiler_params=pltpu.CompilerParams(
            collective_id=0, has_side_effects=True, vmem_limit_bytes=60 * 2**20
        ),
        cost_estimate=pl.CostEstimate(
            flops=2 * 8 * 512 * width * hid, bytes_accessed=2**24, transcendentals=2**20
        ),
    )(tokens, tangent, norm_gain.reshape(1, width), router.T, routes.T, w_gate, w_up, w_down)
    return both[:, 0:width], both[:, width : 2 * width]


def solution(mesh):
    in_specs = (
        P(("dp", "expert"), None),
        P(("dp", "expert"), None),
        P(),
        P(),
        P("expert", "dp", None),
        P("expert", "dp", None),
        P("expert", None, "dp"),
        P(("dp", "expert"), None),
    )
    out_specs = (P(("dp", "expert"), None), P(("dp", "expert"), None))
    body = on_device
    if mesh.shape["dp"] == 4 and mesh.shape["expert"] == 8:
        body = on_device_dense
    return jax.shard_map(
        body, mesh=mesh, in_specs=in_specs, out_specs=out_specs, check_vma=False
    )
```

```python
import functools

import jax
import jax.numpy as jnp
from jax import lax
from jax.experimental import pallas as pl
from jax.experimental.pallas import tpu as pltpu
from jax.sharding import PartitionSpec as P

eps_value = 1e-06


def pick_columns(table, routes):
    hits = routes[:, :, None] == jnp.arange(table.shape[1], dtype=jnp.int32)[None, None, :]
    return jnp.sum(jnp.where(hits, table[:, None, :], jnp.zeros((), table.dtype)), axis=2)


def on_device(tokens, tangent, norm_gain, router, w_gate, w_up, w_down, routes):
    tok_rows, topk = routes.shape
    model_width = tokens.shape[1]
    experts_all = router.shape[1]
    local_experts = w_gate.shape[0]
    groups = lax.axis_size("expert")
    capacity = 2 * tok_rows * topk // experts_all
    xfull = tokens.astype(jnp.float32)
    vfull = tangent.astype(jnp.float32)
    inv_rms = lax.rsqrt(jnp.mean(xfull * xfull, axis=1, keepdims=True) + eps_value)
    normed = (norm_gain * xfull * inv_rms).astype(jnp.bfloat16)
    cross_term = jnp.mean(xfull * vfull, axis=1, keepdims=True)
    normed_tan = (norm_gain * (vfull * inv_rms - xfull * inv_rms**3 * cross_term)).astype(
        jnp.bfloat16
    )
    logits = jnp.dot(normed, router, preferred_element_type=jnp.float32)
    logit_tan = jnp.dot(normed_tan, router, preferred_element_type=jnp.float32)
    selected = pick_columns(logits, routes)
    sel_tan = pick_columns(logit_tan, routes)
    exp_sel = jnp.exp(selected)
    gate_prob = exp_sel / jnp.sum(exp_sel, axis=1, keepdims=True)
    gate_tan = gate_prob * (sel_tan - jnp.sum(gate_prob * sel_tan, axis=1, keepdims=True))
    gate_b = gate_prob.astype(jnp.bfloat16)
    gate_tan_b = gate_tan.astype(jnp.bfloat16)
    pair_count = tok_rows * topk
    flat_ids = routes.reshape(-1)
    order = jnp.arange(pair_count, dtype=jnp.int32)
    earlier = (flat_ids[None, :] == flat_ids[:, None]) & (order[None, :] < order[:, None])
    slot_rank = jnp.sum(earlier.astype(jnp.int32), axis=1)
    slot_of_pair = flat_ids * capacity + slot_rank
    slot_hits = slot_of_pair[None, :] == jnp.arange(experts_all * capacity, dtype=jnp.int32)[:, None]
    slot_table = jnp.max(
        jnp.where(slot_hits, jnp.arange(pair_count, dtype=jnp.int32)[None, :], -1), axis=1
    )
    slot_valid = slot_table >= 0
    safe_pair = jnp.maximum(slot_table, 0)
    tok_idx = safe_pair // topk
    which_k = safe_pair % topk
    bf_zero = jnp.zeros((), jnp.bfloat16)
    send_rows = jnp.stack(
        (
            jnp.where(slot_valid[:, None], normed[tok_idx], bf_zero),
            jnp.where(slot_valid[:, None], normed_tan[tok_idx], bf_zero),
        )
    )
    send_rows = send_rows.reshape(2, groups, local_experts * capacity, model_width)
    send_gates = jnp.stack(
        (
            jnp.where(slot_valid, gate_b[tok_idx, which_k], bf_zero),
            jnp.where(slot_valid, gate_tan_b[tok_idx, which_k], bf_zero),
        )
    )
    send_gates = send_gates.reshape(2, groups, local_experts * capacity)
    recv_rows, recv_gates = (
        lax.all_to_all(send_rows, "expert", split_axis=1, concat_axis=1, tiled=True),
        lax.all_to_all(send_gates, "expert", split_axis=1, concat_axis=1, tiled=True),
    )
    slot_rows = recv_rows.reshape(2, groups, local_experts, capacity, model_width)
    recv_gates = recv_gates.reshape(2, groups, local_experts, capacity).astype(jnp.float32)
    gate_val = recv_gates[0][..., None]
    tan_val = recv_gates[1][..., None]
    gate_full, up_full, down_full = (
        lax.all_gather(w_gate, "dp", axis=1, tiled=True),
        lax.all_gather(w_up, "dp", axis=1, tiled=True),
        lax.all_gather(w_down, "dp", axis=2, tiled=True),
    )
    pre_both = jnp.einsum(
        "tslkd,ldf->tslkf", slot_rows, gate_full, preferred_element_type=jnp.float32
    )
    up_both = jnp.einsum("tslkd,ldf->tslkf", slot_rows, up_full, preferred_element_type=jnp.float32)
    pre_gate = pre_both[0]
    gate_dot = pre_both[1]
    pre_up = up_both[0]
    up_dot = up_both[1]
    sig_gate = jax.nn.sigmoid(pre_gate)
    silu_gate = pre_gate * sig_gate
    slope_gate = sig_gate * (1.0 + pre_gate * (1.0 - sig_gate))
    hidden = silu_gate * pre_up
    hidden_tan = slope_gate * gate_dot * pre_up + silu_gate * up_dot
    mixed_rows = (tan_val * hidden + gate_val * hidden_tan).astype(jnp.bfloat16)
    pair_image = jnp.einsum(
        "slkf,lfd->slkd", mixed_rows, down_full, preferred_element_type=jnp.float32
    )
    pair_send = pair_image.astype(jnp.bfloat16).reshape(
        groups, local_experts * capacity, model_width
    )
    pair_back = lax.all_to_all(pair_send, "expert", split_axis=0, concat_axis=0, tiled=True)
    pair_back = pair_back.reshape(experts_all * capacity, model_width)
    tangent_image = jnp.sum(
        pair_back[slot_of_pair].astype(jnp.float32).reshape(tok_rows, topk, model_width), axis=1
    )
    image_b = tangent_image.astype(jnp.bfloat16)
    send_cot = jnp.where(slot_valid[:, None], image_b[tok_idx], bf_zero).reshape(
        groups, local_experts * capacity, model_width
    )
    recv_cot = lax.all_to_all(send_cot, "expert", split_axis=0, concat_axis=0, tiled=True)
    recv_cot = recv_cot.reshape(groups, local_experts, capacity, model_width)
    back_hidden = jnp.einsum(
        "slkd,lfd->slkf", recv_cot, down_full, preferred_element_type=jnp.float32
    )
    gate_cot = jnp.sum(back_hidden * hidden, axis=3).astype(jnp.bfloat16)
    scaled = gate_val * back_hidden
    grad_gate = (scaled * pre_up * slope_gate).astype(jnp.bfloat16)
    grad_up = (scaled * silu_gate).astype(jnp.bfloat16)
    pair_grad = jnp.einsum(
        "slkf,ldf->slkd", grad_gate, gate_full, preferred_element_type=jnp.float32
    )
    pair_grad = pair_grad + jnp.einsum(
        "slkf,ldf->slkd", grad_up, up_full, preferred_element_type=jnp.float32
    )
    grad_send = pair_grad.astype(jnp.bfloat16).reshape(
        groups, local_experts * capacity, model_width
    )
    cot_send = gate_cot.reshape(groups, local_experts * capacity)
    grad_back, cot_back = (
        lax.all_to_all(grad_send, "expert", split_axis=0, concat_axis=0, tiled=True),
        lax.all_to_all(cot_send, "expert", split_axis=0, concat_axis=0, tiled=True),
    )
    grad_back = grad_back.reshape(experts_all * capacity, model_width)
    cot_back = cot_back.reshape(experts_all * capacity)
    expert_grad = jnp.sum(
        grad_back[slot_of_pair].astype(jnp.float32).reshape(tok_rows, topk, model_width), axis=1
    )
    pair_cot = cot_back[slot_of_pair].astype(jnp.float32).reshape(tok_rows, topk)
    logit_grad = gate_prob * (pair_cot - jnp.sum(gate_prob * pair_cot, axis=1, keepdims=True))
    hits = routes[:, :, None] == jnp.arange(experts_all, dtype=jnp.int32)[None, None, :]
    column_grad = jnp.sum(jnp.where(hits, logit_grad[:, :, None], 0.0), axis=1)
    router_grad = jnp.dot(
        column_grad, router.astype(jnp.float32).T, precision=lax.Precision.HIGHEST
    )
    pulled = norm_gain * (expert_grad + router_grad)
    gram_image = inv_rms * pulled - xfull * inv_rms**3 * jnp.mean(
        pulled * xfull, axis=1, keepdims=True
    )
    return (tangent_image, gram_image)


MESH = pl.DeviceIdType.MESH


def nt_dot(left, right):
    return lax.dot_general(
        left, right, (((1,), (1,)), ((), ())), preferred_element_type=jnp.float32
    )


def nn_dot(left, right):
    return jnp.dot(left, right, preferred_element_type=jnp.float32)


batches = 2


def block_kernel(
    tok_hbm, tan_hbm, gain_hbm, router_hbm, routes_hbm, wg_ref, wu_ref, wd_ref,
    both_hbm,
    tok_ref, tan_ref, gain_ref, router_ref, routes_ref, both_ref,
    wgu, wgu_t, wd, rows, keep_a, keep_s, keep_h, mix, part, own_part, mid, far, landed,
    image_rows, grads, part2, own_part2, mid2, far2, landed2, prob_keep, inv_keep, router_pad,
    w_send, w_recv, w_own, m_send, m_recv, t_send, t_recv, a_send, a_recv, s_send, s_recv,
    z_send, z_recv, l_send, l_recv, i_sems, o_sems,
):
    f32, bf = jnp.float32, jnp.bfloat16
    n_tok, width = tok_ref.shape
    slab, hid = wg_ref.shape[1], wg_ref.shape[2]
    half = hid // 2
    n_sub = n_tok // batches
    n_lane = 4 * n_sub
    n_exp = router_ref.shape[0]
    dp, ex = lax.axis_index("dp"), lax.axis_index("expert")
    y, x = dp // 2, dp % 2
    z, core = ex // 2, ex % 2
    x_index, y_index = y * 2 + 1 - x, (1 - y) * 2 + x
    d_index = (1 - y) * 2 + 1 - x
    x_peer, y_peer = (x_index, ex), (y_index, ex)
    mate = (dp, z * 2 + 1 - core)
    z_peers = [(dp, (z + dz) % 4 * 2 + core) for dz in range(1, 4)]
    at_x, at_own, at_y = 0, n_lane, 2 * n_lane

    def rows_of(base, dz):
        return pl.ds(pl.multiple_of(base + (z + dz) % 4 * n_sub, n_sub), n_sub)

    def tokens_of(b):
        return slice(b * n_sub, (b + 1) * n_sub)

    loads = [
        pltpu.make_async_copy(src, dst, i_sems.at[i])
        for i, (src, dst) in enumerate((
            (tok_hbm, tok_ref), (tan_hbm, tan_ref), (gain_hbm, gain_ref),
            (router_hbm, router_ref), (routes_hbm, routes_ref),
        ))
    ]
    for load in loads:
        load.start()

    barrier = pltpu.get_barrier_semaphore()
    friends = [
        (x_peer, None), (y_peer, None), (mate, None), (z_peers[0], z < 3), (z_peers[2], z > 0)
    ]

    def greet(friend):
        pl.semaphore_signal(barrier, inc=1, device_id=friend, device_id_type=MESH)

    for friend, cond in friends:
        if cond is None:
            greet(friend)
        else:
            pl.when(cond)(functools.partial(greet, friend))
    inner = jnp.where(z > 0, 1, 0) * jnp.where(z < 3, 1, 0)
    pl.semaphore_wait(barrier, 4 + inner)

    pending = []

    def push(src, dst, sems, where, device, cond=None):
        copy = pltpu.make_async_remote_copy(
            src_ref=src, dst_ref=dst, send_sem=sems[0].at[where], recv_sem=sems[1].at[where],
            device_id=device, device_id_type=MESH,
        )
        if cond is None:
            copy.start()
        else:
            pl.when(cond)(copy.start)
        pending.append((copy, cond))
        return copy

    def slab_of(index):
        return pl.ds(pl.multiple_of(index * slab, slab), slab)

    def weight_at(kind, l, index):
        if kind == 2:
            return wd.at[l, pl.ds(pl.multiple_of(core * half, half), half), slab_of(index)]
        first = pl.multiple_of(core * hid + kind * half, half)
        return wgu.at[l, slab_of(index), pl.ds(first, half)]

    def weight_src(kind, l, which):
        part_of = pl.ds(pl.multiple_of(which * half, half), half)
        if kind == 2:
            return wd_ref.at[l, part_of, :]
        return (wg_ref, wu_ref)[kind].at[l, :, part_of]

    direct, relayed, shared, local = {}, {}, {}, {}
    w_sems, m_sems, t_sems = (w_send, w_recv), (m_send, m_recv), (t_send, t_recv)
    a_sems, s_sems, z_sems = (a_send, a_recv), (s_send, s_recv), (z_send, z_recv)
    l_sems = (l_send, l_recv)

    def start_weights(kind):
        for p, l in ((0, 0), (1, 1), (0, 1), (1, 0)):
            for_x, for_y = (1 - x, x) if l == 0 else (y, 1 - y)
            direct[kind, l, p] = push(
                weight_src(kind, l, (for_x, for_y)[p]), weight_at(kind, l, dp),
                w_sems, (kind, l, p), (x_peer, y_peer)[p],
            )
        for l in range(2):
            for_me = (x, y)[l]
            mine = weight_at(kind, l, dp)
            local[kind, l] = pltpu.make_async_copy(
                weight_src(kind, l, for_me), mine, w_own.at[kind, l]
            )
            local[kind, l].start()
            shared[kind, l] = [
                push(weight_src(kind, l, for_me), mine, m_sems, (kind, l, 0), mate)
            ]

    def share_weights(kind, l, slot, index):
        block = weight_at(kind, l, index)
        shared[kind, l].append(push(block, block, m_sems, (kind, l, slot), mate))

    def relay_weights(kind):
        for l in range(2):
            index = (x_index, y_index)[l]
            block = weight_at(kind, l, index)
            direct[kind, l, l].wait_recv()
            relayed[kind, l] = push(block, block, w_sems, (kind, l, 2), (y_peer, x_peer)[l])
            share_weights(kind, l, 1, index)

    def side_weights(kind):
        for l in range(2):
            direct[kind, l, 1 - l].wait_recv()
            share_weights(kind, l, 2, (x_index, y_index)[1 - l])

    def last_weights(kind, l):
        relayed[kind, l].wait_recv()
        share_weights(kind, l, 3, d_index)

    def need_weights(kind, l):
        local[kind, l].wait()
        for copy in shared[kind, l]:
            copy.wait_recv()

    start_weights(0)

    for load in loads:
        load.wait()
    router_pad[...] = jnp.zeros(router_pad.shape, bf)
    router_pad[0:n_exp, :] = router_ref[...]
    xfull = tok_ref[...].astype(f32)
    vfull = tan_ref[...].astype(f32)
    gain = gain_ref[...]
    inv_rms = lax.rsqrt(jnp.mean(xfull * xfull, axis=1, keepdims=True) + eps_value)
    normed = (gain * xfull * inv_rms).astype(bf)
    cross_term = jnp.mean(xfull * vfull, axis=1, keepdims=True)
    inv_cube = inv_rms * inv_rms * inv_rms
    normed_tan = (gain * (vfull * inv_rms - xfull * inv_cube * cross_term)).astype(bf)
    mine = rows_of(at_own, 0)
    for b in range(batches):
        rows[b, mine, 0:width] = normed[tokens_of(b)]
        rows[b, mine, width : 2 * width] = normed_tan[tokens_of(b)]
    logits = nt_dot(normed, router_pad[...])
    logit_tan = nt_dot(normed_tan, router_pad[...])
    ids = lax.broadcasted_iota(jnp.int32, (128, n_tok), 0)
    chosen_by = jnp.zeros((128, n_tok), f32)
    for k in range(routes_ref.shape[0]):
        chosen_by = chosen_by + jnp.where(ids == routes_ref[k : k + 1, :], 1.0, 0.0)
    unit = jnp.where(
        lax.broadcasted_iota(jnp.int32, (n_tok, n_tok), 0)
        == lax.broadcasted_iota(jnp.int32, (n_tok, n_tok), 1),
        1.0, 0.0,
    ).astype(bf)
    chosen = nt_dot(unit, chosen_by.astype(bf))
    exp_sel = jnp.where(chosen > 0.5, jnp.exp(logits), 0.0)
    gate_prob = exp_sel / jnp.sum(exp_sel, axis=1, keepdims=True)
    gate_tan = gate_prob * (
        logit_tan - jnp.sum(gate_prob * logit_tan, axis=1, keepdims=True)
    )
    table = (gate_prob + pltpu.roll(gate_tan, 64, 1)).astype(bf)
    for b in range(batches):
        rows[b, mine, 2 * width : 2 * width + 128] = table[tokens_of(b)]
    prob_keep[...] = gate_prob
    inv_keep[...] = jnp.broadcast_to(inv_rms, (n_tok, 128))

    ups, downs = {}, {}
    bases = (at_x, at_own, at_y)

    def has_up(j):
        return jnp.logical_and(z < 3, z >= j)

    def has_down(j):
        return jnp.logical_and(z > 0, z + j <= 3)

    def chain(which, j):
        if j:
            pl.when(z >= j)(ups[which, j - 1].wait_recv)
            pl.when(z + j <= 3)(downs[which, j - 1].wait_recv)
        if j < 3:
            above = rows.at[:, rows_of(bases[which], 4 - j)]
            below = rows.at[:, rows_of(bases[which], j)]
            ups[which, j] = push(above, above, t_sems, (which, 0, j), z_peers[0], has_up(j))
            downs[which, j] = push(below, below, t_sems, (which, 1, j), z_peers[2], has_down(j))

    from_x = push(rows.at[:, mine], rows.at[:, rows_of(at_x, 0)], t_sems, (0, 2, 0), x_peer)
    from_y = push(rows.at[:, mine], rows.at[:, rows_of(at_y, 0)], t_sems, (2, 2, 0), y_peer)
    chain(1, 0)
    start_weights(1)
    from_x.wait_recv()
    chain(0, 0)
    from_y.wait_recv()
    chain(2, 0)
    relay_weights(0)
    for which in (1, 0, 2):
        chain(which, 1)
    side_weights(0)
    relay_weights(1)
    start_weights(2)
    for which in (1, 0, 2):
        chain(which, 2)
    side_weights(1)
    for kind in range(2):
        for l in range(2):
            last_weights(kind, l)

    def turn_weights(l):
        need_weights(0, l)
        need_weights(1, l)

        @pl.loop(0, 4)
        def _(j):
            at = pl.ds(pl.multiple_of(j * slab, slab), slab)
            wgu_t[l, :, at] = wgu[l, at, :].T

    turn_weights(0)
    turn_weights(1)
    relay_weights(2)
    side_weights(2)
    for which in (1, 0, 2):
        chain(which, 3)

    n_rows = 2 * n_lane
    all_rows = batches * n_rows
    wide_lanes = lax.broadcasted_iota(jnp.int32, (all_rows, 128), 1)

    for l in range(2):
        these = slice(l * n_lane, l * n_lane + n_rows)

        @pl.loop(0, 2)
        def _(k):
            cols = pl.ds(pl.multiple_of(k * hid, hid), hid)
            expert = (z * 2 + k) * 2 + l
            table = rows[:, these, 2 * width : 2 * width + 128].reshape(all_rows, 128).astype(f32)
            gate = jnp.sum(jnp.where(wide_lanes == expert, table, 0.0), axis=1, keepdims=True)
            tan = jnp.sum(
                jnp.where(wide_lanes == expert + 64, table, 0.0), axis=1, keepdims=True
            )
            pre = nn_dot(rows[:, these, 0:width].reshape(all_rows, width), wgu[l, :, cols])
            dots = nn_dot(
                rows[:, these, width : 2 * width].reshape(all_rows, width), wgu[l, :, cols]
            )
            pre_gate, pre_up = pre[:, 0:half], pre[:, half:hid]
            gate_dot, up_dot = dots[:, 0:half], dots[:, half:hid]
            sig = jax.nn.sigmoid(pre_gate)
            silu = pre_gate * sig
            slope_up = sig * (1.0 + pre_gate * (1.0 - sig)) * pre_up
            hidden = silu * pre_up
            mixed = tan * hidden + gate * (slope_up * gate_dot + silu * up_dot)
            keep_a[l, k] = gate * slope_up
            keep_s[l, k] = gate * silu
            keep_h[l, k] = hidden
            mix[l, :, pl.ds(pl.multiple_of(k * half, half), half)] = mixed.astype(bf)

    turns = [
        (part, own_part, mid, far, landed), (part2, own_part2, mid2, far2, landed2)
    ]
    x_copies, y_copies = {}, {}

    def by_z(a, b, c, d):
        return jnp.where(z < 2, jnp.where(z < 1, a, b), jnp.where(z < 3, c, d))

    far_first = {0: 0, 2: by_z(3, 2, 2, 1), 1: by_z(2, 1, 3, 2), 3: by_z(1, 3, 1, 3)}

    def place(turn, b, l, cols, term):
        parts, own = turns[turn][0:2]
        if l == 0:
            parts[b, at_x : at_x + n_lane, cols] = term[0:n_lane].astype(bf)
            own[b, :, cols] = term[n_lane:n_rows]
        else:
            own[b, :, cols] = own[b, :, cols] + term[0:n_lane]
            parts[b, at_y : at_y + n_lane, cols] = term[n_lane:n_rows].astype(bf)

    def send_side(turn, b, s):
        parts, far = turns[turn][0], turns[turn][3]
        peer, base = ((x_peer, at_x), (y_peer, at_y))[s]
        copies = (x_copies, y_copies)[s]
        for turn_no in (2, 1, 3, 0):
            dz = far_first[turn_no]
            copies[turn, b, turn_no] = push(
                parts.at[b, rows_of(base, dz)], far.at[b, s, rows_of(0, dz)],
                s_sems, (turn, b, s, dz), peer,
            )

    def merge(turn, b, turn_no):
        parts, own, mid, far, land = turns[turn]
        dz = far_first[turn_no]
        x_copies[turn, b, turn_no].wait_recv()
        y_copies[turn, b, turn_no].wait_recv()
        at = rows_of(0, dz)
        total = own[b, at, :] + (far[b, 0, at, :].astype(f32) + far[b, 1, at, :].astype(f32))
        if turn_no:
            mid[b, turn_no] = total.astype(bf)
            push(
                mid.at[b, turn_no], land.at[b, z], z_sems, (turn, b, dz),
                (dp, (z + dz) % 4 * 2 + core),
            )
        else:
            own[b, at, :] = total

    def total_of(turn, b):
        own, mid, land = turns[turn][1], turns[turn][2], turns[turn][4]
        total = own[b, rows_of(0, 0), :]
        for dz in (1, 3, 2):
            pltpu.make_async_remote_copy(
                src_ref=mid.at[b, dz], dst_ref=land.at[b, (z + 4 - dz) % 4],
                send_sem=z_send.at[turn, b, dz], recv_sem=z_recv.at[turn, b, dz],
                device_id=z_peers[dz - 1], device_id_type=MESH,
            ).wait_recv()
            total = total + land[b, (z + 4 - dz) % 4].astype(f32)
        return total

    def down(b, l):
        left = mix[l, b * n_rows : (b + 1) * n_rows, :]
        place(0, b, l, slice(0, width), nn_dot(left, wd[l]))
        send_side(0, b, l)

    links, sides, stores = {}, {}, []

    def store(b, part):
        piece = (tokens_of(b), pl.ds(part * width, width))
        stores.append(
            pltpu.make_async_copy(both_ref.at[piece], both_hbm.at[piece], o_sems.at[b, part])
        )
        stores[-1].start()

    def image_to_sides(b, dz, cond=None):
        block = image_rows.at[b, rows_of(at_own, 4 - dz)]
        for s, (peer, base) in enumerate(((x_peer, at_x), (y_peer, at_y))):
            sides[b, s, dz] = push(
                block, image_rows.at[b, rows_of(base, 4 - dz)], a_sems, (b, s, dz), peer, cond
            )

    def image_link(b, way, j):
        block = image_rows.at[b, rows_of(at_own, (4 - j, j)[way])]
        links[b, way, j] = push(
            block, block, l_sems, (b, way, j), z_peers[(0, 2)[way]], (has_up, has_down)[way](j)
        )

    def image_of(b):
        image = total_of(0, b)
        both_ref[tokens_of(b), 0:width] = image
        image_rows[b, mine, :] = image.astype(bf)
        image_link(b, 0, 0)
        image_link(b, 1, 0)
        image_to_sides(b, 0)
        store(b, 0)

    def image_on(b, j):
        for way, here, dz in ((0, z > j, 1 + j), (1, z < 3 - j, 3 - j)):
            pl.when(here)(links[b, way, j].wait_recv)
            if j < 2:
                image_link(b, way, j + 1)
            image_to_sides(b, dz, here)

    def backward(b, l):
        for dz in range(4):
            sides[b, l, dz].wait_recv()
        these = slice(l * n_lane, l * n_lane + n_rows)
        kept = slice(b * n_rows, (b + 1) * n_rows)
        cots = jnp.zeros((n_rows, 128), f32)
        back_both = nt_dot(image_rows[b, these, :], wd[l])
        for k in range(2):
            back = back_both[:, k * half : (k + 1) * half]
            cot = jnp.sum(back * keep_h[l, k, kept], axis=1, keepdims=True)
            cots = cots + jnp.where(wide_lanes[0:n_rows] == (z * 2 + k) * 2 + l, cot, 0.0)
            grads[l, :, k * hid : k * hid + half] = (back * keep_a[l, k, kept]).astype(bf)
            grads[l, :, k * hid + half : (k + 1) * hid] = (back * keep_s[l, k, kept]).astype(bf)
        place(1, b, l, slice(width, width + 128), cots)
        place(1, b, l, slice(0, width), nn_dot(grads[l], wgu_t[l]))
        send_side(1, b, l)

    def gram_of(b):
        total = total_of(1, b)
        these = tokens_of(b)
        expert_grad = total[:, 0:width]
        cot = total[:, width : width + 128]
        prob = prob_keep[these, :]
        column_grad = prob * (cot - jnp.sum(prob * cot, axis=1, keepdims=True))
        high = column_grad.astype(bf)
        rest = column_grad - high.astype(f32)
        middle = rest.astype(bf)
        low = (rest - middle.astype(f32)).astype(bf)
        router = router_pad[...]
        router_grad = nn_dot(high, router) + (nn_dot(middle, router) + nn_dot(low, router))
        xfull = tok_ref[these, :].astype(f32)
        inv_rms = inv_keep[these, 0:1]
        pulled = gain_ref[...] * (expert_grad + router_grad)
        both_ref[these, width : 2 * width] = inv_rms * pulled - xfull * (inv_rms * inv_rms * inv_rms) * jnp.mean(
            pulled * xfull, axis=1, keepdims=True
        )
        store(b, 1)

    last_weights(2, 0)
    last_weights(2, 1)
    need_weights(2, 0)
    down(0, 0)
    need_weights(2, 1)
    down(0, 1)
    down(1, 0)
    down(1, 1)
    merge(0, 0, 2)
    merge(0, 0, 1)
    merge(0, 0, 3)
    merge(0, 0, 0)
    merge(0, 1, 2)
    image_of(0)
    merge(0, 1, 1)
    merge(0, 1, 3)
    image_on(0, 0)
    merge(0, 1, 0)
    image_of(1)
    image_on(0, 1)
    image_on(1, 0)
    image_on(0, 2)
    image_on(1, 1)
    image_on(1, 2)
    backward(0, 0)
    backward(0, 1)
    backward(1, 0)
    backward(1, 1)
    merge(1, 0, 2)
    merge(1, 0, 1)
    merge(1, 0, 3)
    merge(1, 0, 0)
    merge(1, 1, 2)
    merge(1, 1, 1)
    merge(1, 1, 3)
    gram_of(0)
    merge(1, 1, 0)
    gram_of(1)
    for copy in stores:
        copy.wait()
    for copy, cond in pending:
        if cond is None:
            copy.wait_send()
        else:
            pl.when(cond)(copy.wait_send)


def on_device_dense(tokens, tangent, norm_gain, router, w_gate, w_up, w_down, routes):
    n_tok, width = tokens.shape
    hid = w_gate.shape[2]
    half = hid // 2
    n_sub = n_tok // batches
    n_lane = 4 * n_sub
    n_rows = 2 * n_lane
    bf, f32 = jnp.bfloat16, jnp.float32
    hbm = pl.BlockSpec(memory_space=pl.ANY)
    out = jax.ShapeDtypeStruct((n_tok, 2 * width), f32)
    dma = pltpu.SemaphoreType.DMA
    keep = pltpu.VMEM((2, 2, batches * n_rows, half), f32)

    def home(columns):
        return [
            pltpu.VMEM((batches, 3 * n_lane, columns), bf),
            pltpu.VMEM((batches, n_lane, columns), f32),
            pltpu.VMEM((batches, 4, n_sub, columns), bf),
            pltpu.VMEM((batches, 2, n_lane, columns), bf),
            pltpu.VMEM((batches, 4, n_sub, columns), bf),
        ]

    both = pl.pallas_call(
        block_kernel,
        out_shape=out,
        in_specs=[hbm] * 8,
        out_specs=hbm,
        scratch_shapes=[
            pltpu.VMEM((n_tok, width), bf),
            pltpu.VMEM((n_tok, width), bf),
            pltpu.VMEM((1, width), f32),
            pltpu.VMEM((router.shape[1], width), bf),
            pltpu.VMEM((routes.shape[1], n_tok), routes.dtype),
            pltpu.VMEM((n_tok, 2 * width), f32),
            pltpu.VMEM((2, width, 2 * hid), bf),
            pltpu.VMEM((2, 2 * hid, width), bf),
            pltpu.VMEM((2, hid, width), bf),
            pltpu.VMEM((batches, 3 * n_lane, 2 * width + 128), bf),
            keep, keep, keep,
            pltpu.VMEM((2, batches * n_rows, hid), bf),
            *home(width),
            pltpu.VMEM((batches, 3 * n_lane, width), bf),
            pltpu.VMEM((2, n_rows, 2 * hid), bf),
            *home(width + 128),
            pltpu.VMEM((n_tok, 128), f32),
            pltpu.VMEM((n_tok, 128), f32),
            pltpu.VMEM((128, width), bf),
            dma((3, 2, 3)), dma((3, 2, 3)), dma((3, 2)),
            dma((3, 2, 4)), dma((3, 2, 4)),
            dma((3, 3, 3)), dma((3, 3, 3)), dma((batches, 2, 4)), dma((batches, 2, 4)),
            dma((2, batches, 2, 4)), dma((2, batches, 2, 4)),
            dma((2, batches, 4)), dma((2, batches, 4)),
            dma((batches, 2, 3)), dma((batches, 2, 3)), dma((5,)), dma((batches, 2)),
        ],
        compiler_params=pltpu.CompilerParams(
            collective_id=0, has_side_effects=True, vmem_limit_bytes=60 * 2**20
        ),
        cost_estimate=pl.CostEstimate(
            flops=2 * 8 * 512 * width * hid, bytes_accessed=2**24, transcendentals=2**20
        ),
    )(tokens, tangent, norm_gain.reshape(1, width), router.T, routes.T, w_gate, w_up, w_down)
    return both[:, 0:width], both[:, width : 2 * width]


def solution(mesh):
    in_specs = (
        P(("dp", "expert"), None),
        P(("dp", "expert"), None),
        P(),
        P(),
        P("expert", "dp", None),
        P("expert", "dp", None),
        P("expert", None, "dp"),
        P(("dp", "expert"), None),
    )
    out_specs = (P(("dp", "expert"), None), P(("dp", "expert"), None))
    body = on_device
    if mesh.shape["dp"] == 4 and mesh.shape["expert"] == 8:
        body = on_device_dense
    return jax.shard_map(
        body, mesh=mesh, in_specs=in_specs, out_specs=out_specs, check_vma=False
    )
```
